512 devices in a mesh: gx: 8 (over x, core), gy: 8 (over z), gz: 8 (over y).
Axes of the slice: x: 4, y: 8, z: 8, core: 2. Of those that a mesh axis runs over, the one named last changes fastest.
Arguments:
- positions: float32 [3, 32, 32, 6144], P(None, 'gx', 'gy', 'gz'), may hold values from 0 to 1
- charges: float32 [32, 32, 6144], P('gx', 'gy', 'gz'), may hold values from -0.625 to 0.625
- softening: float32 [32, 32, 6144], P('gx', 'gy', 'gz'), may hold values from 0.05 to 0.2
- counts: int32 [32, 32, 96], P('gx', 'gy', 'gz'), may hold values from 1 to 64
- top_locals: float32 [8, 8, 1536], P('gx', 'gy', 'gz'), may hold values from -6 to 6
- b_multipoles: bfloat16 [8, 8, 1536], P('gx', 'gy', 'gz'), may hold values from -24 to 24
- a_multipoles: bfloat16 [16, 16, 3072], P('gx', 'gy', 'gz'), may hold values from -12 to 12
- leaf_multipoles: bfloat16 [32, 32, 6144], P('gx', 'gy', 'gz'), may hold values from -6 to 6
- m2l_table: bfloat16 [343, 4096], replicated, may hold values from -0.0546875 to 0.0546875
- l2l_table: bfloat16 [8, 4096], replicated, may hold values from -0.75 to 0.75
Outputs:
- potential: float32 [32, 32, 6144], P('gx', 'gy', 'gz')
- leaf_locals: float32 [32, 32, 6144], P('gx', 'gy', 'gz')
The draws below stay inside these ranges and needn't reach their ends.
Inputs may be any that keep to these rules, and one draw needn't show every extreme that they name: counts gives the live particles of each leaf; its slots at and beyond that number are padding.
All inputs are finite; a program needn't handle non-finite values.
Results may differ from the reference program's by a relative error of at most 0.008.
Values may be sent and summed in bfloat16 or wider, within the bound.
A program may use at most 128 MiB of HBM per device.

```python
import jax
import jax.numpy as jnp
import numpy as np
from jax import lax

ORDER = 4
K = 64
P_SIZE = 64
NLX = 32
NLY = 32
NLZ = 96


def set_ends(entries, stream_key, low, top_value):
    index_at = [jax.random.randint(jax.random.fold_in(stream_key, axis), (), 0, length) for axis, length in enumerate(entries.shape)]
    widest = entries.shape.index(max(entries.shape))
    beside = index_at[:widest] + [(index_at[widest] + 1) % entries.shape[widest]] + index_at[widest + 1:]
    return entries.at[tuple(index_at)].set(low).at[tuple(beside)].set(top_value)


def block_scale(stream_key, dims, split, low, top_value):
    level, own = 1.0, jax.random.fold_in(stream_key, 6)
    for axis_at, shards_of in split:
        heights = jnp.exp(jax.random.uniform(jax.random.fold_in(own, axis_at), (shards_of,), jnp.float32, low / len(split), top_value / len(split)))
        level = level * jnp.repeat(heights, dims[axis_at] // shards_of).reshape([-1 if axis == axis_at else 1 for axis in range(len(dims))])
    return level


def noise(key, dims, scale, limit, split=(), held_as=jnp.bfloat16):
    loudness = block_scale(key, dims, split, -0.22, 0.18) if split else 1.0
    values = jax.random.normal(key, dims, jnp.float32) * scale * loudness
    return jnp.minimum(jnp.maximum(values, -limit), limit).astype(held_as)


def setup_inputs(seed: int = 0) -> dict:
    key_of = jax.random.split(jax.random.key(seed), 11)
    positions = jnp.clip(1.0 * jax.random.uniform(key_of[0], (3, NLX, NLY, NLZ * P_SIZE), jnp.float32) ** block_scale(key_of[0], (3, NLX, NLY, NLZ * P_SIZE), ((1, 8), (2, 8), (3, 8)), -0.2, 0.2), 0.0, 1.0)
    charges = noise(key_of[1], (NLX, NLY, NLZ * P_SIZE), 0.04, 0.625, ((0, 8), (1, 8), (2, 8)), jnp.float32)
    softening = jnp.clip(0.05 + 0.15 * jax.random.uniform(key_of[2], (NLX, NLY, NLZ * P_SIZE), jnp.float32) ** block_scale(key_of[2], (NLX, NLY, NLZ * P_SIZE), ((0, 8), (1, 8), (2, 8)), -0.2, 0.2), 0.05, 0.2)
    counts = set_ends(jax.random.randint(key_of[3], (NLX, NLY, NLZ), 1, P_SIZE + 1), jax.random.fold_in(key_of[3], 1), 1, P_SIZE).astype(jnp.int32)
    top_locals = noise(key_of[4], (NLX // 4, NLY // 4, NLZ // 4 * K), 1.0, 6.0, ((0, 8), (1, 8), (2, 8)), jnp.float32)
    b_multipoles = noise(key_of[5], (NLX // 4, NLY // 4, NLZ // 4 * K), 4.0, 24.0, ((0, 8), (1, 8), (2, 8)))
    a_multipoles = noise(key_of[6], (NLX // 2, NLY // 2, NLZ // 2 * K), 2.0, 12.0, ((0, 8), (1, 8), (2, 8)))
    leaf_multipoles = noise(key_of[7], (NLX, NLY, NLZ * K), 1.0, 6.0, ((0, 8), (1, 8), (2, 8)))
    m2l_table = noise(key_of[8], (343, K * K), (189 * K) ** -0.5, 0.0546875)
    l2l_table = noise(key_of[9], (8, K * K), K ** -0.5, 0.75)
    return {"positions": positions, "charges": charges, "softening": softening, "counts": counts, "top_locals": top_locals, "b_multipoles": b_multipoles, "a_multipoles": a_multipoles, "leaf_multipoles": leaf_multipoles, "m2l_table": m2l_table, "l2l_table": l2l_table}


def offset_tables():
    offset_index = np.zeros((8, 216), np.int32)
    far_mask = np.zeros((8, 216), np.bool_)
    for parity in range(8):
        parity_x, parity_y, parity_z = (parity // 4, parity // 2 % 2, parity % 2)
        for source in range(216):
            shift_x = source // 36 - 2 - parity_x
            shift_y = source // 6 % 6 - 2 - parity_y
            shift_z = source % 6 - 2 - parity_z
            far_mask[parity, source] = max(abs(shift_x), abs(shift_y), abs(shift_z)) > 1
            offset_index[parity, source] = (shift_x + 3) * 49 + (shift_y + 3) * 7 + (shift_z + 3)
    return (offset_index, far_mask)

def columns(padded):
    size_x, size_y, size_z, coeff_count = padded.shape
    half_x, half_y, half_z = (size_x // 2 - 2, size_y // 2 - 2, size_z // 2 - 2)
    paired = padded.reshape(half_x + 2, 2, half_y + 2, 2, half_z + 2, 2, coeff_count)
    pieces = []
    for step_x in range(3):
        for step_y in range(3):
            for step_z in range(3):
                pieces.append(paired[step_x:step_x + half_x, :, step_y:step_y + half_y, :, step_z:step_z + half_z, :, :])
    stacked = jnp.stack(pieces).reshape(3, 3, 3, half_x, 2, half_y, 2, half_z, 2, coeff_count)
    ordered = stacked.transpose(3, 5, 7, 0, 4, 1, 6, 2, 8, 9)
    return ordered.reshape(half_x * half_y * half_z, 216 * coeff_count)

def children_layout(values, half_x, half_y, half_z):
    coeff_count = values.shape[-1]
    blocked = values.reshape(half_x, half_y, half_z, 2, 2, 2, coeff_count)
    return blocked.transpose(0, 3, 1, 4, 2, 5, 6).reshape(2 * half_x, 2 * half_y, 2 * half_z, coeff_count)

def translate_grid(padded, weights):
    half_x = (padded.shape[0] - 4) // 2
    half_y = (padded.shape[1] - 4) // 2
    half_z = (padded.shape[2] - 4) // 2
    wide_weights = weights.astype(jnp.float32)

    def slab(index):
        window = lax.dynamic_slice_in_dim(padded, 2 * index, 6, 0)
        flat = columns(window).astype(jnp.float32)
        return jnp.einsum('sj,pja->spa', flat, wide_weights, precision=lax.Precision.HIGHEST)
    result = lax.map(slab, jnp.arange(half_x, dtype=jnp.int32))
    return children_layout(result.reshape(-1, 8, result.shape[-1]), half_x, half_y, half_z)

def descend(parents, l2l_shaped):
    half_x, half_y, half_z, coeff_count = parents.shape
    rounded = parents.astype(jnp.bfloat16)
    shifted = jnp.einsum('xyzb,pba->xyzpa', rounded.astype(jnp.float32), l2l_shaped.astype(jnp.float32), precision=lax.Precision.HIGHEST)
    return children_layout(shifted.reshape(-1, 8, coeff_count), half_x, half_y, half_z)

def chebyshev(values, degree_count):
    mapped = 2.0 * values - 1.0
    series = [jnp.ones_like(mapped), mapped]
    for degree in range(2, degree_count):
        series.append(2.0 * mapped * series[-1] - series[-2])
    return jnp.stack(series[:degree_count], axis=-1)

def far_field(local_leaf, coord_x, coord_y, coord_z):
    shaped = local_leaf.reshape(local_leaf.shape[:-1] + (ORDER, ORDER, ORDER))
    summed = jnp.einsum('...abc,...pa,...pb,...pc->...p', shaped, chebyshev(coord_x, ORDER), chebyshev(coord_y, ORDER), chebyshev(coord_z, ORDER), precision=lax.Precision.HIGHEST)
    return summed / ORDER ** 1.5

def pair_sum(targets, sources, shift_x, shift_y):
    slot_count = targets.shape[-1]
    z_lift = (jnp.arange(3 * slot_count) // slot_count - 1).astype(jnp.float32)
    dist_x = sources[0][..., None, :] + shift_x - targets[0][..., :, None]
    dist_y = sources[1][..., None, :] + shift_y - targets[1][..., :, None]
    dist_z = sources[2][..., None, :] + z_lift - targets[2][..., :, None]
    spread = 0.5 * (targets[4][..., :, None] ** 2 + sources[4][..., None, :] ** 2)
    pieces = sources[3][..., None, :] * lax.rsqrt(dist_x * dist_x + dist_y * dist_y + dist_z * dist_z + spread)
    if shift_x == 0 and shift_y == 0:
        itself = jnp.arange(3 * slot_count)[None, :] == jnp.arange(slot_count)[:, None] + slot_count
        pieces = jnp.where(itself, 0.0, pieces)
    return lax.optimization_barrier(jnp.sum(pieces, axis=-1))

def pad_cells(grid):
    return jnp.pad(grid, ((2, 2), (2, 2), (2, 2), (0, 0)))

def reference(positions, charges, softening, counts, top_locals, b_multipoles, a_multipoles, leaf_multipoles, m2l_table, l2l_table):
    m2l_shaped = m2l_table.reshape(343, K, K)
    l2l_shaped = l2l_table.reshape(8, K, K)
    offset_index, far_mask = offset_tables()
    weights = jnp.where(jnp.asarray(far_mask)[:, :, None, None], jnp.take(m2l_shaped, jnp.asarray(offset_index), axis=0), jnp.zeros((), jnp.bfloat16)).reshape(8, 216 * K, K)
    grid_b = b_multipoles.reshape(NLX // 4, NLY // 4, NLZ // 4, K)
    grid_a = a_multipoles.reshape(NLX // 2, NLY // 2, NLZ // 2, K)
    grid_leaf = leaf_multipoles.reshape(NLX, NLY, NLZ, K)
    local_b = top_locals.reshape(NLX // 4, NLY // 4, NLZ // 4, K) + 0.25 * translate_grid(pad_cells(grid_b), weights)
    local_a = descend(local_b, l2l_shaped) + 0.5 * translate_grid(pad_cells(grid_a), weights)
    local_leaf = descend(local_a, l2l_shaped) + translate_grid(pad_cells(grid_leaf), weights)
    active = jnp.arange(P_SIZE, dtype=jnp.int32)[None, None, None, :] < counts[..., None]
    spots = positions.reshape(3, NLX, NLY, NLZ, P_SIZE)
    masked = jnp.where(active, charges.reshape(NLX, NLY, NLZ, P_SIZE), 0.0)
    fields = jnp.stack([spots[0], spots[1], spots[2], masked, softening.reshape(NLX, NLY, NLZ, P_SIZE)])
    padded = jnp.pad(fields, ((0, 0), (1, 1), (1, 1), (1, 1), (0, 0)))

    def slab(index):
        window = lax.dynamic_slice_in_dim(padded, index, 3, 1)
        stacked = jnp.concatenate([window[:, :, :, depth:depth + NLZ, :] for depth in range(3)], axis=-1)
        targets = window[:, 1, 1:-1, 1:-1, :]
        nearby = jnp.zeros((NLY, NLZ, P_SIZE), jnp.float32)
        for step_x in range(3):
            for step_y in range(3):
                nearby = nearby + pair_sum(targets, stacked[:, step_x, step_y:step_y + NLY], step_x - 1, step_y - 1)
        locals_row = lax.dynamic_index_in_dim(local_leaf, index, 0, keepdims=False)
        distant = far_field(locals_row, targets[0], targets[1], targets[2])
        alive_row = lax.dynamic_index_in_dim(active, index, 0, keepdims=False)
        return jnp.where(alive_row, distant + nearby, 0.0)
    potential = lax.map(slab, jnp.arange(NLX, dtype=jnp.int32))
    return (potential.reshape(NLX, NLY, NLZ * P_SIZE), local_leaf.reshape(NLX, NLY, NLZ * K))
```

```python
import functools
import jax
import jax.numpy as jnp
from jax import lax
from jax.experimental import pallas as pl
from jax.experimental.pallas import tpu as pltpu
from jax.sharding import PartitionSpec as P

F32 = jnp.float32
BF16 = jnp.bfloat16
MESH = pl.DeviceIdType.MESH
AXES = ("gx", "gy", "gz")
T2_ROWS = 49 * 384 + 256


def iota(shape, dim):
    return lax.broadcasted_iota(jnp.int32, shape, dim)


def count_lanes(counts, pair):
    rows = counts.shape[0]
    lane = iota((rows, 128), 1)
    low = counts[:, 2 * pair : 2 * pair + 1]
    high = counts[:, 2 * pair + 1 : 2 * pair + 2]
    return jnp.where(lane < 64, low, high), lane & 63


def unpack_rows(block, base, s2, rows):
    for c in range(32):
        s2[pl.ds(base * 32 + c, rows, stride=32), :] = block[:, c * 128 : (c + 1) * 128]


def pair_rows(first, second, low_lanes):
    turned_first = pltpu.roll(first, 64, 1)
    turned_second = pltpu.roll(second, 64, 1)
    even = jnp.where(low_lanes, first, turned_second)
    odd = jnp.where(low_lanes, turned_first, second)
    return even.astype(BF16), odd.astype(BF16)


def exchange_kernel(
    pos, chg, soft, cnt, bm, am, lm, m2l_hbm, l2l,
    pf_out, ml_out, ma_out, mb_out, t2,
    pf, ml, ma, mb, zs, zr, ps, mls, mas, ms, zf, mt, s2,
    send, recv, local,
):
    gx, gy, gz = (lax.axis_index(a) for a in AXES)

    def at(ox, oy, oz):
        return (
            lax.rem(gx + (ox + 8), 8),
            lax.rem(gy + (oy + 8), 8),
            lax.rem(gz + (oz + 8), 8),
        )

    table = pltpu.make_async_copy(m2l_hbm, mt, local.at[0])
    table.start()
    barrier = pltpu.get_barrier_semaphore()
    around = [at(0, 0, 1), at(0, 0, -1)]
    for o in (1, -1, 2, -2, 3, -3):
        around += [at(o, 0, 0), at(0, o, 0)]
    for who in around:
        pl.semaphore_signal(barrier, inc=1, device_id=who, device_id_type=MESH)

    number = [0]

    def remote(src, dst, who):
        i = number[0]
        number[0] += 1
        copy = pltpu.make_async_remote_copy(
            src_ref=src, dst_ref=dst, send_sem=send.at[i], recv_sem=recv.at[i],
            device_id=who, device_id_type=MESH,
        )
        copy.start()
        return copy

    for x in range(4):
        block = lm[x].astype(F32)
        for zp in range(6):
            ms[zp * 16 + x * 4 : zp * 16 + x * 4 + 4, :] = block[:, zp * 128 : zp * 128 + 128]
    for x in range(2):
        block = am[x].astype(F32)
        for zp in range(3):
            ms[96 + zp * 4 + x * 2 : 98 + zp * 4 + x * 2, :] = block[:, zp * 128 : zp * 128 + 128]
    bcells = bm[0].astype(F32)
    ms[108:109, :] = bcells[:, 0:128]
    ms[109:110, :] = jnp.concatenate([bcells[:, 64:128], bcells[:, 128:192]], axis=1)
    ms[110:112, :] = jnp.zeros((2, 128), F32)
    row, col = iota((128, 128), 0), iota((128, 128), 1)
    moved = (row & 64) + ((row & 1) << 5) + ((row & 63) >> 1)
    order = jnp.where(moved == col, 1.0, 0.0).astype(BF16)
    ms[...] = jnp.dot(ms[...].astype(BF16), order, preferred_element_type=F32)

    ps[...] = jnp.zeros_like(ps)
    mas[...] = jnp.zeros_like(mas)
    zf[...] = jnp.zeros_like(zf)
    for x in range(4):
        fields = [pos[0, x] - 0.5, pos[1, x] - 0.5, pos[2, x] - 0.5, chg[x], soft[x]]
        counts = cnt[x]
        for zp in range(6):
            limit, slot = count_lanes(counts, zp)
            for f in range(5):
                piece = fields[f][:, zp * 128 : zp * 128 + 128]
                if f == 3:
                    piece = jnp.where(slot < limit, piece, 0.0)
                ps[pl.ds(x * 192 + f * 8 + 1 + zp, 4, stride=48), :] = piece
                if zp == 0:
                    zf[f * 16 + x * 4 : f * 16 + x * 4 + 4, :] = piece
                if zp == 5:
                    zf[112 + f * 16 + x * 4 : 112 + f * 16 + x * 4 + 4, :] = piece
    for side, (lp, ap) in enumerate(((0, 0), (5, 2))):
        base = side * 112
        zf[base + 80 : base + 96, :] = ms[lp * 16 : lp * 16 + 16, :]
        zf[base + 96 : base + 100, :] = ms[96 + ap * 4 : 100 + ap * 4, :]
        zf[base + 100 : base + 102, :] = ms[108:110, :]
        zs[side] = zf[base : base + 112, :].astype(BF16)
    pl.semaphore_wait(barrier, 14)

    z_copies = [
        remote(zs.at[0], zr.at[1], at(0, 0, -1)),
        remote(zs.at[1], zr.at[0], at(0, 0, 1)),
    ]
    for zp in range(6):
        for x in range(4):
            mls[pl.ds(x * 32 + zp + 1, 4, stride=8), :] = ms[
                zp * 16 + x * 4 : zp * 16 + x * 4 + 4, :
            ]
    for zp in range(3):
        for x in range(2):
            mas[pl.ds(x * 16 + zp + 1, 2, stride=8), :] = ms[
                96 + zp * 4 + x * 2 : 98 + zp * 4 + x * 2, :
            ]

    table.wait()

    def unpack(i, carry):
        block = mt[pl.ds(pl.multiple_of(i * 16, 16), 16), :].astype(F32)
        unpack_rows(block, i * 16, s2, 16)
        return carry

    lax.fori_loop(0, 21, unpack, 0)
    unpack_rows(mt[336:343, :].astype(F32), 336, s2, 7)
    unpack_rows(l2l[...].astype(F32), 343, s2, 8)

    for copy in z_copies:
        copy.wait()
    keep_low = jnp.where(gz > 0, 1.0, 0.0).astype(F32)
    keep_high = jnp.where(gz < 7, 1.0, 0.0).astype(F32)
    b_rows = []
    for side, (keep, zp_l, zp_a) in enumerate(((keep_low, 0, 0), (keep_high, 7, 4))):
        got = zr[side].astype(F32) * keep
        for x in range(4):
            for f in range(5):
                ps[pl.ds(x * 192 + f * 8 + zp_l, 4, stride=48), :] = got[
                    f * 16 + x * 4 : f * 16 + x * 4 + 4, :
                ]
            mls[pl.ds(x * 32 + zp_l, 4, stride=8), :] = got[80 + x * 4 : 84 + x * 4, :]
        for x in range(2):
            mas[pl.ds(x * 16 + zp_a, 2, stride=8), :] = got[96 + x * 2 : 98 + x * 2, :]
        b_rows.append((got[100:101, :], got[101:102, :]))
    (la, lb), (ra, rb) = b_rows
    oa, ob = ms[108:109, :], ms[109:110, :]
    low1 = iota((1, 128), 1) < 64
    middle = jnp.where(low1, pltpu.roll(lb, 64, 1), pltpu.roll(oa, 64, 1))
    middle_r = jnp.where(low1, pltpu.roll(ob, 64, 1), pltpu.roll(ra, 64, 1))
    pairs = [la, lb, middle, oa, ob, middle_r, ra, rb]
    even_z = lax.rem(gz, 2) == 0
    zf[0:16, :] = jnp.zeros((16, 128), F32)
    for l in range(3):
        at_even = l + 1 - l % 2
        at_odd = l + 1 - (l + 1) % 2
        for j in range(3):
            zf[4 * j + l : 4 * j + l + 1, :] = jnp.where(
                even_z, pairs[at_even + 2 * j], pairs[at_odd + 2 * j]
            )
    mb[3, 3] = zf[0:16, :].astype(BF16)
    x_b = []
    for o in (1, -1, 2, -2, 3, -3):
        x_b.append(remote(mb.at[3, 3], mb.at[3 - o, 3], at(o, 0, 0)))
    for x in range(4):
        for y in range(4):
            for t in range(3):
                r = (x * 4 + y) * 48 + t * 16
                pf[1 + x, 1 + y, t] = ps[r : r + 16, :].astype(BF16)
        for yp in range(2):
            r = x * 32 + yp * 16
            ml[2 + x, 1 + yp] = mls[r : r + 16, :].astype(BF16)
    for x in range(2):
        ma[2 + x, 1] = mas[x * 16 : x * 16 + 16, :].astype(BF16)

    own_x, own_xl, own_xa = pl.ds(1, 4), pl.ds(2, 4), pl.ds(2, 2)
    up, down = at(0, 1, 0), at(0, -1, 0)
    y_copies = [
        remote(pf.at[own_x, pl.ds(4, 1)], pf.at[own_x, pl.ds(0, 1)], up),
        remote(pf.at[own_x, pl.ds(1, 1)], pf.at[own_x, pl.ds(5, 1)], down),
        remote(ml.at[own_xl, pl.ds(2, 1)], ml.at[own_xl, pl.ds(0, 1)], up),
        remote(ml.at[own_xl, pl.ds(1, 1)], ml.at[own_xl, pl.ds(3, 1)], down),
        remote(ma.at[own_xa, pl.ds(1, 1)], ma.at[own_xa, pl.ds(0, 1)], up),
        remote(ma.at[own_xa, pl.ds(1, 1)], ma.at[own_xa, pl.ds(2, 1)], down),
    ]

    low_lanes = iota((32, 128), 1) < 64

    def pair_up(g, carry):
        near = (jnp.abs(g // 7 - 3) <= 1) & (jnp.abs(lax.rem(g, 7) - 3) <= 1)
        kept = jnp.where(near, 0.0, 1.0).astype(F32)
        tables = []
        for i in range(7):
            one = s2[pl.ds(pl.multiple_of((g * 7 + i) * 32, 32), 32), :]
            if 2 <= i <= 4:
                one = one * kept
            tables.append((one, pltpu.roll(one, 64, 1)))
        for w in range(6):
            (first, turned_first), (second, turned_second) = tables[w + 1], tables[w]
            to = g * 384 + w * 64
            t2[pl.ds(pl.multiple_of(to, 32), 32), :] = jnp.where(
                low_lanes, first, turned_second
            ).astype(BF16)
            t2[pl.ds(pl.multiple_of(to + 32, 32), 32), :] = jnp.where(
                low_lanes, turned_first, second
            ).astype(BF16)
        return carry

    lax.fori_loop(0, 20, pair_up, 0)
    for copy in x_b:
        copy.wait()
    y_b = []
    for o in (1, -1, 2, -2, 3, -3):
        y_b.append(remote(mb.at[:, pl.ds(3, 1)], mb.at[:, pl.ds(3 - o, 1)], at(0, o, 0)))
    for copy in y_copies:
        copy.wait()

    up, down = at(1, 0, 0), at(-1, 0, 0)
    x_copies = [
        remote(pf.at[pl.ds(4, 1)], pf.at[pl.ds(0, 1)], up),
        remote(pf.at[pl.ds(1, 1)], pf.at[pl.ds(5, 1)], down),
        remote(ml.at[pl.ds(4, 2)], ml.at[pl.ds(0, 2)], up),
        remote(ml.at[pl.ds(2, 2)], ml.at[pl.ds(6, 2)], down),
        remote(ma.at[pl.ds(2, 2)], ma.at[pl.ds(0, 2)], up),
        remote(ma.at[pl.ds(2, 2)], ma.at[pl.ds(4, 2)], down),
    ]
    lax.fori_loop(20, 49, pair_up, 0)
    for child in range(4):
        r = (343 + 2 * child) * 32
        even, odd = pair_rows(s2[r : r + 32, :], s2[r + 32 : r + 64, :], low_lanes)
        to = 49 * 384 + child * 64
        t2[to : to + 32, :] = even
        t2[to + 32 : to + 64, :] = odd
    for copy in x_copies + y_b:
        copy.wait()
    pf_out[...] = pf[...]
    ml_out[...] = ml[...]
    ma_out[...] = ma[...]
    mb_out[...] = mb[...]


def exchange(pos, chg, soft, cnt, bm, am, lm, m2l, l2l):
    vmem = pl.BlockSpec(memory_space=pltpu.VMEM)
    sizes = [(6, 6, 3, 16, 128), (8, 4, 16, 128), (6, 3, 16, 128), (7, 7, 16, 128)]
    return pl.pallas_call(
        exchange_kernel,
        name="exchange",
        out_shape=[jax.ShapeDtypeStruct(s, BF16) for s in sizes + [(T2_ROWS, 128)]],
        in_specs=[vmem] * 7 + [pl.BlockSpec(memory_space=pl.ANY), vmem],
        out_specs=[vmem] * 5,
        scratch_shapes=[pltpu.VMEM(s, BF16) for s in sizes]
        + [
            pltpu.VMEM((2, 112, 128), BF16),
            pltpu.VMEM((2, 112, 128), BF16),
            pltpu.VMEM((768, 128), F32),
            pltpu.VMEM((128, 128), F32),
            pltpu.VMEM((32, 128), F32),
            pltpu.VMEM((112, 128), F32),
            pltpu.VMEM((224, 128), F32),
            pltpu.VMEM((343, 4096), BF16),
            pltpu.VMEM((352 * 32, 128), F32),
            pltpu.SemaphoreType.DMA((26,)),
            pltpu.SemaphoreType.DMA((26,)),
            pltpu.SemaphoreType.DMA((1,)),
        ],
        compiler_params=pltpu.CompilerParams(
            collective_id=0, has_side_effects=True, vmem_limit_bytes=40 * 2**20
        ),
        cost_estimate=pl.CostEstimate(flops=10**7, bytes_accessed=10**7, transcendentals=0),
    )(pos, chg, soft, cnt, bm, am, lm, m2l, l2l)


def pieces(value, count):
    out = []
    for _ in range(count - 1):
        head = value.astype(BF16).astype(F32)
        out.append(head)
        value = value - head
    return out + [value]


def compute_kernel(
    gx, gy, gz,
    pf, ml, ma, mb, t2, pos, soft, cnt, top,
    pot_out, loc_out,
    a_mat, q_mat, b_mat, ft, fs, wt, near, lw, la, lb, lr, pa, ln,
):
    ones = jnp.ones((8, 128), F32)
    zp_row = iota((8, 128), 0)
    er, ec = iota((16, 1664), 0), iota((16, 1664), 1)
    leaf_of = jnp.where(ec < 768, (ec >> 6) + 2, ((ec - 768) >> 6) + 1)
    spread = jnp.where(((er & 7) * 2 + (er >> 3)) == leaf_of, 1.0, 0.0).astype(BF16)

    def column(c, slot):
        cx, cy = c // 6, lax.rem(c, 6)
        xy = pf[cx, cy, 0].astype(F32)
        zq = pf[cx, cy, 1].astype(F32)
        s = pf[cx, cy, 2].astype(F32)[0:8]
        x, y, z, q = xy[0:8], xy[8:16], zq[0:8], zq[8:16]
        out = ((cx == 0) & (gx == 0)) | ((cx == 5) & (gx == 7))
        out = out | ((cy == 0) & (gy == 0)) | ((cy == 5) & (gy == 7))
        q = q * jnp.where(out, 0.0, 1.0).astype(F32)
        fx, fy = cx.astype(F32) - 2.5, cy.astype(F32) - 2.5
        ix, iy = ones * fx, ones * fy
        n = (x + ix) * (x + ix) + (y + iy) * (y + iy) + z * z + 0.5 * (s * s)
        feats = [x, x, ix, ix, y, y, iy, iy, z, z, ones, ones, ones] + pieces(n, 3)
        for f in range(16):
            wt[slot, pl.ds(f, 8, stride=16), :] = feats[f]
        turned = wt[slot].T.astype(BF16)
        rows = pl.ds(pl.multiple_of(c * 64, 64), 64)
        a_mat[rows, 0:128] = turned[0:64]
        a_mat[rows, 128:256] = turned[64:128]
        qt = q.T
        qq = jnp.concatenate([qt[0:64], qt[64:128]], axis=1).astype(BF16)
        q_mat[rows, :] = jnp.dot(qq, spread, preferred_element_type=F32).astype(BF16)

    def columns(i, carry):
        for u in range(4):
            column(i * 4 + u, u)
        return carry

    lax.fori_loop(0, 9, columns, 0)

    lane = iota((64, 128), 1)

    def put(f, v):
        for zp in range(6):
            fs[zp, pl.ds(f, 4, stride=16), :] = v[:, zp * 128 : zp * 128 + 128]

    for x in range(4):
        px, py, pz = (pos[d, x] - 0.5 for d in range(3))
        s = soft[x]
        fx = px + (x - 1.5)
        fy = py + (iota((4, 768), 0).astype(F32) - 1.5)
        ax, bx = pieces(fx, 2)
        ay, by = pieces(fy, 2)
        bx, by = bx.astype(BF16).astype(F32), by.astype(BF16).astype(F32)
        xx, yy = ax + bx, ay + by
        base = xx * xx + yy * yy + 0.5 * (s * s)
        for f, v in ((0, ax), (1, bx), (2, ax), (3, bx), (4, ay), (5, by), (6, ay), (7, by)):
            put(f, -2.0 * v)
        for f in (13, 14, 15):
            put(f, jnp.ones((4, 768), F32))
        for d in range(3):
            az, bz = pieces(pz - (d - 1.0), 2)
            bz = bz.astype(BF16).astype(F32)
            zz = az + bz
            n = base + zz * zz
            for f, v in zip((8, 9, 10, 11, 12), [-2.0 * az, -2.0 * bz] + pieces(n, 3)):
                put(f, v)
            for zp in range(6):
                made = fs[zp]
                for e in range(2):
                    mine = lane < 64 if e == 0 else lane >= 64
                    half = jnp.where(mine, made, 0.0).astype(BF16)
                    for y in range(4):
                        ft[x * 4 + y, d, e, :, zp * 128 : zp * 128 + 128] = half[
                            y * 16 : y * 16 + 16
                        ]

    b_mat[...] = jnp.zeros_like(b_mat)
    other = jnp.where(iota((64, 256), 0) == (iota((64, 256), 1) & 63), 0.0, 1.0).astype(F32)
    other = jnp.concatenate([jnp.ones((64, 256), F32), other, jnp.ones((64, 256), F32)], axis=0)
    offsets = (768, 0, 896)

    def group(g, carry):
        x, y = g // 4, lax.rem(g, 4)
        for k in range(3):
            for d in range(3):
                for h in range(2):
                    for e in range(2):
                        cell = 4 * k + 2 + 2 * h + e + d - 1
                        r = (cell % 2) * 128 + (cell // 2) * 16
                        b_mat[k * 3 + d, r : r + 16, h * 128 : h * 128 + 128] = ft[
                            g, d, e, :, (2 * k + h) * 128 : (2 * k + h) * 128 + 128
                        ]
        for k in range(3):
            acc = jnp.zeros((8, 256), F32)
            for d in range(3):
                weights = b_mat[k * 3 + d]
                at_q = offsets[d] + 256 * k
                for dx in range(3):
                    rows = pl.ds(pl.multiple_of(((x + dx) * 6 + y) * 64, 64), 192)
                    r2 = jnp.dot(a_mat[rows, :], weights, preferred_element_type=F32)
                    q = q_mat[rows, at_q : at_q + 256].astype(F32)
                    if d == 1 and dx == 1:
                        q = q * other
                    acc = acc + jnp.sum((lax.rsqrt(r2) * q).reshape(24, 8, 256), axis=0)
            near[pl.ds(g, 1), k * 256 : k * 256 + 256] = jnp.sum(acc, axis=0, keepdims=True)
        return carry

    lax.fori_loop(0, 16, group, 0)

    def shifted(v):
        return [v, pltpu.roll(v, 7, 0), pltpu.roll(v, 6, 0)]

    def inside(coord, offset):
        return (coord + offset >= 0) & (coord + offset <= 7)

    for xs in range(8):
        over_x = -1 if xs < 2 else (1 if xs >= 6 else 0)
        turned = []
        for yp in range(4):
            over_y = -1 if yp < 1 else (1 if yp >= 3 else 0)
            keep = jnp.where(inside(gx, over_x) & inside(gy, over_y), 1.0, 0.0).astype(F32)
            tile = ml[xs, yp].astype(F32) * keep
            turned.append((shifted(tile[0:8]), shifted(tile[8:16])))
        for w in range(6):
            for j in range(3):
                lw[xs, w, :, j * 128 : j * 128 + 128] = jnp.concatenate(
                    [turned[w // 2][w % 2][j], turned[w // 2 + 1][w % 2][j]], axis=0
                ).astype(BF16)
    zero8 = jnp.zeros((8, 128), F32)
    a_tiles = {}
    for xs in range(6):
        over_x = -1 if xs < 2 else (1 if xs >= 4 else 0)
        for yp in range(3):
            over_y = yp - 1
            keep = jnp.where(inside(gx, over_x) & inside(gy, over_y), 1.0, 0.0).astype(F32)
            tile = ma[xs, yp].astype(F32) * keep
            a_tiles[xs, yp] = (shifted(tile[0:8]), shifted(tile[8:16]))
    for dx in range(7):
        for w in range(6):
            for j in range(3):
                first = a_tiles[dx - 1, w // 2][w % 2][j] if dx >= 1 else zero8
                second = a_tiles[dx, w // 2][w % 2][j] if dx <= 5 else zero8
                la[dx, w, :, j * 128 : j * 128 + 128] = jnp.concatenate(
                    [first, second], axis=0
                ).astype(BF16)
    row16 = iota((16, 128), 0)
    odd_x, odd_y = lax.rem(gx, 2), lax.rem(gy, 2)
    for dx in range(7):
        ok_x = inside(gx, dx - 3)
        if dx == 0:
            ok_x = ok_x & (odd_x == 1)
        if dx == 6:
            ok_x = ok_x & (odd_x == 0)
        for w in range(6):
            dy = w + 1 - odd_y
            keep = jnp.where(ok_x & inside(gy, dy - 3), 1.0, 0.0).astype(F32)
            tile = mb[dx, dy].astype(F32) * keep
            for j in range(3):
                lb[dx, w, :, j * 128 : j * 128 + 128] = jnp.where(
                    (row16 >> 2) == j, tile, 0.0
                ).astype(BF16)

    total = [jnp.zeros((16, 256), F32) for _ in range(6)]
    for dx in range(7):
        xs_of = [x for x in range(4) if not (dx == 0 and x % 2 == 0) and not (dx == 6 and x % 2 == 1)]
        for w in range(6):
            g = dx * 7 + w + 1
            weights = jnp.concatenate(
                [t2[g * 384 : (g + 1) * 384, :], t2[(g - 1) * 384 : g * 384, :]], axis=1
            )
            left = [lw[x + dx - 1, w] for x in xs_of] + [la[dx, w], lb[dx, w]]
            made = jnp.dot(
                jnp.concatenate(left, axis=0), weights, preferred_element_type=F32
            )
            for i, slot in enumerate(xs_of + [4, 5]):
                total[slot] = total[slot] + made[i * 16 : i * 16 + 16]

    row, col = iota((64, 64), 0), iota((64, 64), 1)
    order = jnp.where(((row & 1) << 5) + (row >> 1) == col, 1.0, 0.0).astype(BF16)

    def ordered(v):
        return jnp.dot(v.astype(BF16), order, preferred_element_type=F32).astype(BF16)

    v_of = []
    for px in range(2):
        r = 49 * 384 + px * 128
        v_of.append(jnp.concatenate([t2[r : r + 64, :], t2[r + 64 : r + 128, :]], axis=1))
    sb = total[5]
    sb = sb[0:4] + sb[4:8] + sb[8:12]
    sb = jnp.where(odd_y == 1, sb[:, 128:256], sb[:, 0:128])
    parity = lax.rem(iota((4, 64), 0) + gz, 2)
    sb = jnp.where(parity == 1, sb[:, 64:128], sb[:, 0:64])
    topv = top[0]
    top4 = jnp.concatenate(
        [topv[:, 0:64], topv[:, 64:128], topv[:, 128:192], jnp.zeros((1, 64), F32)], axis=0
    )
    local_b = ordered(jnp.concatenate([top4 + 0.25 * sb, jnp.zeros((12, 64), F32)], axis=0))
    for xa in range(2):
        down = jnp.dot(local_b, v_of[xa], preferred_element_type=F32)[0:4]
        local_a = 0.5 * total[4][xa * 8 : xa * 8 + 4] + down
        for ya in range(2):
            for p in range(2):
                b = ya * 128 + p * 64
                pa[pl.ds(xa * 16 + ya * 8 + p, 4, stride=2), 0:64] = local_a[:, b : b + 64]
    for xa in range(2):
        parent = ordered(pa[xa * 16 : xa * 16 + 16, 0:64])
        for px in range(2):
            x = 2 * xa + px
            leaf = total[x] + jnp.dot(parent, v_of[px], preferred_element_type=F32)
            lr[x * 32 : x * 32 + 16, :] = leaf[:, 0:128]
            lr[x * 32 + 16 : x * 32 + 32, :] = leaf[:, 128:256]
    for x in range(4):
        for y in range(4):
            for zp in range(6):
                r = x * 32 + (y % 2) * 16 + (y // 2) * 8 + zp
                ln[x * 4 + y : x * 4 + y + 1, zp * 128 : zp * 128 + 128] = lr[r : r + 1, :]

    lane8 = iota((8, 128), 1)
    for i in range(2):
        for zp in range(6):
            lanes = slice(zp * 128, zp * 128 + 128)
            coef = ln[i * 8 : i * 8 + 8, lanes]
            cheb = []
            for d in range(3):
                u = 2.0 * jnp.concatenate(
                    [pos[d, 2 * i, :, lanes], pos[d, 2 * i + 1, :, lanes]], axis=0
                ) - 1.0
                t2nd = 2.0 * u * u - 1.0
                cheb.append([None, u, t2nd, 2.0 * u * t2nd - u])
            out = None
            for a in range(4):
                sum_b = None
                for b in range(4):
                    sum_c = None
                    for c in range(4):
                        index = (lane8 & 64) + (16 * a + 4 * b + c)
                        term = jnp.take_along_axis(coef, index, axis=1, mode="promise_in_bounds")
                        if c:
                            term = term * cheb[2][c]
                        sum_c = term if sum_c is None else sum_c + term
                    if b:
                        sum_c = sum_c * cheb[1][b]
                    sum_b = sum_c if sum_b is None else sum_b + sum_c
                if a:
                    sum_b = sum_b * cheb[0][a]
                out = sum_b if out is None else out + sum_b
            value = out * 0.125 + near[i * 8 : i * 8 + 8, lanes]
            limit, slot = count_lanes(
                jnp.concatenate([cnt[2 * i], cnt[2 * i + 1]], axis=0), zp
            )
            value = jnp.where(slot < limit, value, 0.0)
            for h in range(2):
                pot_out[2 * i + h, :, lanes] = value[h * 4 : h * 4 + 4]
                loc_out[2 * i + h, :, lanes] = coef[h * 4 : h * 4 + 4]


def compute_entry(*refs):
    compute_kernel(*(lax.axis_index(a) for a in AXES), *refs)


def compute(pf, ml, ma, mb, t2, pos, soft, cnt, top, body=compute_entry):
    vmem = pl.BlockSpec(memory_space=pltpu.VMEM)
    return pl.pallas_call(
        body,
        name="compute",
        out_shape=[jax.ShapeDtypeStruct((4, 4, 768), F32)] * 2,
        in_specs=[vmem] * 9,
        out_specs=[vmem] * 2,
        scratch_shapes=[
            pltpu.VMEM((2304, 256), BF16),
            pltpu.VMEM((2304, 1664), BF16),
            pltpu.VMEM((9, 256, 256), BF16),
            pltpu.VMEM((16, 3, 2, 16, 768), BF16),
            pltpu.VMEM((6, 64, 128), F32),
            pltpu.VMEM((4, 128, 128), F32),
            pltpu.VMEM((16, 768), F32),
            pltpu.VMEM((8, 6, 16, 384), BF16),
            pltpu.VMEM((7, 6, 16, 384), BF16),
            pltpu.VMEM((7, 6, 16, 384), BF16),
            pltpu.VMEM((128, 128), F32),
            pltpu.VMEM((32, 128), F32),
            pltpu.VMEM((16, 768), F32),
        ],
        compiler_params=pltpu.CompilerParams(vmem_limit_bytes=48 * 2**20),
        cost_estimate=pl.CostEstimate(flops=10**10, bytes_accessed=10**7, transcendentals=2 * 10**7),
    )(pf, ml, ma, mb, t2, pos, soft, cnt, top)


def per_device(pos, chg, soft, cnt, top, bm, am, lm, m2l, l2l):
    halos = exchange(pos, chg, soft, cnt, bm, am, lm, m2l, l2l)
    return tuple(compute(*halos, pos, soft, cnt, top))


def solution(mesh):
    split = P("gx", "gy", "gz")
    in_specs = (P(None, "gx", "gy", "gz"),) + (split,) * 7 + (P(), P())
    return jax.shard_map(
        per_device, mesh=mesh, in_specs=in_specs, out_specs=(split, split), check_vma=False
    )
```

```python
import functools
import jax
import jax.numpy as jnp
from jax import lax
from jax.experimental import pallas as pl
from jax.experimental.pallas import tpu as pltpu
from jax.sharding import PartitionSpec as P

F32 = jnp.float32
BF16 = jnp.bfloat16
MESH = pl.DeviceIdType.MESH
AXES = ("gx", "gy", "gz")
T2_ROWS = 49 * 384 + 256
VMEM_BYTES = 63 * 2**20


def iota(shape, dim):
    return lax.broadcasted_iota(jnp.int32, shape, dim)


def count_lanes(counts, pair):
    rows = counts.shape[0]
    lane = iota((rows, 128), 1)
    low = counts[:, 2 * pair : 2 * pair + 1]
    high = counts[:, 2 * pair + 1 : 2 * pair + 2]
    return jnp.where(lane < 64, low, high), lane & 63


def unpack_rows(block, base, s2, rows):
    for c in range(32):
        s2[pl.ds(base * 32 + c, rows, stride=32), :] = block[:, c * 128 : (c + 1) * 128]


def pair_rows(first, second, low_lanes):
    turned_first = pltpu.roll(first, 64, 1)
    turned_second = pltpu.roll(second, 64, 1)
    even = jnp.where(low_lanes, first, turned_second)
    odd = jnp.where(low_lanes, turned_first, second)
    return even.astype(BF16), odd.astype(BF16)


def pieces(value, count):
    out = []
    for _ in range(count - 1):
        head = value.astype(BF16).astype(F32)
        out.append(head)
        value = value - head
    return out + [value]


def inside(coord, offset):
    return (coord + offset >= 0) & (coord + offset <= 7)


def source_columns(where, gx, gy, pf, wt, a_mat, q_mat):
    ones = jnp.ones((8, 128), F32)
    same = jnp.where(iota((128, 128), 0) == iota((128, 128), 1), 1.0, 0.0).astype(BF16)
    er, ec = iota((16, 1024), 0), iota((16, 1024), 1)
    spread = jnp.where(((er & 7) * 2 + (er >> 3)) == (ec >> 6), 1.0, 0.0).astype(BF16)
    charges = []
    for slot, (cx, cy) in enumerate(where):
        xy = pf[cx, cy, 0].astype(F32)
        zq = pf[cx, cy, 1].astype(F32)
        s = pf[cx, cy, 2].astype(F32)[0:8]
        x, y, z, q = xy[0:8], xy[8:16], zq[0:8], zq[8:16]
        over_x = jnp.where(cx == 0, -1, jnp.where(cx == 5, 1, 0))
        over_y = jnp.where(cy == 0, -1, jnp.where(cy == 5, 1, 0))
        q = q * jnp.where(inside(gx, over_x) & inside(gy, over_y), 1.0, 0.0).astype(F32)
        ix = ones * (jnp.asarray(cx, F32) - 2.5)
        iy = ones * (jnp.asarray(cy, F32) - 2.5)
        n = (x + ix) * (x + ix) + (y + iy) * (y + iy) + z * z + 0.5 * (s * s)
        feats = [x, x, ix, ix, y, y, iy, iy, z, z, ones, ones, ones] + pieces(n, 3)
        for f in range(16):
            wt[slot, pl.ds(f, 8, stride=16), :] = feats[f]
        wt[slot, 128:136, :] = q
    for slot, (cx, cy) in enumerate(where):
        turned = lax.dot_general(
            same, wt[slot].astype(BF16), (((1,), (1,)), ((), ())), preferred_element_type=F32
        )
        rows = pl.ds(pl.multiple_of((cx * 6 + cy) * 64, 64), 64)
        a_mat[rows, 0:128] = turned[0:64, 0:128].astype(BF16)
        a_mat[rows, 128:256] = turned[64:128, 0:128].astype(BF16)
        charges.append(
            jnp.concatenate([turned[0:64, 128:136], turned[64:128, 128:136]], axis=1)
        )
    wide = jnp.dot(
        jnp.concatenate(charges, axis=0).astype(BF16), spread, preferred_element_type=F32
    )
    low = iota((64, 128), 1) < 64
    for slot, (cx, cy) in enumerate(where):
        rows = pl.ds(pl.multiple_of((cx * 6 + cy) * 64, 64), 64)
        v = [wide[slot * 64 : slot * 64 + 64, m * 128 : m * 128 + 128] for m in range(8)]
        for m in range(6):
            q_mat[rows, m * 128 : m * 128 + 128] = v[m + 1].astype(BF16)
        for m in range(7):
            q_mat[rows, 768 + m * 128 : 896 + m * 128] = jnp.where(low, v[m + 1], v[m]).astype(BF16)


def target_features(pos, soft, fs, ft):
    lane = iota((64, 128), 1)

    def put(f, v):
        for zp in range(6):
            fs[zp, pl.ds(f, 4, stride=16), :] = v[:, zp * 128 : zp * 128 + 128]

    for x in range(4):
        px, py, pz = (pos[d, x] - 0.5 for d in range(3))
        s = soft[x]
        fx = px + (x - 1.5)
        fy = py + (iota((4, 768), 0).astype(F32) - 1.5)
        ax, bx = pieces(fx, 2)
        ay, by = pieces(fy, 2)
        bx, by = bx.astype(BF16).astype(F32), by.astype(BF16).astype(F32)
        xx, yy = ax + bx, ay + by
        base = xx * xx + yy * yy + 0.5 * (s * s)
        for f, v in ((0, ax), (1, bx), (2, ax), (3, bx), (4, ay), (5, by), (6, ay), (7, by)):
            put(f, -2.0 * v)
        for f in (13, 14, 15):
            put(f, jnp.ones((4, 768), F32))
        for d in range(3):
            az, bz = pieces(pz - (d - 1.0), 2)
            bz = bz.astype(BF16).astype(F32)
            zz = az + bz
            n = base + zz * zz
            for f, v in zip((8, 9, 10, 11, 12), [-2.0 * az, -2.0 * bz] + pieces(n, 3)):
                put(f, v)
            for zp in range(6):
                made = fs[zp]
                if d != 1:
                    made = pltpu.roll(made, 64, 1)
                for e in range(2):
                    mine = lane < 64 if (e == 0) == (d == 1) else lane >= 64
                    half = jnp.where(mine, made, 0.0).astype(BF16)
                    for y in range(4):
                        ft[x * 4 + y, d, e, :, zp * 128 : zp * 128 + 128] = half[
                            y * 16 : y * 16 + 16
                        ]


Q_AT = (768, 0, 896)


def set_weights(b_mat, slot, ft, g):
    for k in range(3):
        for d in range(3):
            for h in range(2):
                for e in range(2):
                    cell = 4 * k + 2 + 2 * h + e + d - 1
                    r = (cell % 2) * 128 + (cell // 2) * 16
                    b_mat[slot, k * 3 + d, r : r + 16, h * 128 : h * 128 + 128] = ft[
                        g, d, e, :, (2 * k + h) * 128 : (2 * k + h) * 128 + 128
                    ]


def add_pairs(left, q_of, b_mat, slot, near8, g, own=None):
    rows = left.shape[0]
    for k in range(3):
        lanes = slice(256 * k, 256 * k + 256)
        for d in range(3):
            r2 = jnp.dot(left, b_mat[slot, k * 3 + d], preferred_element_type=F32)
            q = q_of(Q_AT[d] + 256 * k).astype(F32)
            if d == 1 and own is not None:
                q = q * own
            part = jnp.sum((lax.rsqrt(r2) * q).reshape(rows // 8, 8, 256), axis=0)
            if d == 0:
                swapped = part
            elif d == 1:
                plain = part
            else:
                swapped = swapped + part
        near8[g, 0, :, lanes] += plain
        near8[g, 1, :, lanes] += swapped


def slab_pairs(t, a_mat, q_mat, b_mat, ft, near8):
    x, dx = t // 3, lax.rem(t, 3)
    cx = x + dx
    itself = jnp.where(iota((64, 256), 0) == (iota((64, 256), 1) & 63), 0.0, 1.0).astype(F32)
    itself = jnp.where(dx == 1, itself, 1.0)
    one = jnp.ones((64, 256), F32)
    for y in range(4):
        low, high = max(1, y), min(4, y + 2)
        set_weights(b_mat, y, ft, x * 4 + y)
        rows = pl.ds(pl.multiple_of((cx * 6 + low) * 64, 64), (high - low + 1) * 64)
        own = jnp.concatenate([itself if cy == y + 1 else one for cy in range(low, high + 1)], axis=0)
        add_pairs(
            a_mat[rows, :], lambda at: q_mat[rows, at : at + 256], b_mat, y, near8, x * 4 + y, own
        )


def edge_pairs(x, a_mat, q_mat, b_mat, ft, near8):
    for slot, (y, cy) in enumerate(((0, 0), (3, 5))):
        set_weights(b_mat, slot, ft, x * 4 + y)
        rows = [pl.ds(pl.multiple_of(((x + i) * 6 + cy) * 64, 64), 64) for i in range(3)]
        add_pairs(
            jnp.concatenate([a_mat[r, :] for r in rows], axis=0),
            lambda at: jnp.concatenate([q_mat[r, at : at + 256] for r in rows], axis=0),
            b_mat, slot, near8, x * 4 + y,
        )


def gather_near(near8, near):
    for g in range(16):
        for zp in range(6):
            lanes = slice(zp * 128, zp * 128 + 128)
            both = near8[g, 0, :, lanes] + pltpu.roll(near8[g, 1, :, lanes], 64, 1)
            near[g : g + 1, lanes] = jnp.sum(both, axis=0, keepdims=True)


def far_kernel(
    gx, gy, gz,
    ml, ma, mb, t2, near, pos, cnt, top,
    pot_out, loc_out,
    lw, la, lb, lr, pa, ln,
):
    def shifted(v):
        return [v, pltpu.roll(v, 7, 0), pltpu.roll(v, 6, 0)]

    for xs in range(8):
        over_x = -1 if xs < 2 else (1 if xs >= 6 else 0)
        turned = []
        for yp in range(4):
            over_y = -1 if yp < 1 else (1 if yp >= 3 else 0)
            keep = jnp.where(inside(gx, over_x) & inside(gy, over_y), 1.0, 0.0).astype(F32)
            tile = ml[xs, yp].astype(F32) * keep
            turned.append((shifted(tile[0:8]), shifted(tile[8:16])))
        for w in range(6):
            for j in range(3):
                lw[xs, w, :, j * 128 : j * 128 + 128] = jnp.concatenate(
                    [turned[w // 2][w % 2][j], turned[w // 2 + 1][w % 2][j]], axis=0
                ).astype(BF16)
    zero8 = jnp.zeros((8, 128), F32)
    a_tiles = {}
    for xs in range(6):
        over_x = -1 if xs < 2 else (1 if xs >= 4 else 0)
        for yp in range(3):
            over_y = yp - 1
            keep = jnp.where(inside(gx, over_x) & inside(gy, over_y), 1.0, 0.0).astype(F32)
            tile = ma[xs, yp].astype(F32) * keep
            a_tiles[xs, yp] = (shifted(tile[0:8]), shifted(tile[8:16]))
    for dx in range(7):
        for w in range(6):
            for j in range(3):
                first = a_tiles[dx - 1, w // 2][w % 2][j] if dx >= 1 else zero8
                second = a_tiles[dx, w // 2][w % 2][j] if dx <= 5 else zero8
                la[dx, w, :, j * 128 : j * 128 + 128] = jnp.concatenate(
                    [first, second], axis=0
                ).astype(BF16)
    row16 = iota((16, 128), 0)
    odd_x, odd_y = lax.rem(gx, 2), lax.rem(gy, 2)
    for dx in range(7):
        ok_x = inside(gx, dx - 3)
        if dx == 0:
            ok_x = ok_x & (odd_x == 1)
        if dx == 6:
            ok_x = ok_x & (odd_x == 0)
        for w in range(6):
            dy = w + 1 - odd_y
            keep = jnp.where(ok_x & inside(gy, dy - 3), 1.0, 0.0).astype(F32)
            tile = mb[dx, dy].astype(F32) * keep
            for j in range(3):
                lb[dx, w, :, j * 128 : j * 128 + 128] = jnp.where(
                    (row16 >> 2) == j, tile, 0.0
                ).astype(BF16)

    total = [jnp.zeros((16, 256), F32) for _ in range(6)]
    for dx in range(7):
        xs_of = [x for x in range(4) if not (dx == 0 and x % 2 == 0) and not (dx == 6 and x % 2 == 1)]
        for w in range(6):
            g = dx * 7 + w + 1
            weights = jnp.concatenate(
                [t2[g * 384 : (g + 1) * 384, :], t2[(g - 1) * 384 : g * 384, :]], axis=1
            )
            left = [lw[x + dx - 1, w] for x in xs_of] + [la[dx, w], lb[dx, w]]
            made = jnp.dot(
                jnp.concatenate(left, axis=0), weights, preferred_element_type=F32
            )
            for i, slot in enumerate(xs_of + [4, 5]):
                total[slot] = total[slot] + made[i * 16 : i * 16 + 16]

    row, col = iota((64, 64), 0), iota((64, 64), 1)
    order = jnp.where(((row & 1) << 5) + (row >> 1) == col, 1.0, 0.0).astype(BF16)

    def ordered(v):
        return jnp.dot(v.astype(BF16), order, preferred_element_type=F32).astype(BF16)

    v_of = []
    for px in range(2):
        r = 49 * 384 + px * 128
        v_of.append(jnp.concatenate([t2[r : r + 64, :], t2[r + 64 : r + 128, :]], axis=1))
    sb = total[5]
    sb = sb[0:4] + sb[4:8] + sb[8:12]
    sb = jnp.where(odd_y == 1, sb[:, 128:256], sb[:, 0:128])
    parity = lax.rem(iota((4, 64), 0) + gz, 2)
    sb = jnp.where(parity == 1, sb[:, 64:128], sb[:, 0:64])
    topv = top[0]
    top4 = jnp.concatenate(
        [topv[:, 0:64], topv[:, 64:128], topv[:, 128:192], jnp.zeros((1, 64), F32)], axis=0
    )
    local_b = ordered(jnp.concatenate([top4 + 0.25 * sb, jnp.zeros((12, 64), F32)], axis=0))
    for xa in range(2):
        down = jnp.dot(local_b, v_of[xa], preferred_element_type=F32)[0:4]
        local_a = 0.5 * total[4][xa * 8 : xa * 8 + 4] + down
        for ya in range(2):
            for p in range(2):
                b = ya * 128 + p * 64
                pa[pl.ds(xa * 16 + ya * 8 + p, 4, stride=2), 0:64] = local_a[:, b : b + 64]
    for xa in range(2):
        parent = ordered(pa[xa * 16 : xa * 16 + 16, 0:64])
        for px in range(2):
            x = 2 * xa + px
            leaf = total[x] + jnp.dot(parent, v_of[px], preferred_element_type=F32)
            lr[x * 32 : x * 32 + 16, :] = leaf[:, 0:128]
            lr[x * 32 + 16 : x * 32 + 32, :] = leaf[:, 128:256]
    for x in range(4):
        for y in range(4):
            for zp in range(6):
                r = x * 32 + (y % 2) * 16 + (y // 2) * 8 + zp
                ln[x * 4 + y : x * 4 + y + 1, zp * 128 : zp * 128 + 128] = lr[r : r + 1, :]

    lane8 = iota((8, 128), 1)
    for i in range(2):
        for zp in range(6):
            lanes = slice(zp * 128, zp * 128 + 128)
            coef = ln[i * 8 : i * 8 + 8, lanes]
            cheb = []
            for d in range(3):
                u = 2.0 * jnp.concatenate(
                    [pos[d, 2 * i, :, lanes], pos[d, 2 * i + 1, :, lanes]], axis=0
                ) - 1.0
                t2nd = 2.0 * u * u - 1.0
                cheb.append([None, u, t2nd, 2.0 * u * t2nd - u])
            out = None
            for a in range(4):
                sum_b = None
                for b in range(4):
                    sum_c = None
                    for c in range(4):
                        index = (lane8 & 64) + (16 * a + 4 * b + c)
                        term = jnp.take_along_axis(coef, index, axis=1, mode="promise_in_bounds")
                        if c:
                            term = term * cheb[2][c]
                        sum_c = term if sum_c is None else sum_c + term
                    if b:
                        sum_c = sum_c * cheb[1][b]
                    sum_b = sum_c if sum_b is None else sum_b + sum_c
                if a:
                    sum_b = sum_b * cheb[0][a]
                out = sum_b if out is None else out + sum_b
            value = out * 0.125 + near[i * 8 : i * 8 + 8, lanes]
            limit, slot = count_lanes(
                jnp.concatenate([cnt[2 * i], cnt[2 * i + 1]], axis=0), zp
            )
            value = jnp.where(slot < limit, value, 0.0)
            for h in range(2):
                pot_out[2 * i + h, :, lanes] = value[h * 4 : h * 4 + 4]
                loc_out[2 * i + h, :, lanes] = coef[h * 4 : h * 4 + 4]


def whole_kernel(
    pos_in, chg_in, soft_in, cnt_in, top_in, bm_in, am_in, lm_in, m2l_in, l2l_in,
    pot_out, loc_out,
    t2, near, pos, cnt, top, lw, la, lb, lr, pa, ln,
    pf, ml, ma, mb, zs, zr, ps, mls, mas, ms, zf, mt, s2,
    chg, soft, bm, am, lm, l2l, a_mat, q_mat, b_mat, ft, fs, wt, near8,
    send, recv, local,
):
    gx, gy, gz = (lax.axis_index(a) for a in AXES)

    def at(ox, oy, oz):
        return (
            lax.rem(gx + (ox + 8), 8),
            lax.rem(gy + (oy + 8), 8),
            lax.rem(gz + (oz + 8), 8),
        )

    fetched = [(lm_in, lm), (am_in, am), (bm_in, bm), (pos_in, pos), (cnt_in, cnt)]
    fetched += [(chg_in, chg), (soft_in, soft), (l2l_in, l2l), (top_in, top), (m2l_in, mt)]
    fetched = [
        pltpu.make_async_copy(src, dst, local.at[i]) for i, (src, dst) in enumerate(fetched)
    ]
    for copy in fetched:
        copy.start()
    barrier = pltpu.get_barrier_semaphore()
    around = [at(0, 0, 1), at(0, 0, -1)]
    for o in (1, -1, 2, -2, 3, -3):
        around += [at(o, 0, 0), at(0, o, 0)]
    for who in around:
        pl.semaphore_signal(barrier, inc=1, device_id=who, device_id_type=MESH)

    number = [0]

    def remote(src, dst, who):
        i = number[0]
        number[0] += 1
        copy = pltpu.make_async_remote_copy(
            src_ref=src, dst_ref=dst, send_sem=send.at[i], recv_sem=recv.at[i],
            device_id=who, device_id_type=MESH,
        )
        copy.start()
        return copy

    for copy in fetched[:3]:
        copy.wait()
    for x in range(4):
        block = lm[x].astype(F32)
        for zp in range(6):
            ms[zp * 16 + x * 4 : zp * 16 + x * 4 + 4, :] = block[:, zp * 128 : zp * 128 + 128]
    for x in range(2):
        block = am[x].astype(F32)
        for zp in range(3):
            ms[96 + zp * 4 + x * 2 : 98 + zp * 4 + x * 2, :] = block[:, zp * 128 : zp * 128 + 128]
    bcells = bm[0].astype(F32)
    ms[108:109, :] = bcells[:, 0:128]
    ms[109:110, :] = jnp.concatenate([bcells[:, 64:128], bcells[:, 128:192]], axis=1)
    ms[110:112, :] = jnp.zeros((2, 128), F32)
    row, col = iota((128, 128), 0), iota((128, 128), 1)
    moved = (row & 64) + ((row & 1) << 5) + ((row & 63) >> 1)
    order = jnp.where(moved == col, 1.0, 0.0).astype(BF16)
    ms[...] = jnp.dot(ms[...].astype(BF16), order, preferred_element_type=F32)

    for copy in fetched[3:7]:
        copy.wait()
    ps[...] = jnp.zeros_like(ps)
    mas[...] = jnp.zeros_like(mas)
    zf[...] = jnp.zeros_like(zf)
    for x in range(4):
        fields = [pos[0, x] - 0.5, pos[1, x] - 0.5, pos[2, x] - 0.5, chg[x], soft[x]]
        counts = cnt[x]
        for zp in range(6):
            limit, slot = count_lanes(counts, zp)
            for f in range(5):
                piece = fields[f][:, zp * 128 : zp * 128 + 128]
                if f == 3:
                    piece = jnp.where(slot < limit, piece, 0.0)
                ps[pl.ds(x * 192 + f * 8 + 1 + zp, 4, stride=48), :] = piece
                if zp == 0:
                    zf[f * 16 + x * 4 : f * 16 + x * 4 + 4, :] = piece
                if zp == 5:
                    zf[112 + f * 16 + x * 4 : 112 + f * 16 + x * 4 + 4, :] = piece
    for side, (lp, ap) in enumerate(((0, 0), (5, 2))):
        base = side * 112
        zf[base + 80 : base + 96, :] = ms[lp * 16 : lp * 16 + 16, :]
        zf[base + 96 : base + 100, :] = ms[96 + ap * 4 : 100 + ap * 4, :]
        zf[base + 100 : base + 102, :] = ms[108:110, :]
        zs[side] = zf[base : base + 112, :].astype(BF16)
    pl.semaphore_wait(barrier, 14)

    z_copies = [
        remote(zs.at[0], zr.at[1], at(0, 0, -1)),
        remote(zs.at[1], zr.at[0], at(0, 0, 1)),
    ]
    for zp in range(6):
        for x in range(4):
            mls[pl.ds(x * 32 + zp + 1, 4, stride=8), :] = ms[
                zp * 16 + x * 4 : zp * 16 + x * 4 + 4, :
            ]
    for zp in range(3):
        for x in range(2):
            mas[pl.ds(x * 16 + zp + 1, 2, stride=8), :] = ms[
                96 + zp * 4 + x * 2 : 98 + zp * 4 + x * 2, :
            ]

    near8[...] = jnp.zeros_like(near8)
    b_mat[...] = jnp.zeros_like(b_mat)
    wt[...] = jnp.zeros_like(wt)
    target_features(pos, soft, fs, ft)

    for copy in fetched[7:]:
        copy.wait()

    def unpack(i, carry):
        block = mt[pl.ds(pl.multiple_of(i * 16, 16), 16), :].astype(F32)
        unpack_rows(block, i * 16, s2, 16)
        return carry

    lax.fori_loop(0, 21, unpack, 0)
    unpack_rows(mt[336:343, :].astype(F32), 336, s2, 7)
    unpack_rows(l2l[...].astype(F32), 343, s2, 8)

    for copy in z_copies:
        copy.wait()
    keep_low = jnp.where(gz > 0, 1.0, 0.0).astype(F32)
    keep_high = jnp.where(gz < 7, 1.0, 0.0).astype(F32)
    b_rows = []
    for side, (keep, zp_l, zp_a) in enumerate(((keep_low, 0, 0), (keep_high, 7, 4))):
        got = zr[side].astype(F32) * keep
        for x in range(4):
            for f in range(5):
                ps[pl.ds(x * 192 + f * 8 + zp_l, 4, stride=48), :] = got[
                    f * 16 + x * 4 : f * 16 + x * 4 + 4, :
                ]
            mls[pl.ds(x * 32 + zp_l, 4, stride=8), :] = got[80 + x * 4 : 84 + x * 4, :]
        for x in range(2):
            mas[pl.ds(x * 16 + zp_a, 2, stride=8), :] = got[96 + x * 2 : 98 + x * 2, :]
        b_rows.append((got[100:101, :], got[101:102, :]))
    (left_a, left_b), (ra, rb) = b_rows
    oa, ob = ms[108:109, :], ms[109:110, :]
    low1 = iota((1, 128), 1) < 64
    middle = jnp.where(low1, pltpu.roll(left_b, 64, 1), pltpu.roll(oa, 64, 1))
    middle_r = jnp.where(low1, pltpu.roll(ob, 64, 1), pltpu.roll(ra, 64, 1))
    pairs = [left_a, left_b, middle, oa, ob, middle_r, ra, rb]
    even_z = lax.rem(gz, 2) == 0
    zf[0:16, :] = jnp.zeros((16, 128), F32)
    for l in range(3):
        at_even = l + 1 - l % 2
        at_odd = l + 1 - (l + 1) % 2
        for j in range(3):
            zf[4 * j + l : 4 * j + l + 1, :] = jnp.where(
                even_z, pairs[at_even + 2 * j], pairs[at_odd + 2 * j]
            )
    mb[3, 3] = zf[0:16, :].astype(BF16)
    x_b = []
    for o in (1, -1, 2, -2, 3, -3):
        x_b.append(remote(mb.at[3, 3], mb.at[3 - o, 3], at(o, 0, 0)))
    for x in range(4):
        for y in range(4):
            for t in range(3):
                r = (x * 4 + y) * 48 + t * 16
                pf[1 + x, 1 + y, t] = ps[r : r + 16, :].astype(BF16)
        for yp in range(2):
            r = x * 32 + yp * 16
            ml[2 + x, 1 + yp] = mls[r : r + 16, :].astype(BF16)
    for x in range(2):
        ma[2 + x, 1] = mas[x * 16 : x * 16 + 16, :].astype(BF16)

    own_x, own_xl, own_xa = pl.ds(1, 4), pl.ds(2, 4), pl.ds(2, 2)
    up, down = at(0, 1, 0), at(0, -1, 0)
    y_copies = [
        remote(pf.at[own_x, pl.ds(4, 1)], pf.at[own_x, pl.ds(0, 1)], up),
        remote(pf.at[own_x, pl.ds(1, 1)], pf.at[own_x, pl.ds(5, 1)], down),
        remote(ml.at[own_xl, pl.ds(2, 1)], ml.at[own_xl, pl.ds(0, 1)], up),
        remote(ml.at[own_xl, pl.ds(1, 1)], ml.at[own_xl, pl.ds(3, 1)], down),
        remote(ma.at[own_xa, pl.ds(1, 1)], ma.at[own_xa, pl.ds(0, 1)], up),
        remote(ma.at[own_xa, pl.ds(1, 1)], ma.at[own_xa, pl.ds(2, 1)], down),
    ]

    low_lanes = iota((32, 128), 1) < 64

    def pair_up(g, carry):
        near = (jnp.abs(g // 7 - 3) <= 1) & (jnp.abs(lax.rem(g, 7) - 3) <= 1)
        kept = jnp.where(near, 0.0, 1.0).astype(F32)
        tables = []
        for i in range(7):
            one = s2[pl.ds(pl.multiple_of((g * 7 + i) * 32, 32), 32), :]
            if 2 <= i <= 4:
                one = one * kept
            tables.append((one, pltpu.roll(one, 64, 1)))
        for w in range(6):
            (first, turned_first), (second, turned_second) = tables[w + 1], tables[w]
            to = g * 384 + w * 64
            t2[pl.ds(pl.multiple_of(to, 32), 32), :] = jnp.where(
                low_lanes, first, turned_second
            ).astype(BF16)
            t2[pl.ds(pl.multiple_of(to + 32, 32), 32), :] = jnp.where(
                low_lanes, turned_first, second
            ).astype(BF16)
        return carry

    def own_columns(i, carry):
        source_columns([(i, cy) for cy in range(1, 5)], gx, gy, pf, wt, a_mat, q_mat)
        return carry

    lax.fori_loop(1, 5, own_columns, 0)
    for copy in x_b:
        copy.wait()
    y_b = []
    for o in (1, -1, 2, -2, 3, -3):
        y_b.append(remote(mb.at[:, pl.ds(3, 1)], mb.at[:, pl.ds(3 - o, 1)], at(0, o, 0)))
    for copy in y_copies:
        copy.wait()

    up, down = at(1, 0, 0), at(-1, 0, 0)
    x_copies = [
        remote(pf.at[pl.ds(4, 1)], pf.at[pl.ds(0, 1)], up),
        remote(pf.at[pl.ds(1, 1)], pf.at[pl.ds(5, 1)], down),
        remote(ml.at[pl.ds(4, 2)], ml.at[pl.ds(0, 2)], up),
        remote(ml.at[pl.ds(2, 2)], ml.at[pl.ds(6, 2)], down),
        remote(ma.at[pl.ds(2, 2)], ma.at[pl.ds(0, 2)], up),
        remote(ma.at[pl.ds(2, 2)], ma.at[pl.ds(4, 2)], down),
    ]
    def own_pairs(t, carry):
        slab_pairs(t, a_mat, q_mat, b_mat, ft, near8)
        for u in range(5):
            pair_up(jnp.minimum((t - 1) * 5 + u, 48), 0)
        return carry

    lax.fori_loop(1, 11, own_pairs, 0)
    for child in range(4):
        r = (343 + 2 * child) * 32
        even, odd = pair_rows(s2[r : r + 32, :], s2[r + 32 : r + 64, :], low_lanes)
        to = 49 * 384 + child * 64
        t2[to : to + 32, :] = even
        t2[to + 32 : to + 64, :] = odd
    for copy in x_copies + y_b:
        copy.wait()

    def columns_y(i, carry):
        source_columns([(i, 0), (i, 5)], gx, gy, pf, wt, a_mat, q_mat)
        return carry

    def columns_x(i, carry):
        source_columns([(i * 5, cy) for cy in range(6)], gx, gy, pf, wt, a_mat, q_mat)
        return carry

    def slab_edges(i, carry):
        slab_pairs(i * 11, a_mat, q_mat, b_mat, ft, near8)
        return carry

    def row_edges(x, carry):
        edge_pairs(x, a_mat, q_mat, b_mat, ft, near8)
        return carry

    lax.fori_loop(1, 5, columns_y, 0)
    lax.fori_loop(0, 2, columns_x, 0)
    lax.fori_loop(0, 2, slab_edges, 0)
    lax.fori_loop(0, 4, row_edges, 0)
    gather_near(near8, near)
    far_kernel(
        gx, gy, gz, ml, ma, mb, t2, near, pos, cnt, top, pot_out, loc_out, lw, la, lb, lr, pa, ln
    )


NEAR_SCRATCH = [
    ((2304, 256), BF16),
    ((2304, 1664), BF16),
    ((4, 9, 256, 256), BF16),
    ((16, 3, 2, 16, 768), BF16),
    ((6, 64, 128), F32),
    ((6, 144, 128), F32),
    ((16, 2, 8, 768), F32),
]


FAR_SCRATCH = [
    ((8, 6, 16, 384), BF16),
    ((7, 6, 16, 384), BF16),
    ((7, 6, 16, 384), BF16),
    ((128, 128), F32),
    ((32, 128), F32),
    ((16, 768), F32),
]


def run(*args):
    halos = [(6, 6, 3, 16, 128), (8, 4, 16, 128), (6, 3, 16, 128), (7, 7, 16, 128)]
    scratch = [((T2_ROWS, 128), BF16), ((16, 768), F32), ((3, 4, 4, 768), F32)]
    scratch += [((4, 4, 12), jnp.int32), ((1, 1, 192), F32)] + FAR_SCRATCH
    scratch += [(s, BF16) for s in halos]
    scratch += [((2, 112, 128), BF16), ((2, 112, 128), BF16), ((768, 128), F32), ((128, 128), F32)]
    scratch += [((32, 128), F32), ((112, 128), F32), ((224, 128), F32), ((343, 4096), BF16)]
    scratch += [((352 * 32, 128), F32), ((4, 4, 768), F32), ((4, 4, 768), F32)]
    scratch += [((1, 1, 192), BF16), ((2, 2, 384), BF16), ((4, 4, 768), BF16), ((8, 4096), BF16)]
    return pl.pallas_call(
        whole_kernel,
        name="downward",
        out_shape=[jax.ShapeDtypeStruct((4, 4, 768), F32)] * 2,
        in_specs=[pl.BlockSpec(memory_space=pltpu.HBM)] * 10,
        out_specs=[pl.BlockSpec(memory_space=pltpu.VMEM)] * 2,
        scratch_shapes=[pltpu.VMEM(s, t) for s, t in scratch + NEAR_SCRATCH]
        + [
            pltpu.SemaphoreType.DMA((26,)),
            pltpu.SemaphoreType.DMA((26,)),
            pltpu.SemaphoreType.DMA((10,)),
        ],
        compiler_params=pltpu.CompilerParams(
            collective_id=0, has_side_effects=True, vmem_limit_bytes=VMEM_BYTES
        ),
        cost_estimate=pl.CostEstimate(
            flops=10**10, bytes_accessed=10**7, transcendentals=2 * 10**7
        ),
    )(*args)


def per_device(pos, chg, soft, cnt, top, bm, am, lm, m2l, l2l):
    return tuple(run(pos, chg, soft, cnt, top, bm, am, lm, m2l, l2l))


def solution(mesh):
    split = P("gx", "gy", "gz")
    in_specs = (P(None, "gx", "gy", "gz"),) + (split,) * 7 + (P(), P())
    return jax.shard_map(
        per_device, mesh=mesh, in_specs=in_specs, out_specs=(split, split), check_vma=False
    )
```

```python
import functools
import jax
import jax.numpy as jnp
from jax import lax
from jax.experimental import pallas as pl
from jax.experimental.pallas import tpu as pltpu
from jax.sharding import PartitionSpec as P

F32 = jnp.float32
BF16 = jnp.bfloat16
MESH = pl.DeviceIdType.MESH
AXES = ("gx", "gy", "gz")
T2_ROWS = 49 * 384 + 256
VMEM_BYTES = 63 * 2**20


def iota(shape, dim):
    return lax.broadcasted_iota(jnp.int32, shape, dim)


def count_lanes(counts, pair):
    rows = counts.shape[0]
    lane = iota((rows, 128), 1)
    low = counts[:, 2 * pair : 2 * pair + 1]
    high = counts[:, 2 * pair + 1 : 2 * pair + 2]
    return jnp.where(lane < 64, low, high), lane & 63


def unpack_rows(block, base, s2, rows):
    for c in range(32):
        s2[pl.ds(base * 32 + c, rows, stride=32), :] = block[:, c * 128 : (c + 1) * 128]


def pair_rows(first, second, low_lanes):
    turned_first = pltpu.roll(first, 64, 1)
    turned_second = pltpu.roll(second, 64, 1)
    even = jnp.where(low_lanes, first, turned_second)
    odd = jnp.where(low_lanes, turned_first, second)
    return even.astype(BF16), odd.astype(BF16)


def pieces(value, count):
    out = []
    for _ in range(count - 1):
        head = value.astype(BF16).astype(F32)
        out.append(head)
        value = value - head
    return out + [value]


def inside(coord, offset):
    return (coord + offset >= 0) & (coord + offset <= 7)


def source_columns(where, gx, gy, pf, wt, base=0):
    ones = jnp.ones((8, 128), F32)
    same = jnp.where(iota((128, 128), 0) == iota((128, 128), 1), 1.0, 0.0).astype(BF16)
    er, ec = iota((16, 1024), 0), iota((16, 1024), 1)
    spread = jnp.where(((er & 7) * 2 + (er >> 3)) == (ec >> 6), 1.0, 0.0).astype(BF16)
    charges = []
    for slot, (cx, cy, _, _, _) in enumerate(where):
        slot = slot + base
        xy = pf[cx, cy, 0].astype(F32)
        zq = pf[cx, cy, 1].astype(F32)
        s = pf[cx, cy, 2].astype(F32)[0:8]
        x, y, z, q = xy[0:8], xy[8:16], zq[0:8], zq[8:16]
        over_x = jnp.where(cx == 0, -1, jnp.where(cx == 5, 1, 0))
        over_y = jnp.where(cy == 0, -1, jnp.where(cy == 5, 1, 0))
        q = q * jnp.where(inside(gx, over_x) & inside(gy, over_y), 1.0, 0.0).astype(F32)
        ix = ones * (jnp.asarray(cx, F32) - 2.5)
        iy = ones * (jnp.asarray(cy, F32) - 2.5)
        n = (x + ix) * (x + ix) + (y + iy) * (y + iy) + z * z + 0.5 * (s * s)
        feats = [x, x, ix, ix, y, y, iy, iy, z, z, ones, ones, ones] + pieces(n, 3)
        for f in range(16):
            wt[slot, pl.ds(f, 8, stride=16), :] = feats[f]
        wt[slot, 128:136, :] = q
    for slot, (_, _, a_mat, q_mat, at) in enumerate(where):
        turned = lax.dot_general(
            same, wt[slot + base].astype(BF16), (((1,), (1,)), ((), ())), preferred_element_type=F32
        )
        rows = pl.ds(pl.multiple_of(at * 64, 64), 64)
        a_mat[rows, 0:128] = turned[0:64, 0:128].astype(BF16)
        a_mat[rows, 128:256] = turned[64:128, 0:128].astype(BF16)
        charges.append(
            jnp.concatenate([turned[0:64, 128:136], turned[64:128, 128:136]], axis=1)
        )
    wide = jnp.dot(
        jnp.concatenate(charges, axis=0).astype(BF16), spread, preferred_element_type=F32
    )
    low = iota((64, 128), 1) < 64
    for slot, (_, _, a_mat, q_mat, at) in enumerate(where):
        rows = pl.ds(pl.multiple_of(at * 64, 64), 64)
        v = [wide[slot * 64 : slot * 64 + 64, m * 128 : m * 128 + 128] for m in range(8)]
        for m in range(6):
            q_mat[rows, m * 128 : m * 128 + 128] = v[m + 1].astype(BF16)
        for m in range(7):
            q_mat[rows, 768 + m * 128 : 896 + m * 128] = jnp.where(low, v[m + 1], v[m]).astype(BF16)


def target_features(pos, soft, fs, ft):
    lane = iota((64, 128), 1)

    def put(f, v):
        for zp in range(6):
            fs[zp, pl.ds(f, 4, stride=16), :] = v[:, zp * 128 : zp * 128 + 128]

    for x in range(4):
        px, py, pz = (pos[d, x] - 0.5 for d in range(3))
        s = soft[x]
        fx = px + (x - 1.5)
        fy = py + (iota((4, 768), 0).astype(F32) - 1.5)
        ax, bx = pieces(fx, 2)
        ay, by = pieces(fy, 2)
        bx, by = bx.astype(BF16).astype(F32), by.astype(BF16).astype(F32)
        xx, yy = ax + bx, ay + by
        base = xx * xx + yy * yy + 0.5 * (s * s)
        for f, v in ((0, ax), (1, bx), (2, ax), (3, bx), (4, ay), (5, by), (6, ay), (7, by)):
            put(f, -2.0 * v)
        for f in (13, 14, 15):
            put(f, jnp.ones((4, 768), F32))
        for d in range(3):
            az, bz = pieces(pz - (d - 1.0), 2)
            bz = bz.astype(BF16).astype(F32)
            zz = az + bz
            n = base + zz * zz
            for f, v in zip((8, 9, 10, 11, 12), [-2.0 * az, -2.0 * bz] + pieces(n, 3)):
                put(f, v)
            for zp in range(6):
                made = fs[zp]
                if d != 1:
                    made = pltpu.roll(made, 64, 1)
                for e in range(2):
                    mine = lane < 64 if (e == 0) == (d == 1) else lane >= 64
                    half = jnp.where(mine, made, 0.0).astype(BF16)
                    for y in range(4):
                        ft[x * 4 + y, d, e, :, zp * 128 : zp * 128 + 128] = half[
                            y * 16 : y * 16 + 16
                        ]


Q_AT = (768, 0, 896)


def set_weights(b_mat, slot, ft, g):
    for k in range(3):
        for d in range(3):
            for h in range(2):
                for e in range(2):
                    cell = 4 * k + 2 + 2 * h + e + d - 1
                    r = (cell % 2) * 128 + (cell // 2) * 16
                    b_mat[slot, k * 3 + d, r : r + 16, h * 128 : h * 128 + 128] = ft[
                        g, d, e, :, (2 * k + h) * 128 : (2 * k + h) * 128 + 128
                    ]


def add_pairs(left, q_of, b_mat, slot, near8, g, own=None):
    rows = left.shape[0]
    for k in range(3):
        lanes = slice(256 * k, 256 * k + 256)
        for d in range(3):
            r2 = jnp.dot(left, b_mat[slot, k * 3 + d], preferred_element_type=F32)
            q = q_of(Q_AT[d] + 256 * k).astype(F32)
            if d == 1 and own is not None:
                q = q * own
            part = jnp.sum((lax.rsqrt(r2) * q).reshape(rows // 8, 8, 256), axis=0)
            if d == 0:
                swapped = part
            elif d == 1:
                plain = part
            else:
                swapped = swapped + part
        near8[g, 0, :, lanes] += plain
        near8[g, 1, :, lanes] += swapped


def slab_pairs(x, itself, a_mat, q_mat, at, b_mat, ft, near8):
    one = jnp.ones((64, 256), F32)
    for y in range(4):
        low, high = max(0, y - 1), min(3, y + 1)
        set_weights(b_mat, y, ft, x * 4 + y)
        rows = pl.ds(pl.multiple_of((at + low) * 64, 64), (high - low + 1) * 64)
        own = None
        if itself is not None:
            own = jnp.concatenate(
                [itself if cy == y else one for cy in range(low, high + 1)], axis=0
            )
        add_pairs(
            a_mat[rows, :], lambda at: q_mat[rows, at : at + 256], b_mat, y, near8, x * 4 + y, own
        )


def own_slab(t, a_own, q_own, b_mat, ft, near8):
    x, dx = t // 3, lax.rem(t, 3)
    itself = jnp.where(iota((64, 256), 0) == (iota((64, 256), 1) & 63), 0.0, 1.0).astype(F32)
    itself = jnp.where(dx == 1, itself, 1.0)
    slab_pairs(x, itself, a_own, q_own, (x + dx - 1) * 4, b_mat, ft, near8)


def edge_pairs(x, a_edge, q_edge, b_mat, ft, near8):
    for side, y in enumerate((0, 3)):
        set_weights(b_mat, 4 + side, ft, x * 4 + y)
        rows = pl.ds(pl.multiple_of((side * 6 + x) * 64, 64), 192)
        add_pairs(
            a_edge[rows, :], lambda at: q_edge[rows, at : at + 256], b_mat, 4 + side, near8, x * 4 + y
        )


def gather_near(near8, near):
    for g in range(16):
        for zp in range(6):
            lanes = slice(zp * 128, zp * 128 + 128)
            both = near8[g, 0, :, lanes] + pltpu.roll(near8[g, 1, :, lanes], 64, 1)
            near[g : g + 1, lanes] = jnp.sum(both, axis=0, keepdims=True)


def far_kernel(
    gx, gy, gz,
    ml, ma, mb, t2, near, pos, cnt, top,
    pot_out, loc_out,
    lw, la, lb, lr, pa, ln, to_lanes,
):
    def shifted(v):
        return [v, pltpu.roll(v, 7, 0), pltpu.roll(v, 6, 0)]

    for xs in range(8):
        over_x = -1 if xs < 2 else (1 if xs >= 6 else 0)
        turned = []
        for yp in range(4):
            over_y = -1 if yp < 1 else (1 if yp >= 3 else 0)
            keep = jnp.where(inside(gx, over_x) & inside(gy, over_y), 1.0, 0.0).astype(F32)
            tile = ml[xs, yp].astype(F32) * keep
            turned.append((shifted(tile[0:8]), shifted(tile[8:16])))
        for w in range(6):
            for j in range(3):
                lw[xs, w, :, j * 128 : j * 128 + 128] = jnp.concatenate(
                    [turned[w // 2][w % 2][j], turned[w // 2 + 1][w % 2][j]], axis=0
                ).astype(BF16)
    zero8 = jnp.zeros((8, 128), F32)
    a_tiles = {}
    for xs in range(6):
        over_x = -1 if xs < 2 else (1 if xs >= 4 else 0)
        for yp in range(3):
            over_y = yp - 1
            keep = jnp.where(inside(gx, over_x) & inside(gy, over_y), 1.0, 0.0).astype(F32)
            tile = ma[xs, yp].astype(F32) * keep
            a_tiles[xs, yp] = (shifted(tile[0:8]), shifted(tile[8:16]))
    for dx in range(7):
        for w in range(6):
            for j in range(3):
                first = a_tiles[dx - 1, w // 2][w % 2][j] if dx >= 1 else zero8
                second = a_tiles[dx, w // 2][w % 2][j] if dx <= 5 else zero8
                la[dx, w, :, j * 128 : j * 128 + 128] = jnp.concatenate(
                    [first, second], axis=0
                ).astype(BF16)
    row16 = iota((16, 128), 0)
    odd_x, odd_y = lax.rem(gx, 2), lax.rem(gy, 2)
    for dx in range(7):
        ok_x = inside(gx, dx - 3)
        if dx == 0:
            ok_x = ok_x & (odd_x == 1)
        if dx == 6:
            ok_x = ok_x & (odd_x == 0)
        for w in range(6):
            dy = w + 1 - odd_y
            keep = jnp.where(ok_x & inside(gy, dy - 3), 1.0, 0.0).astype(F32)
            tile = mb[dx, dy].astype(F32) * keep
            for j in range(3):
                lb[dx, w, :, j * 128 : j * 128 + 128] = jnp.where(
                    (row16 >> 2) == j, tile, 0.0
                ).astype(BF16)

    total = [jnp.zeros((16, 256), F32) for _ in range(6)]
    for dx in range(7):
        xs_of = [x for x in range(4) if not (dx == 0 and x % 2 == 0) and not (dx == 6 and x % 2 == 1)]
        for w in range(6):
            g = dx * 7 + w + 1
            weights = jnp.concatenate(
                [t2[g * 384 : (g + 1) * 384, :], t2[(g - 1) * 384 : g * 384, :]], axis=1
            )
            left = [lw[x + dx - 1, w] for x in xs_of] + [la[dx, w], lb[dx, w]]
            made = jnp.dot(
                jnp.concatenate(left, axis=0), weights, preferred_element_type=F32
            )
            for i, slot in enumerate(xs_of + [4, 5]):
                total[slot] = total[slot] + made[i * 16 : i * 16 + 16]

    row, col = iota((64, 64), 0), iota((64, 64), 1)
    order = jnp.where(((row & 1) << 5) + (row >> 1) == col, 1.0, 0.0).astype(BF16)

    def ordered(v):
        return jnp.dot(v.astype(BF16), order, preferred_element_type=F32).astype(BF16)

    v_of = []
    for px in range(2):
        r = 49 * 384 + px * 128
        v_of.append(jnp.concatenate([t2[r : r + 64, :], t2[r + 64 : r + 128, :]], axis=1))
    sb = total[5]
    sb = sb[0:4] + sb[4:8] + sb[8:12]
    sb = jnp.where(odd_y == 1, sb[:, 128:256], sb[:, 0:128])
    parity = lax.rem(iota((4, 64), 0) + gz, 2)
    sb = jnp.where(parity == 1, sb[:, 64:128], sb[:, 0:64])
    topv = top[0]
    top4 = jnp.concatenate(
        [topv[:, 0:64], topv[:, 64:128], topv[:, 128:192], jnp.zeros((1, 64), F32)], axis=0
    )
    local_b = ordered(jnp.concatenate([top4 + 0.25 * sb, jnp.zeros((12, 64), F32)], axis=0))
    for xa in range(2):
        down = jnp.dot(local_b, v_of[xa], preferred_element_type=F32)[0:4]
        local_a = 0.5 * total[4][xa * 8 : xa * 8 + 4] + down
        for ya in range(2):
            for p in range(2):
                b = ya * 128 + p * 64
                pa[pl.ds(xa * 16 + ya * 8 + p, 4, stride=2), 0:64] = local_a[:, b : b + 64]
    for xa in range(2):
        parent = ordered(pa[xa * 16 : xa * 16 + 16, 0:64])
        for px in range(2):
            x = 2 * xa + px
            leaf = total[x] + jnp.dot(parent, v_of[px], preferred_element_type=F32)
            lr[x * 32 : x * 32 + 16, :] = leaf[:, 0:128]
            lr[x * 32 + 16 : x * 32 + 32, :] = leaf[:, 128:256]
    for x in range(4):
        for y in range(4):
            for zp in range(6):
                r = x * 32 + (y % 2) * 16 + (y // 2) * 8 + zp
                ln[x * 4 + y : x * 4 + y + 1, zp * 128 : zp * 128 + 128] = lr[r : r + 1, :]

    coef = jnp.concatenate([ln[:, zp * 128 : zp * 128 + 128] for zp in range(6)], axis=0)
    high, low = pieces(coef, 2)
    coef = jnp.concatenate([high.astype(BF16), low.astype(BF16)], axis=1)
    cheb = []
    for d in range(3):
        u = 2.0 * jnp.concatenate(
            [pos[d, x, :, zp * 128 : zp * 128 + 128] for zp in range(6) for x in range(4)], axis=0
        ) - 1.0
        second = 2.0 * u * u - 1.0
        cheb.append([None, u, second, 2.0 * u * second - u])
    out = None
    for a in range(4):
        spread = jnp.dot(
            coef, to_lanes[:, a * 2048 : a * 2048 + 2048], preferred_element_type=F32
        )
        sum_b = None
        for b in range(4):
            sum_c = None
            for c in range(4):
                term = spread[:, (4 * b + c) * 128 : (4 * b + c) * 128 + 128]
                if c:
                    term = term * cheb[2][c]
                sum_c = term if sum_c is None else sum_c + term
            if b:
                sum_c = sum_c * cheb[1][b]
            sum_b = sum_c if sum_b is None else sum_b + sum_c
        if a:
            sum_b = sum_b * cheb[0][a]
        out = sum_b if out is None else out + sum_b
    for zp in range(6):
        lanes = slice(zp * 128, zp * 128 + 128)
        value = out[zp * 16 : zp * 16 + 16] * 0.125 + near[:, lanes]
        for x in range(4):
            limit, slot = count_lanes(cnt[x], zp)
            pot_out[x, :, lanes] = jnp.where(slot < limit, value[x * 4 : x * 4 + 4], 0.0)
            loc_out[x, :, lanes] = ln[x * 4 : x * 4 + 4, lanes]


def lane_spread(to_lanes):
    row, col = iota((128, 128), 0), iota((128, 128), 1)

    def one(c, carry):
        block = jnp.where(row == (col & 64) + c, 1.0, 0.0).astype(BF16)
        lanes = pl.ds(pl.multiple_of(c * 128, 128), 128)
        to_lanes[0:128, lanes] = block
        to_lanes[128:256, lanes] = block
        return carry

    lax.fori_loop(0, 64, one, 0)


def whole_kernel(
    pos_in, chg_in, soft_in, cnt_in, top_in, bm_in, am_in, lm_in, m2l_in, l2l_in,
    pot_out, loc_out,
    t2, near, pos, cnt, top, lw, la, lb, lr, pa, ln, to_lanes,
    pf, ml, ma, mb, zs, zr, ps, mls, mas, ms, zf, mt, s2,
    chg, soft, bm, am, lm, l2l,
    a_own, q_own, a_side, q_side, a_edge, q_edge, b_mat, ft, fs, wt, near8,
    send, recv, local,
):
    gx, gy, gz = (lax.axis_index(a) for a in AXES)

    def at(ox, oy, oz):
        return (
            lax.rem(gx + (ox + 8), 8),
            lax.rem(gy + (oy + 8), 8),
            lax.rem(gz + (oz + 8), 8),
        )

    fetched = [(lm_in, lm), (am_in, am), (bm_in, bm), (pos_in, pos), (cnt_in, cnt)]
    fetched += [(chg_in, chg), (soft_in, soft), (l2l_in, l2l), (top_in, top), (m2l_in, mt)]
    fetched = [
        pltpu.make_async_copy(src, dst, local.at[i]) for i, (src, dst) in enumerate(fetched)
    ]
    for copy in fetched:
        copy.start()
    barrier = pltpu.get_barrier_semaphore()
    around = [at(0, 0, 1), at(0, 0, -1)]
    for o in (1, -1, 2, -2, 3, -3):
        around += [at(o, 0, 0), at(0, o, 0)]
    for who in around:
        pl.semaphore_signal(barrier, inc=1, device_id=who, device_id_type=MESH)

    number = [0]

    def remote(src, dst, who):
        i = number[0]
        number[0] += 1
        copy = pltpu.make_async_remote_copy(
            src_ref=src, dst_ref=dst, send_sem=send.at[i], recv_sem=recv.at[i],
            device_id=who, device_id_type=MESH,
        )
        copy.start()
        return copy

    for copy in fetched[:3]:
        copy.wait()
    for x in range(4):
        block = lm[x].astype(F32)
        for zp in range(6):
            ms[zp * 16 + x * 4 : zp * 16 + x * 4 + 4, :] = block[:, zp * 128 : zp * 128 + 128]
    for x in range(2):
        block = am[x].astype(F32)
        for zp in range(3):
            ms[96 + zp * 4 + x * 2 : 98 + zp * 4 + x * 2, :] = block[:, zp * 128 : zp * 128 + 128]
    bcells = bm[0].astype(F32)
    ms[108:109, :] = bcells[:, 0:128]
    ms[109:110, :] = jnp.concatenate([bcells[:, 64:128], bcells[:, 128:192]], axis=1)
    ms[110:112, :] = jnp.zeros((2, 128), F32)
    row, col = iota((128, 128), 0), iota((128, 128), 1)
    moved = (row & 64) + ((row & 1) << 5) + ((row & 63) >> 1)
    order = jnp.where(moved == col, 1.0, 0.0).astype(BF16)
    ms[...] = jnp.dot(ms[...].astype(BF16), order, preferred_element_type=F32)

    for copy in fetched[3:7]:
        copy.wait()
    own = []
    for x in range(4):
        own.append([pos[0, x] - 0.5, pos[1, x] - 0.5, pos[2, x] - 0.5, chg[x], soft[x]])

    def own_piece(x, f, zp):
        piece = own[x][f][:, zp * 128 : zp * 128 + 128]
        if f == 3:
            limit, slot = count_lanes(cnt[x], zp)
            piece = jnp.where(slot < limit, piece, 0.0)
        return piece

    zf[...] = jnp.zeros_like(zf)
    for side, (lp, ap) in enumerate(((0, 0), (5, 2))):
        base = side * 112
        for x in range(4):
            for f in range(5):
                zf[base + f * 16 + x * 4 : base + f * 16 + x * 4 + 4, :] = own_piece(x, f, lp)
        zf[base + 80 : base + 96, :] = ms[lp * 16 : lp * 16 + 16, :]
        zf[base + 96 : base + 100, :] = ms[96 + ap * 4 : 100 + ap * 4, :]
        zf[base + 100 : base + 102, :] = ms[108:110, :]
        zs[side] = zf[base : base + 112, :].astype(BF16)
    pl.semaphore_wait(barrier, 14)

    z_copies = [
        remote(zs.at[0], zr.at[1], at(0, 0, -1)),
        remote(zs.at[1], zr.at[0], at(0, 0, 1)),
    ]
    ps[...] = jnp.zeros_like(ps)
    mas[...] = jnp.zeros_like(mas)
    for x in range(4):
        for zp in range(6):
            for f in range(5):
                ps[pl.ds(x * 192 + f * 8 + 1 + zp, 4, stride=48), :] = own_piece(x, f, zp)
    for zp in range(6):
        for x in range(4):
            mls[pl.ds(x * 32 + zp + 1, 4, stride=8), :] = ms[
                zp * 16 + x * 4 : zp * 16 + x * 4 + 4, :
            ]
    for zp in range(3):
        for x in range(2):
            mas[pl.ds(x * 16 + zp + 1, 2, stride=8), :] = ms[
                96 + zp * 4 + x * 2 : 98 + zp * 4 + x * 2, :
            ]

    near8[...] = jnp.zeros_like(near8)
    b_mat[...] = jnp.zeros_like(b_mat)
    wt[...] = jnp.zeros_like(wt)
    target_features(pos, soft, fs, ft)
    lane_spread(to_lanes)

    for copy in fetched[7:]:
        copy.wait()

    def unpack(i, carry):
        block = mt[pl.ds(pl.multiple_of(i * 16, 16), 16), :].astype(F32)
        unpack_rows(block, i * 16, s2, 16)
        return carry

    lax.fori_loop(0, 21, unpack, 0)
    unpack_rows(mt[336:343, :].astype(F32), 336, s2, 7)
    unpack_rows(l2l[...].astype(F32), 343, s2, 8)

    for copy in z_copies:
        copy.wait()
    keep_low = jnp.where(gz > 0, 1.0, 0.0).astype(F32)
    keep_high = jnp.where(gz < 7, 1.0, 0.0).astype(F32)
    b_rows = []
    for side, (keep, zp_l, zp_a) in enumerate(((keep_low, 0, 0), (keep_high, 7, 4))):
        got = zr[side].astype(F32) * keep
        for x in range(4):
            for f in range(5):
                ps[pl.ds(x * 192 + f * 8 + zp_l, 4, stride=48), :] = got[
                    f * 16 + x * 4 : f * 16 + x * 4 + 4, :
                ]
            mls[pl.ds(x * 32 + zp_l, 4, stride=8), :] = got[80 + x * 4 : 84 + x * 4, :]
        for x in range(2):
            mas[pl.ds(x * 16 + zp_a, 2, stride=8), :] = got[96 + x * 2 : 98 + x * 2, :]
        b_rows.append((got[100:101, :], got[101:102, :]))
    (left_a, left_b), (ra, rb) = b_rows
    oa, ob = ms[108:109, :], ms[109:110, :]
    low1 = iota((1, 128), 1) < 64
    middle = jnp.where(low1, pltpu.roll(left_b, 64, 1), pltpu.roll(oa, 64, 1))
    middle_r = jnp.where(low1, pltpu.roll(ob, 64, 1), pltpu.roll(ra, 64, 1))
    pairs = [left_a, left_b, middle, oa, ob, middle_r, ra, rb]
    even_z = lax.rem(gz, 2) == 0
    zf[0:16, :] = jnp.zeros((16, 128), F32)
    for l in range(3):
        at_even = l + 1 - l % 2
        at_odd = l + 1 - (l + 1) % 2
        for j in range(3):
            zf[4 * j + l : 4 * j + l + 1, :] = jnp.where(
                even_z, pairs[at_even + 2 * j], pairs[at_odd + 2 * j]
            )
    mb[3, 3] = zf[0:16, :].astype(BF16)
    x_b = []
    for o in (1, -1, 2, -2, 3, -3):
        x_b.append(remote(mb.at[3, 3], mb.at[3 - o, 3], at(o, 0, 0)))
    for x in range(4):
        for y in range(4):
            for t in range(3):
                r = (x * 4 + y) * 48 + t * 16
                pf[1 + x, 1 + y, t] = ps[r : r + 16, :].astype(BF16)
        for yp in range(2):
            r = x * 32 + yp * 16
            ml[2 + x, 1 + yp] = mls[r : r + 16, :].astype(BF16)
    for x in range(2):
        ma[2 + x, 1] = mas[x * 16 : x * 16 + 16, :].astype(BF16)

    own_x, own_xl, own_xa = pl.ds(1, 4), pl.ds(2, 4), pl.ds(2, 2)
    up, down = at(0, 1, 0), at(0, -1, 0)
    y_copies = [
        remote(pf.at[own_x, pl.ds(4, 1)], pf.at[own_x, pl.ds(0, 1)], up),
        remote(pf.at[own_x, pl.ds(1, 1)], pf.at[own_x, pl.ds(5, 1)], down),
        remote(ml.at[own_xl, pl.ds(2, 1)], ml.at[own_xl, pl.ds(0, 1)], up),
        remote(ml.at[own_xl, pl.ds(1, 1)], ml.at[own_xl, pl.ds(3, 1)], down),
        remote(ma.at[own_xa, pl.ds(1, 1)], ma.at[own_xa, pl.ds(0, 1)], up),
        remote(ma.at[own_xa, pl.ds(1, 1)], ma.at[own_xa, pl.ds(2, 1)], down),
    ]

    low_lanes = iota((32, 128), 1) < 64

    def pair_up(g, carry):
        near = (jnp.abs(g // 7 - 3) <= 1) & (jnp.abs(lax.rem(g, 7) - 3) <= 1)
        kept = jnp.where(near, 0.0, 1.0).astype(F32)
        tables = []
        for i in range(7):
            one = s2[pl.ds(pl.multiple_of((g * 7 + i) * 32, 32), 32), :]
            if 2 <= i <= 4:
                one = one * kept
            tables.append((one, pltpu.roll(one, 64, 1)))
        for w in range(6):
            (first, turned_first), (second, turned_second) = tables[w + 1], tables[w]
            to = g * 384 + w * 64
            t2[pl.ds(pl.multiple_of(to, 32), 32), :] = jnp.where(
                low_lanes, first, turned_second
            ).astype(BF16)
            t2[pl.ds(pl.multiple_of(to + 32, 32), 32), :] = jnp.where(
                low_lanes, turned_first, second
            ).astype(BF16)
        return carry

    def own_columns(i, carry):
        where = [(i, cy, a_own, q_own, (i - 1) * 4 + cy - 1) for cy in range(1, 5)]
        source_columns(where, gx, gy, pf, wt)
        return carry

    def pair_some(i):
        for u in range(6):
            pair_up(jnp.minimum(i * 6 + u, 48), 0)

    def own_pairs(t, carry):
        own_slab(t, a_own, q_own, b_mat, ft, near8)
        pair_some(t - 1)
        return carry

    lax.fori_loop(1, 5, own_columns, 0)
    lax.fori_loop(1, 5, own_pairs, 0)
    for copy in x_b:
        copy.wait()
    y_b = []
    for o in (1, -1, 2, -2, 3, -3):
        y_b.append(remote(mb.at[:, pl.ds(3, 1)], mb.at[:, pl.ds(3 - o, 1)], at(0, o, 0)))
    for copy in y_copies:
        copy.wait()

    up, down = at(1, 0, 0), at(-1, 0, 0)
    x_copies = [
        remote(pf.at[pl.ds(4, 1)], pf.at[pl.ds(0, 1)], up),
        remote(pf.at[pl.ds(1, 1)], pf.at[pl.ds(5, 1)], down),
        remote(ml.at[pl.ds(4, 2)], ml.at[pl.ds(0, 2)], up),
        remote(ml.at[pl.ds(2, 2)], ml.at[pl.ds(6, 2)], down),
        remote(ma.at[pl.ds(2, 2)], ma.at[pl.ds(0, 2)], up),
        remote(ma.at[pl.ds(2, 2)], ma.at[pl.ds(4, 2)], down),
    ]
    def own_pairs_y(t, carry):
        cx = t - 4
        where = [(cx, 0, a_edge, q_edge, cx), (cx, 5, a_edge, q_edge, cx + 6)]
        source_columns(where, gx, gy, pf, wt)
        own_slab(t, a_own, q_own, b_mat, ft, near8)
        pair_some(t - 1)
        return carry

    lax.fori_loop(5, 9, own_pairs_y, 0)
    pair_up(48, 0)
    for child in range(4):
        r = (343 + 2 * child) * 32
        even, odd = pair_rows(s2[r : r + 32, :], s2[r + 32 : r + 64, :], low_lanes)
        to = 49 * 384 + child * 64
        t2[to : to + 32, :] = even
        t2[to + 32 : to + 64, :] = odd
    for copy in x_copies + y_b:
        copy.wait()

    def own_pairs_x(i, carry):
        cx = i * 5
        where = [(cx, 0, a_edge, q_edge, cx), (cx, 5, a_edge, q_edge, cx + 6)]
        where += [(cx, cy, a_side, q_side, i * 4 + cy - 1) for cy in range(1, 5)]
        source_columns(where, gx, gy, pf, wt)
        own_slab(i + 9, a_own, q_own, b_mat, ft, near8)
        edge_pairs(i + 1, a_edge, q_edge, b_mat, ft, near8)
        return carry

    def last_pairs(i, carry):
        slab_pairs(i * 3, None, a_side, q_side, i * 4, b_mat, ft, near8)
        edge_pairs(i * 3, a_edge, q_edge, b_mat, ft, near8)
        return carry

    lax.fori_loop(0, 2, own_pairs_x, 0)
    lax.fori_loop(0, 2, last_pairs, 0)
    gather_near(near8, near)
    far_kernel(
        gx, gy, gz, ml, ma, mb, t2, near, pos, cnt, top, pot_out, loc_out,
        lw, la, lb, lr, pa, ln, to_lanes,
    )


NEAR_SCRATCH = [
    ((1024, 256), BF16),
    ((1024, 1664), BF16),
    ((512, 256), BF16),
    ((512, 1664), BF16),
    ((768, 256), BF16),
    ((768, 1664), BF16),
    ((6, 9, 256, 256), BF16),
    ((16, 3, 2, 16, 768), BF16),
    ((6, 64, 128), F32),
    ((6, 144, 128), F32),
    ((16, 2, 8, 768), F32),
]


FAR_SCRATCH = [
    ((8, 6, 16, 384), BF16),
    ((7, 6, 16, 384), BF16),
    ((7, 6, 16, 384), BF16),
    ((128, 128), F32),
    ((32, 128), F32),
    ((16, 768), F32),
    ((256, 8192), BF16),
]


def run(*args):
    halos = [(6, 6, 3, 16, 128), (8, 4, 16, 128), (6, 3, 16, 128), (7, 7, 16, 128)]
    scratch = [((T2_ROWS, 128), BF16), ((16, 768), F32), ((3, 4, 4, 768), F32)]
    scratch += [((4, 4, 12), jnp.int32), ((1, 1, 192), F32)] + FAR_SCRATCH
    scratch += [(s, BF16) for s in halos]
    scratch += [((2, 112, 128), BF16), ((2, 112, 128), BF16), ((768, 128), F32), ((128, 128), F32)]
    scratch += [((32, 128), F32), ((112, 128), F32), ((224, 128), F32), ((343, 4096), BF16)]
    scratch += [((352 * 32, 128), F32), ((4, 4, 768), F32), ((4, 4, 768), F32)]
    scratch += [((1, 1, 192), BF16), ((2, 2, 384), BF16), ((4, 4, 768), BF16), ((8, 4096), BF16)]
    return pl.pallas_call(
        whole_kernel,
        name="downward",
        out_shape=[jax.ShapeDtypeStruct((4, 4, 768), F32)] * 2,
        in_specs=[pl.BlockSpec(memory_space=pltpu.HBM)] * 10,
        out_specs=[pl.BlockSpec(memory_space=pltpu.VMEM)] * 2,
        scratch_shapes=[pltpu.VMEM(s, t) for s, t in scratch + NEAR_SCRATCH]
        + [
            pltpu.SemaphoreType.DMA((26,)),
            pltpu.SemaphoreType.DMA((26,)),
            pltpu.SemaphoreType.DMA((10,)),
        ],
        compiler_params=pltpu.CompilerParams(
            collective_id=0, has_side_effects=True, vmem_limit_bytes=VMEM_BYTES
        ),
        cost_estimate=pl.CostEstimate(
            flops=10**10, bytes_accessed=10**7, transcendentals=2 * 10**7
        ),
    )(*args)


def per_device(pos, chg, soft, cnt, top, bm, am, lm, m2l, l2l):
    return tuple(run(pos, chg, soft, cnt, top, bm, am, lm, m2l, l2l))


def solution(mesh):
    split = P("gx", "gy", "gz")
    in_specs = (P(None, "gx", "gy", "gz"),) + (split,) * 7 + (P(), P())
    return jax.shard_map(
        per_device, mesh=mesh, in_specs=in_specs, out_specs=(split, split), check_vma=False
    )
```

```python
import functools
import jax
import jax.numpy as jnp
from jax import lax
from jax.experimental import pallas as pl
from jax.experimental.pallas import tpu as pltpu
from jax.sharding import PartitionSpec as P

F32 = jnp.float32
BF16 = jnp.bfloat16
MESH = pl.DeviceIdType.MESH
AXES = ("gx", "gy", "gz")
T2_ROWS = 49 * 384 + 256
VMEM_BYTES = 63 * 2**20


def iota(shape, dim):
    return lax.broadcasted_iota(jnp.int32, shape, dim)


def count_lanes(counts, pair):
    rows = counts.shape[0]
    lane = iota((rows, 128), 1)
    low = counts[:, 2 * pair : 2 * pair + 1]
    high = counts[:, 2 * pair + 1 : 2 * pair + 2]
    return jnp.where(lane < 64, low, high), lane & 63


def unpack_rows(block, base, s2, rows):
    for c in range(32):
        s2[pl.ds(base * 40 + c, rows, stride=40), :] = block[:, c * 128 : (c + 1) * 128]


def pair_rows(first, second, low_lanes):
    turned_first = pltpu.roll(first, 64, 1)
    turned_second = pltpu.roll(second, 64, 1)
    even = jnp.where(low_lanes, first, turned_second)
    odd = jnp.where(low_lanes, turned_first, second)
    return even.astype(BF16), odd.astype(BF16)


def pieces(value, count):
    out = []
    for _ in range(count - 1):
        head = value.astype(BF16).astype(F32)
        out.append(head)
        value = value - head
    return out + [value]


def inside(coord, offset):
    return (coord + offset >= 0) & (coord + offset <= 7)


def source_columns(where, gx, gy, pf, wt, base=0):
    ones = jnp.ones((8, 128), F32)
    same = jnp.where(iota((128, 128), 0) == iota((128, 128), 1), 1.0, 0.0).astype(BF16)
    er, ec = iota((16, 1024), 0), iota((16, 1024), 1)
    spread = jnp.where(((er & 7) * 2 + (er >> 3)) == (ec >> 6), 1.0, 0.0).astype(BF16)
    charges = []
    for slot, (cx, cy, _, _, _) in enumerate(where):
        slot = slot + base
        xy = pf[cx, cy, 0].astype(F32)
        zq = pf[cx, cy, 1].astype(F32)
        s = pf[cx, cy, 2].astype(F32)[0:8]
        x, y, z, q = xy[0:8], xy[8:16], zq[0:8], zq[8:16]
        over_x = jnp.where(cx == 0, -1, jnp.where(cx == 5, 1, 0))
        over_y = jnp.where(cy == 0, -1, jnp.where(cy == 5, 1, 0))
        q = q * jnp.where(inside(gx, over_x) & inside(gy, over_y), 1.0, 0.0).astype(F32)
        ix = ones * (jnp.asarray(cx, F32) - 2.5)
        iy = ones * (jnp.asarray(cy, F32) - 2.5)
        n = (x + ix) * (x + ix) + (y + iy) * (y + iy) + z * z + 0.5 * (s * s)
        feats = [x, x, ix, ix, y, y, iy, iy, z, z, ones, ones, ones] + pieces(n, 3)
        for f in range(16):
            wt[slot, pl.ds(f, 8, stride=24), :] = feats[f]
        wt[slot, 192:200, :] = q
    for slot, (_, _, a_mat, q_mat, at) in enumerate(where):
        tile = [wt[slot + base, zp * 24 : zp * 24 + 16, :] for zp in range(8)]
        tile = jnp.concatenate(tile + [wt[slot + base, 192:208, :]], axis=0)
        turned = lax.dot_general(
            same, tile.astype(BF16), (((1,), (1,)), ((), ())), preferred_element_type=F32
        )
        rows = pl.ds(pl.multiple_of(at * 64, 64), 64)
        a_mat[rows, 0:128] = turned[0:64, 0:128].astype(BF16)
        a_mat[rows, 128:256] = turned[64:128, 0:128].astype(BF16)
        charges.append(
            jnp.concatenate([turned[0:64, 128:136], turned[64:128, 128:136]], axis=1)
        )
    wide = jnp.dot(
        jnp.concatenate(charges, axis=0).astype(BF16), spread, preferred_element_type=F32
    )
    low = iota((64, 128), 1) < 64
    for slot, (_, _, a_mat, q_mat, at) in enumerate(where):
        rows = pl.ds(pl.multiple_of(at * 64, 64), 64)
        v = [wide[slot * 64 : slot * 64 + 64, m * 128 : m * 128 + 128] for m in range(8)]
        for m in range(6):
            q_mat[rows, m * 128 : m * 128 + 128] = v[m + 1].astype(BF16)
        for m in range(7):
            q_mat[rows, 768 + m * 128 : 896 + m * 128] = jnp.where(low, v[m + 1], v[m]).astype(BF16)


def target_features(pos, soft, fs, ft):
    lane = iota((64, 128), 1)

    def put(f, v):
        for zp in range(6):
            fs[zp, pl.ds(f, 4, stride=24), :] = v[:, zp * 128 : zp * 128 + 128]

    for x in range(4):
        px, py, pz = (pos[d, x] - 0.5 for d in range(3))
        s = soft[x]
        fx = px + (x - 1.5)
        fy = py + (iota((4, 768), 0).astype(F32) - 1.5)
        ax, bx = pieces(fx, 2)
        ay, by = pieces(fy, 2)
        bx, by = bx.astype(BF16).astype(F32), by.astype(BF16).astype(F32)
        xx, yy = ax + bx, ay + by
        base = xx * xx + yy * yy + 0.5 * (s * s)
        for f, v in ((0, ax), (1, bx), (2, ax), (3, bx), (4, ay), (5, by), (6, ay), (7, by)):
            put(f, -2.0 * v)
        for f in (13, 14, 15):
            put(f, jnp.ones((4, 768), F32))
        for d in range(3):
            az, bz = pieces(pz - (d - 1.0), 2)
            bz = bz.astype(BF16).astype(F32)
            zz = az + bz
            n = base + zz * zz
            for f, v in zip((8, 9, 10, 11, 12), [-2.0 * az, -2.0 * bz] + pieces(n, 3)):
                put(f, v)
            for zp in range(6):
                made = jnp.concatenate(
                    [fs[zp, y * 24 : y * 24 + 16, :] for y in range(4)], axis=0
                )
                if d != 1:
                    made = pltpu.roll(made, 64, 1)
                for e in range(2):
                    mine = lane < 64 if (e == 0) == (d == 1) else lane >= 64
                    half = jnp.where(mine, made, 0.0).astype(BF16)
                    for y in range(4):
                        ft[x * 4 + y, d, e, :, zp * 128 : zp * 128 + 128] = half[
                            y * 16 : y * 16 + 16
                        ]


Q_AT = (768, 0, 896)


def set_weights(b_mat, slot, ft, g):
    for k in range(3):
        for d in range(3):
            for h in range(2):
                for e in range(2):
                    cell = 4 * k + 2 + 2 * h + e + d - 1
                    r = (cell % 2) * 128 + (cell // 2) * 16
                    b_mat[slot, k * 3 + d, r : r + 16, h * 128 : h * 128 + 128] = ft[
                        g, d, e, :, (2 * k + h) * 128 : (2 * k + h) * 128 + 128
                    ]


def add_pairs(left, q_of, b_mat, slot, near8, g, own=None):
    rows = left.shape[0]
    for k in range(3):
        lanes = slice(256 * k, 256 * k + 256)
        for d in range(3):
            r2 = jnp.dot(left, b_mat[slot, k * 3 + d], preferred_element_type=F32)
            q = q_of(Q_AT[d] + 256 * k).astype(F32)
            if d == 1 and own is not None:
                q = q * own
            part = jnp.sum((lax.rsqrt(r2) * q).reshape(rows // 8, 8, 256), axis=0)
            if d == 0:
                swapped = part
            elif d == 1:
                plain = part
            else:
                swapped = swapped + part
        near8[g, 0, :, lanes] += plain
        near8[g, 1, :, lanes] += swapped


def slab_pairs(x, itself, a_mat, q_mat, at, b_mat, ft, near8):
    one = jnp.ones((64, 256), F32)
    for y in range(4):
        low, high = max(0, y - 1), min(3, y + 1)
        set_weights(b_mat, y, ft, x * 4 + y)
        rows = pl.ds(pl.multiple_of((at + low) * 64, 64), (high - low + 1) * 64)
        own = None
        if itself is not None:
            own = jnp.concatenate(
                [itself if cy == y else one for cy in range(low, high + 1)], axis=0
            )
        add_pairs(
            a_mat[rows, :], lambda at: q_mat[rows, at : at + 256], b_mat, y, near8, x * 4 + y, own
        )


def own_slab(t, a_own, q_own, b_mat, ft, near8):
    x, dx = t // 3, lax.rem(t, 3)
    itself = jnp.where(iota((64, 256), 0) == (iota((64, 256), 1) & 63), 0.0, 1.0).astype(F32)
    itself = jnp.where(dx == 1, itself, 1.0)
    slab_pairs(x, itself, a_own, q_own, (x + dx - 1) * 4, b_mat, ft, near8)


def edge_pairs(x, a_edge, q_edge, b_mat, ft, near8):
    for side, y in enumerate((0, 3)):
        set_weights(b_mat, 4 + side, ft, x * 4 + y)
        rows = pl.ds(pl.multiple_of((side * 6 + x) * 64, 64), 192)
        add_pairs(
            a_edge[rows, :], lambda at: q_edge[rows, at : at + 256], b_mat, 4 + side, near8, x * 4 + y
        )


def gather_near(near8, near):
    for g in range(16):
        for zp in range(6):
            lanes = slice(zp * 128, zp * 128 + 128)
            both = near8[g, 0, :, lanes] + pltpu.roll(near8[g, 1, :, lanes], 64, 1)
            near[g : g + 1, lanes] = jnp.sum(both, axis=0, keepdims=True)


def far_kernel(
    gx, gy, gz,
    ml, ma, mb, t2, near, pos, cnt, top,
    pot_out, loc_out,
    lw, la, lb, lr, pa, ln, to_lanes,
):
    def shifted(v):
        return [v, pltpu.roll(v, 7, 0), pltpu.roll(v, 6, 0)]

    for xs in range(8):
        over_x = -1 if xs < 2 else (1 if xs >= 6 else 0)
        turned = []
        for yp in range(4):
            over_y = -1 if yp < 1 else (1 if yp >= 3 else 0)
            keep = jnp.where(inside(gx, over_x) & inside(gy, over_y), 1.0, 0.0).astype(F32)
            tile = ml[xs, yp].astype(F32) * keep
            turned.append((shifted(tile[0:8]), shifted(tile[8:16])))
        for w in range(6):
            for j in range(3):
                lw[xs, w, :, j * 128 : j * 128 + 128] = jnp.concatenate(
                    [turned[w // 2][w % 2][j], turned[w // 2 + 1][w % 2][j]], axis=0
                ).astype(BF16)
    zero8 = jnp.zeros((8, 128), F32)
    a_tiles = {}
    for xs in range(6):
        over_x = -1 if xs < 2 else (1 if xs >= 4 else 0)
        for yp in range(3):
            over_y = yp - 1
            keep = jnp.where(inside(gx, over_x) & inside(gy, over_y), 1.0, 0.0).astype(F32)
            tile = ma[xs, yp].astype(F32) * keep
            a_tiles[xs, yp] = (shifted(tile[0:8]), shifted(tile[8:16]))
    for dx in range(7):
        for w in range(6):
            for j in range(3):
                first = a_tiles[dx - 1, w // 2][w % 2][j] if dx >= 1 else zero8
                second = a_tiles[dx, w // 2][w % 2][j] if dx <= 5 else zero8
                la[dx, w, :, j * 128 : j * 128 + 128] = jnp.concatenate(
                    [first, second], axis=0
                ).astype(BF16)
    row16 = iota((16, 128), 0)
    odd_x, odd_y = lax.rem(gx, 2), lax.rem(gy, 2)
    for dx in range(7):
        ok_x = inside(gx, dx - 3)
        if dx == 0:
            ok_x = ok_x & (odd_x == 1)
        if dx == 6:
            ok_x = ok_x & (odd_x == 0)
        for w in range(6):
            dy = w + 1 - odd_y
            keep = jnp.where(ok_x & inside(gy, dy - 3), 1.0, 0.0).astype(F32)
            tile = mb[dx, dy].astype(F32) * keep
            for j in range(3):
                lb[dx, w, :, j * 128 : j * 128 + 128] = jnp.where(
                    (row16 >> 2) == j, tile, 0.0
                ).astype(BF16)

    total = [jnp.zeros((16, 256), F32) for _ in range(6)]
    for dx in range(7):
        xs_of = [x for x in range(4) if not (dx == 0 and x % 2 == 0) and not (dx == 6 and x % 2 == 1)]
        for w in range(6):
            g = dx * 7 + w + 1
            weights = jnp.concatenate(
                [t2[g * 384 : (g + 1) * 384, :], t2[(g - 1) * 384 : g * 384, :]], axis=1
            )
            left = [lw[x + dx - 1, w] for x in xs_of] + [la[dx, w], lb[dx, w]]
            made = jnp.dot(
                jnp.concatenate(left, axis=0), weights, preferred_element_type=F32
            )
            for i, slot in enumerate(xs_of + [4, 5]):
                total[slot] = total[slot] + made[i * 16 : i * 16 + 16]

    row, col = iota((64, 64), 0), iota((64, 64), 1)
    order = jnp.where(((row & 1) << 5) + (row >> 1) == col, 1.0, 0.0).astype(BF16)

    def ordered(v):
        return jnp.dot(v.astype(BF16), order, preferred_element_type=F32).astype(BF16)

    v_of = []
    for px in range(2):
        r = 49 * 384 + px * 128
        v_of.append(jnp.concatenate([t2[r : r + 64, :], t2[r + 64 : r + 128, :]], axis=1))
    sb = total[5]
    sb = sb[0:4] + sb[4:8] + sb[8:12]
    sb = jnp.where(odd_y == 1, sb[:, 128:256], sb[:, 0:128])
    parity = lax.rem(iota((4, 64), 0) + gz, 2)
    sb = jnp.where(parity == 1, sb[:, 64:128], sb[:, 0:64])
    topv = top[0]
    top4 = jnp.concatenate(
        [topv[:, 0:64], topv[:, 64:128], topv[:, 128:192], jnp.zeros((1, 64), F32)], axis=0
    )
    local_b = ordered(jnp.concatenate([top4 + 0.25 * sb, jnp.zeros((12, 64), F32)], axis=0))
    for xa in range(2):
        down = jnp.dot(local_b, v_of[xa], preferred_element_type=F32)[0:4]
        local_a = 0.5 * total[4][xa * 8 : xa * 8 + 4] + down
        for ya in range(2):
            for p in range(2):
                b = ya * 128 + p * 64
                pa[pl.ds(xa * 16 + ya * 8 + p, 4, stride=2), 0:64] = local_a[:, b : b + 64]
    for xa in range(2):
        parent = ordered(pa[xa * 16 : xa * 16 + 16, 0:64])
        for px in range(2):
            x = 2 * xa + px
            leaf = total[x] + jnp.dot(parent, v_of[px], preferred_element_type=F32)
            lr[x * 32 : x * 32 + 16, :] = leaf[:, 0:128]
            lr[x * 32 + 16 : x * 32 + 32, :] = leaf[:, 128:256]
    for x in range(4):
        for y in range(4):
            for zp in range(6):
                r = x * 32 + (y % 2) * 16 + (y // 2) * 8 + zp
                ln[x * 4 + y : x * 4 + y + 1, zp * 128 : zp * 128 + 128] = lr[r : r + 1, :]

    coef = jnp.concatenate([ln[:, zp * 128 : zp * 128 + 128] for zp in range(6)], axis=0)
    high, low = pieces(coef, 2)
    coef = jnp.concatenate([high.astype(BF16), low.astype(BF16)], axis=1)
    cheb = []
    for d in range(3):
        u = 2.0 * jnp.concatenate(
            [pos[d, x, :, zp * 128 : zp * 128 + 128] for zp in range(6) for x in range(4)], axis=0
        ) - 1.0
        second = 2.0 * u * u - 1.0
        cheb.append([None, u, second, 2.0 * u * second - u])
    out = None
    for a in range(4):
        spread = jnp.dot(
            coef, to_lanes[:, a * 2048 : a * 2048 + 2048], preferred_element_type=F32
        )
        sum_b = None
        for b in range(4):
            sum_c = None
            for c in range(4):
                term = spread[:, (4 * b + c) * 128 : (4 * b + c) * 128 + 128]
                if c:
                    term = term * cheb[2][c]
                sum_c = term if sum_c is None else sum_c + term
            if b:
                sum_c = sum_c * cheb[1][b]
            sum_b = sum_c if sum_b is None else sum_b + sum_c
        if a:
            sum_b = sum_b * cheb[0][a]
        out = sum_b if out is None else out + sum_b
    for zp in range(6):
        lanes = slice(zp * 128, zp * 128 + 128)
        value = out[zp * 16 : zp * 16 + 16] * 0.125 + near[:, lanes]
        for x in range(4):
            limit, slot = count_lanes(cnt[x], zp)
            pot_out[x, :, lanes] = jnp.where(slot < limit, value[x * 4 : x * 4 + 4], 0.0)
            loc_out[x, :, lanes] = ln[x * 4 : x * 4 + 4, lanes]


def lane_spread(to_lanes):
    row, col = iota((128, 128), 0), iota((128, 128), 1)

    def one(c, carry):
        block = jnp.where(row == (col & 64) + c, 1.0, 0.0).astype(BF16)
        lanes = pl.ds(pl.multiple_of(c * 128, 128), 128)
        to_lanes[0:128, lanes] = block
        to_lanes[128:256, lanes] = block
        return carry

    lax.fori_loop(0, 64, one, 0)


def whole_kernel(
    pos_in, chg_in, soft_in, cnt_in, top_in, bm_in, am_in, lm_in, m2l_in, l2l_in,
    pot_out, loc_out,
    t2, near, pos, cnt, top, lw, la, lb, lr, pa, ln, to_lanes,
    pf, ml, ma, mb, zs, zr, ps, mls, mas, ms, zf, mt, s2,
    chg, soft, bm, am, lm, l2l,
    a_own, q_own, a_side, q_side, a_edge, q_edge, b_mat, ft, fs, wt, near8,
    send, recv, local,
):
    gx, gy, gz = (lax.axis_index(a) for a in AXES)

    def at(ox, oy, oz):
        return (
            lax.rem(gx + (ox + 8), 8),
            lax.rem(gy + (oy + 8), 8),
            lax.rem(gz + (oz + 8), 8),
        )

    fetched = [(lm_in, lm), (am_in, am), (bm_in, bm), (pos_in, pos), (cnt_in, cnt)]
    fetched += [(chg_in, chg), (soft_in, soft), (l2l_in, l2l), (top_in, top), (m2l_in, mt)]
    fetched = [
        pltpu.make_async_copy(src, dst, local.at[i]) for i, (src, dst) in enumerate(fetched)
    ]
    for copy in fetched:
        copy.start()
    barrier = pltpu.get_barrier_semaphore()
    around = [at(0, 0, 1), at(0, 0, -1)]
    for o in (1, -1, 2, -2, 3, -3):
        around += [at(o, 0, 0), at(0, o, 0)]
    for who in around:
        pl.semaphore_signal(barrier, inc=1, device_id=who, device_id_type=MESH)

    number = [0]

    def remote(src, dst, who):
        i = number[0]
        number[0] += 1
        copy = pltpu.make_async_remote_copy(
            src_ref=src, dst_ref=dst, send_sem=send.at[i], recv_sem=recv.at[i],
            device_id=who, device_id_type=MESH,
        )
        copy.start()
        return copy

    for copy in fetched[:3]:
        copy.wait()
    for x in range(4):
        block = lm[x].astype(F32)
        for zp in range(6):
            ms[zp * 16 + x * 4 : zp * 16 + x * 4 + 4, :] = block[:, zp * 128 : zp * 128 + 128]
    for x in range(2):
        block = am[x].astype(F32)
        for zp in range(3):
            ms[96 + zp * 4 + x * 2 : 98 + zp * 4 + x * 2, :] = block[:, zp * 128 : zp * 128 + 128]
    bcells = bm[0].astype(F32)
    ms[108:109, :] = bcells[:, 0:128]
    ms[109:110, :] = jnp.concatenate([bcells[:, 64:128], bcells[:, 128:192]], axis=1)
    ms[110:112, :] = jnp.zeros((2, 128), F32)
    row, col = iota((128, 128), 0), iota((128, 128), 1)
    moved = (row & 64) + ((row & 1) << 5) + ((row & 63) >> 1)
    order = jnp.where(moved == col, 1.0, 0.0).astype(BF16)
    ms[...] = jnp.dot(ms[...].astype(BF16), order, preferred_element_type=F32)

    for copy in fetched[3:7]:
        copy.wait()
    own = []
    for x in range(4):
        own.append([pos[0, x] - 0.5, pos[1, x] - 0.5, pos[2, x] - 0.5, chg[x], soft[x]])

    def own_piece(x, f, zp):
        piece = own[x][f][:, zp * 128 : zp * 128 + 128]
        if f == 3:
            limit, slot = count_lanes(cnt[x], zp)
            piece = jnp.where(slot < limit, piece, 0.0)
        return piece

    zf[...] = jnp.zeros_like(zf)
    for side, (lp, ap) in enumerate(((0, 0), (5, 2))):
        base = side * 112
        for x in range(4):
            for f in range(5):
                zf[base + f * 16 + x * 4 : base + f * 16 + x * 4 + 4, :] = own_piece(x, f, lp)
        zf[base + 80 : base + 96, :] = ms[lp * 16 : lp * 16 + 16, :]
        zf[base + 96 : base + 100, :] = ms[96 + ap * 4 : 100 + ap * 4, :]
        zf[base + 100 : base + 102, :] = ms[108:110, :]
        zs[side] = zf[base : base + 112, :].astype(BF16)
    pl.semaphore_wait(barrier, 14)

    z_copies = [
        remote(zs.at[0], zr.at[1], at(0, 0, -1)),
        remote(zs.at[1], zr.at[0], at(0, 0, 1)),
    ]
    ps[...] = jnp.zeros_like(ps)
    mas[...] = jnp.zeros_like(mas)
    for x in range(4):
        for zp in range(6):
            for f in range(5):
                ps[pl.ds(x * 224 + f * 8 + 1 + zp, 4, stride=56), :] = own_piece(x, f, zp)
    for zp in range(6):
        for x in range(4):
            mls[pl.ds(x * 32 + zp + 1, 4, stride=8), :] = ms[
                zp * 16 + x * 4 : zp * 16 + x * 4 + 4, :
            ]
    for zp in range(3):
        for x in range(2):
            mas[pl.ds(x * 16 + zp + 1, 2, stride=8), :] = ms[
                96 + zp * 4 + x * 2 : 98 + zp * 4 + x * 2, :
            ]

    near8[...] = jnp.zeros_like(near8)
    b_mat[...] = jnp.zeros_like(b_mat)
    wt[...] = jnp.zeros_like(wt)
    target_features(pos, soft, fs, ft)
    lane_spread(to_lanes)

    for copy in fetched[7:]:
        copy.wait()

    def unpack(i, carry):
        block = mt[pl.ds(pl.multiple_of(i * 16, 16), 16), :].astype(F32)
        unpack_rows(block, i * 16, s2, 16)
        return carry

    lax.fori_loop(0, 21, unpack, 0)
    unpack_rows(mt[336:343, :].astype(F32), 336, s2, 7)
    unpack_rows(l2l[...].astype(F32), 343, s2, 8)

    for copy in z_copies:
        copy.wait()
    keep_low = jnp.where(gz > 0, 1.0, 0.0).astype(F32)
    keep_high = jnp.where(gz < 7, 1.0, 0.0).astype(F32)
    b_rows = []
    for side, (keep, zp_l, zp_a) in enumerate(((keep_low, 0, 0), (keep_high, 7, 4))):
        got = zr[side].astype(F32) * keep
        for x in range(4):
            for f in range(5):
                ps[pl.ds(x * 224 + f * 8 + zp_l, 4, stride=56), :] = got[
                    f * 16 + x * 4 : f * 16 + x * 4 + 4, :
                ]
            mls[pl.ds(x * 32 + zp_l, 4, stride=8), :] = got[80 + x * 4 : 84 + x * 4, :]
        for x in range(2):
            mas[pl.ds(x * 16 + zp_a, 2, stride=8), :] = got[96 + x * 2 : 98 + x * 2, :]
        b_rows.append((got[100:101, :], got[101:102, :]))
    (left_a, left_b), (ra, rb) = b_rows
    oa, ob = ms[108:109, :], ms[109:110, :]
    low1 = iota((1, 128), 1) < 64
    middle = jnp.where(low1, pltpu.roll(left_b, 64, 1), pltpu.roll(oa, 64, 1))
    middle_r = jnp.where(low1, pltpu.roll(ob, 64, 1), pltpu.roll(ra, 64, 1))
    pairs = [left_a, left_b, middle, oa, ob, middle_r, ra, rb]
    even_z = lax.rem(gz, 2) == 0
    zf[0:16, :] = jnp.zeros((16, 128), F32)
    for l in range(3):
        at_even = l + 1 - l % 2
        at_odd = l + 1 - (l + 1) % 2
        for j in range(3):
            zf[4 * j + l : 4 * j + l + 1, :] = jnp.where(
                even_z, pairs[at_even + 2 * j], pairs[at_odd + 2 * j]
            )
    mb[3, 3] = zf[0:16, :].astype(BF16)
    x_b = []
    for o in (1, -1, 2, -2, 3, -3):
        x_b.append(remote(mb.at[3, 3], mb.at[3 - o, 3], at(o, 0, 0)))
    for x in range(4):
        for y in range(4):
            for t in range(3):
                r = (x * 4 + y) * 56 + t * 16
                pf[1 + x, 1 + y, t] = ps[r : r + 16, :].astype(BF16)
        for yp in range(2):
            r = x * 32 + yp * 16
            ml[2 + x, 1 + yp] = mls[r : r + 16, :].astype(BF16)
    for x in range(2):
        ma[2 + x, 1] = mas[x * 16 : x * 16 + 16, :].astype(BF16)

    own_x, own_xl, own_xa = pl.ds(1, 4), pl.ds(2, 4), pl.ds(2, 2)
    up, down = at(0, 1, 0), at(0, -1, 0)
    y_copies = [
        remote(pf.at[own_x, pl.ds(4, 1)], pf.at[own_x, pl.ds(0, 1)], up),
        remote(pf.at[own_x, pl.ds(1, 1)], pf.at[own_x, pl.ds(5, 1)], down),
        remote(ml.at[own_xl, pl.ds(2, 1)], ml.at[own_xl, pl.ds(0, 1)], up),
        remote(ml.at[own_xl, pl.ds(1, 1)], ml.at[own_xl, pl.ds(3, 1)], down),
        remote(ma.at[own_xa, pl.ds(1, 1)], ma.at[own_xa, pl.ds(0, 1)], up),
        remote(ma.at[own_xa, pl.ds(1, 1)], ma.at[own_xa, pl.ds(2, 1)], down),
    ]

    low_lanes = iota((32, 128), 1) < 64

    def pair_up(g, carry):
        near = (jnp.abs(g // 7 - 3) <= 1) & (jnp.abs(lax.rem(g, 7) - 3) <= 1)
        kept = jnp.where(near, 0.0, 1.0).astype(F32)
        tables = []
        for i in range(7):
            one = s2[pl.ds(pl.multiple_of((g * 7 + i) * 40, 8), 32), :]
            if 2 <= i <= 4:
                one = one * kept
            tables.append((one, pltpu.roll(one, 64, 1)))
        for w in range(6):
            (first, turned_first), (second, turned_second) = tables[w + 1], tables[w]
            to = g * 384 + w * 64
            t2[pl.ds(pl.multiple_of(to, 32), 32), :] = jnp.where(
                low_lanes, first, turned_second
            ).astype(BF16)
            t2[pl.ds(pl.multiple_of(to + 32, 32), 32), :] = jnp.where(
                low_lanes, turned_first, second
            ).astype(BF16)
        return carry

    def own_columns(i, carry):
        where = [(i, cy, a_own, q_own, (i - 1) * 4 + cy - 1) for cy in range(1, 5)]
        source_columns(where, gx, gy, pf, wt)
        return carry

    def pair_some(i):
        for u in range(6):
            pair_up(jnp.minimum(i * 6 + u, 48), 0)

    def own_pairs(t, carry):
        own_slab(t, a_own, q_own, b_mat, ft, near8)
        pair_some(t - 1)
        return carry

    lax.fori_loop(1, 5, own_columns, 0)
    lax.fori_loop(1, 5, own_pairs, 0)
    for copy in x_b:
        copy.wait()
    y_b = []
    for o in (1, -1, 2, -2, 3, -3):
        y_b.append(remote(mb.at[:, pl.ds(3, 1)], mb.at[:, pl.ds(3 - o, 1)], at(0, o, 0)))
    for copy in y_copies:
        copy.wait()

    up, down = at(1, 0, 0), at(-1, 0, 0)
    x_copies = [
        remote(pf.at[pl.ds(4, 1)], pf.at[pl.ds(0, 1)], up),
        remote(pf.at[pl.ds(1, 1)], pf.at[pl.ds(5, 1)], down),
        remote(ml.at[pl.ds(4, 2)], ml.at[pl.ds(0, 2)], up),
        remote(ml.at[pl.ds(2, 2)], ml.at[pl.ds(6, 2)], down),
        remote(ma.at[pl.ds(2, 2)], ma.at[pl.ds(0, 2)], up),
        remote(ma.at[pl.ds(2, 2)], ma.at[pl.ds(4, 2)], down),
    ]
    def own_pairs_y(t, carry):
        cx = t - 4
        where = [(cx, 0, a_edge, q_edge, cx), (cx, 5, a_edge, q_edge, cx + 6)]
        source_columns(where, gx, gy, pf, wt)
        own_slab(t, a_own, q_own, b_mat, ft, near8)
        pair_some(t - 1)
        return carry

    lax.fori_loop(5, 9, own_pairs_y, 0)
    pair_up(48, 0)
    for child in range(4):
        r = (343 + 2 * child) * 40
        even, odd = pair_rows(s2[r : r + 32, :], s2[r + 40 : r + 40 + 32, :], low_lanes)
        to = 49 * 384 + child * 64
        t2[to : to + 32, :] = even
        t2[to + 32 : to + 64, :] = odd
    for copy in x_copies + y_b:
        copy.wait()

    def own_pairs_x(i, carry):
        cx = i * 5
        where = [(cx, 0, a_edge, q_edge, cx), (cx, 5, a_edge, q_edge, cx + 6)]
        where += [(cx, cy, a_side, q_side, i * 4 + cy - 1) for cy in range(1, 5)]
        source_columns(where, gx, gy, pf, wt)
        own_slab(i + 9, a_own, q_own, b_mat, ft, near8)
        edge_pairs(i + 1, a_edge, q_edge, b_mat, ft, near8)
        return carry

    def last_pairs(i, carry):
        slab_pairs(i * 3, None, a_side, q_side, i * 4, b_mat, ft, near8)
        edge_pairs(i * 3, a_edge, q_edge, b_mat, ft, near8)
        return carry

    lax.fori_loop(0, 2, own_pairs_x, 0)
    lax.fori_loop(0, 2, last_pairs, 0)
    gather_near(near8, near)
    far_kernel(
        gx, gy, gz, ml, ma, mb, t2, near, pos, cnt, top, pot_out, loc_out,
        lw, la, lb, lr, pa, ln, to_lanes,
    )


NEAR_SCRATCH = [
    ((1024, 256), BF16),
    ((1024, 1664), BF16),
    ((512, 256), BF16),
    ((512, 1664), BF16),
    ((768, 256), BF16),
    ((768, 1664), BF16),
    ((6, 9, 256, 256), BF16),
    ((16, 3, 2, 16, 768), BF16),
    ((6, 96, 128), F32),
    ((6, 208, 128), F32),
    ((16, 2, 8, 768), F32),
]


FAR_SCRATCH = [
    ((8, 6, 16, 384), BF16),
    ((7, 6, 16, 384), BF16),
    ((7, 6, 16, 384), BF16),
    ((128, 128), F32),
    ((32, 128), F32),
    ((16, 768), F32),
    ((256, 8192), BF16),
]


def run(*args):
    halos = [(6, 6, 3, 16, 128), (8, 4, 16, 128), (6, 3, 16, 128), (7, 7, 16, 128)]
    scratch = [((T2_ROWS, 128), BF16), ((16, 768), F32), ((3, 4, 4, 768), F32)]
    scratch += [((4, 4, 12), jnp.int32), ((1, 1, 192), F32)] + FAR_SCRATCH
    scratch += [(s, BF16) for s in halos]
    scratch += [((2, 112, 128), BF16), ((2, 112, 128), BF16), ((896, 128), F32), ((128, 128), F32)]
    scratch += [((32, 128), F32), ((112, 128), F32), ((224, 128), F32), ((343, 4096), BF16)]
    scratch += [((352 * 40, 128), F32), ((4, 4, 768), F32), ((4, 4, 768), F32)]
    scratch += [((1, 1, 192), BF16), ((2, 2, 384), BF16), ((4, 4, 768), BF16), ((8, 4096), BF16)]
    return pl.pallas_call(
        whole_kernel,
        name="downward",
        out_shape=[jax.ShapeDtypeStruct((4, 4, 768), F32)] * 2,
        in_specs=[pl.BlockSpec(memory_space=pltpu.HBM)] * 10,
        out_specs=[pl.BlockSpec(memory_space=pltpu.VMEM)] * 2,
        scratch_shapes=[pltpu.VMEM(s, t) for s, t in scratch + NEAR_SCRATCH]
        + [
            pltpu.SemaphoreType.DMA((26,)),
            pltpu.SemaphoreType.DMA((26,)),
            pltpu.SemaphoreType.DMA((10,)),
        ],
        compiler_params=pltpu.CompilerParams(
            collective_id=0, has_side_effects=True, vmem_limit_bytes=VMEM_BYTES
        ),
        cost_estimate=pl.CostEstimate(
            flops=10**10, bytes_accessed=10**7, transcendentals=2 * 10**7
        ),
    )(*args)


def hand_over_kernel(pot_in, loc_in, pot_out, loc_out, sems):
    copies = [
        pltpu.make_async_copy(pot_in, pot_out, sems.at[0]),
        pltpu.make_async_copy(loc_in, loc_out, sems.at[1]),
    ]
    for copy in copies:
        copy.start()
    for copy in copies:
        copy.wait()


def hand_over(*results):
    hbm = pl.BlockSpec(memory_space=pltpu.HBM)
    return pl.pallas_call(
        hand_over_kernel,
        name="hand_over",
        out_shape=[jax.ShapeDtypeStruct((4, 4, 768), F32)] * 2,
        in_specs=[hbm] * 2,
        out_specs=[hbm] * 2,
        scratch_shapes=[pltpu.SemaphoreType.DMA((2,))],
        compiler_params=pltpu.CompilerParams(vmem_limit_bytes=VMEM_BYTES),
    )(*results)


def per_device(pos, chg, soft, cnt, top, bm, am, lm, m2l, l2l):
    return tuple(hand_over(*run(pos, chg, soft, cnt, top, bm, am, lm, m2l, l2l)))


def solution(mesh):
    split = P("gx", "gy", "gz")
    in_specs = (P(None, "gx", "gy", "gz"),) + (split,) * 7 + (P(), P())
    return jax.shard_map(
        per_device, mesh=mesh, in_specs=in_specs, out_specs=(split, split), check_vma=False
    )
```

```python
import functools
import jax
import jax.numpy as jnp
from jax import lax
from jax.experimental import pallas as pl
from jax.experimental.pallas import tpu as pltpu
from jax.sharding import PartitionSpec as P

F32 = jnp.float32
BF16 = jnp.bfloat16
MESH = pl.DeviceIdType.MESH
AXES = ("gx", "gy", "gz")
T2_ROWS = 49 * 384 + 256
VMEM_BYTES = 63 * 2**20


def iota(shape, dim):
    return lax.broadcasted_iota(jnp.int32, shape, dim)


def count_lanes(counts, pair):
    rows = counts.shape[0]
    lane = iota((rows, 128), 1)
    low = counts[:, 2 * pair : 2 * pair + 1]
    high = counts[:, 2 * pair + 1 : 2 * pair + 2]
    return jnp.where(lane < 64, low, high), lane & 63


def unpack_rows(block, base, s2, rows):
    for c in range(32):
        s2[pl.ds(base * 40 + c, rows, stride=40), :] = block[:, c * 128 : (c + 1) * 128]


def pair_rows(first, second, low_lanes):
    turned_first = pltpu.roll(first, 64, 1)
    turned_second = pltpu.roll(second, 64, 1)
    even = jnp.where(low_lanes, first, turned_second)
    odd = jnp.where(low_lanes, turned_first, second)
    return even.astype(BF16), odd.astype(BF16)


def pieces(value, count):
    out = []
    for _ in range(count - 1):
        head = value.astype(BF16).astype(F32)
        out.append(head)
        value = value - head
    return out + [value]


def inside(coord, offset):
    return (coord + offset >= 0) & (coord + offset <= 7)


def source_columns(where, gx, gy, pf, wt, base=0):
    ones = jnp.ones((8, 128), F32)
    same = jnp.where(iota((128, 128), 0) == iota((128, 128), 1), 1.0, 0.0).astype(BF16)
    er, ec = iota((16, 1024), 0), iota((16, 1024), 1)
    spread = jnp.where(((er & 7) * 2 + (er >> 3)) == (ec >> 6), 1.0, 0.0).astype(BF16)
    charges = []
    for slot, (cx, cy, _, _, _) in enumerate(where):
        slot = slot + base
        xy = pf[cx, cy, 0].astype(F32)
        zq = pf[cx, cy, 1].astype(F32)
        s = pf[cx, cy, 2].astype(F32)[0:8]
        x, y, z, q = xy[0:8], xy[8:16], zq[0:8], zq[8:16]
        over_x = jnp.where(cx == 0, -1, jnp.where(cx == 5, 1, 0))
        over_y = jnp.where(cy == 0, -1, jnp.where(cy == 5, 1, 0))
        q = q * jnp.where(inside(gx, over_x) & inside(gy, over_y), 1.0, 0.0).astype(F32)
        ix = ones * (jnp.asarray(cx, F32) - 2.5)
        iy = ones * (jnp.asarray(cy, F32) - 2.5)
        n = (x + ix) * (x + ix) + (y + iy) * (y + iy) + z * z + 0.5 * (s * s)
        feats = [x, x, ix, ix, y, y, iy, iy, z, z, ones, ones, ones] + pieces(n, 3)
        for f in range(16):
            wt[slot, pl.ds(f, 8, stride=24), :] = feats[f]
        wt[slot, 192:200, :] = q
    for slot, (_, _, a_mat, q_mat, at) in enumerate(where):
        tile = [wt[slot + base, zp * 24 : zp * 24 + 16, :] for zp in range(8)]
        tile = jnp.concatenate(tile + [wt[slot + base, 192:208, :]], axis=0)
        turned = lax.dot_general(
            same, tile.astype(BF16), (((1,), (1,)), ((), ())), preferred_element_type=F32
        )
        rows = pl.ds(pl.multiple_of(at * 64, 64), 64)
        a_mat[rows, 0:128] = turned[0:64, 0:128].astype(BF16)
        a_mat[rows, 128:256] = turned[64:128, 0:128].astype(BF16)
        charges.append(
            jnp.concatenate([turned[0:64, 128:136], turned[64:128, 128:136]], axis=1)
        )
    wide = jnp.dot(
        jnp.concatenate(charges, axis=0).astype(BF16), spread, preferred_element_type=F32
    )
    low = iota((64, 128), 1) < 64
    for slot, (_, _, a_mat, q_mat, at) in enumerate(where):
        rows = pl.ds(pl.multiple_of(at * 64, 64), 64)
        v = [wide[slot * 64 : slot * 64 + 64, m * 128 : m * 128 + 128] for m in range(8)]
        for m in range(6):
            q_mat[rows, m * 128 : m * 128 + 128] = v[m + 1].astype(BF16)
        for m in range(7):
            q_mat[rows, 768 + m * 128 : 896 + m * 128] = jnp.where(low, v[m + 1], v[m]).astype(BF16)


def target_features(pos, soft, fs, ft):
    lane = iota((64, 128), 1)

    def put(f, v):
        for zp in range(6):
            fs[zp, pl.ds(f, 4, stride=24), :] = v[:, zp * 128 : zp * 128 + 128]

    for x in range(4):
        px, py, pz = (pos[d, x] - 0.5 for d in range(3))
        s = soft[x]
        fx = px + (x - 1.5)
        fy = py + (iota((4, 768), 0).astype(F32) - 1.5)
        ax, bx = pieces(fx, 2)
        ay, by = pieces(fy, 2)
        bx, by = bx.astype(BF16).astype(F32), by.astype(BF16).astype(F32)
        xx, yy = ax + bx, ay + by
        base = xx * xx + yy * yy + 0.5 * (s * s)
        for f, v in ((0, ax), (1, bx), (2, ax), (3, bx), (4, ay), (5, by), (6, ay), (7, by)):
            put(f, -2.0 * v)
        for f in (13, 14, 15):
            put(f, jnp.ones((4, 768), F32))
        for d in range(3):
            az, bz = pieces(pz - (d - 1.0), 2)
            bz = bz.astype(BF16).astype(F32)
            zz = az + bz
            n = base + zz * zz
            for f, v in zip((8, 9, 10, 11, 12), [-2.0 * az, -2.0 * bz] + pieces(n, 3)):
                put(f, v)
            for zp in range(6):
                made = jnp.concatenate(
                    [fs[zp, y * 24 : y * 24 + 16, :] for y in range(4)], axis=0
                )
                if d != 1:
                    made = pltpu.roll(made, 64, 1)
                for e in range(2):
                    mine = lane < 64 if (e == 0) == (d == 1) else lane >= 64
                    half = jnp.where(mine, made, 0.0).astype(BF16)
                    for y in range(4):
                        ft[x * 4 + y, d, e, :, zp * 128 : zp * 128 + 128] = half[
                            y * 16 : y * 16 + 16
                        ]


Q_AT = (768, 0, 896)


def set_weights(b_mat, slot, ft, g):
    for k in range(3):
        for d in range(3):
            for h in range(2):
                for e in range(2):
                    cell = 4 * k + 2 + 2 * h + e + d - 1
                    r = (cell % 2) * 128 + (cell // 2) * 16
                    b_mat[slot, k * 3 + d, r : r + 16, h * 128 : h * 128 + 128] = ft[
                        g, d, e, :, (2 * k + h) * 128 : (2 * k + h) * 128 + 128
                    ]


def add_pairs(left, q_of, b_mat, slot, near8, g, own=None):
    rows = left.shape[0]
    for k in range(3):
        lanes = slice(256 * k, 256 * k + 256)
        for d in range(3):
            r2 = jnp.dot(left, b_mat[slot, k * 3 + d], preferred_element_type=F32)
            q = q_of(Q_AT[d] + 256 * k).astype(F32)
            if d == 1 and own is not None:
                q = q * own
            part = jnp.sum((lax.rsqrt(r2) * q).reshape(rows // 8, 8, 256), axis=0)
            if d == 0:
                swapped = part
            elif d == 1:
                plain = part
            else:
                swapped = swapped + part
        near8[g, 0, :, lanes] += plain
        near8[g, 1, :, lanes] += swapped


def slab_pairs(x, itself, a_mat, q_mat, at, b_mat, ft, near8):
    one = jnp.ones((64, 256), F32)
    for y in range(4):
        low, high = max(0, y - 1), min(3, y + 1)
        set_weights(b_mat, y, ft, x * 4 + y)
        rows = pl.ds(pl.multiple_of((at + low) * 64, 64), (high - low + 1) * 64)
        own = None
        if itself is not None:
            own = jnp.concatenate(
                [itself if cy == y else one for cy in range(low, high + 1)], axis=0
            )
        add_pairs(
            a_mat[rows, :], lambda at: q_mat[rows, at : at + 256], b_mat, y, near8, x * 4 + y, own
        )


def own_slab(t, a_own, q_own, b_mat, ft, near8):
    x, dx = t // 3, lax.rem(t, 3)
    itself = jnp.where(iota((64, 256), 0) == (iota((64, 256), 1) & 63), 0.0, 1.0).astype(F32)
    itself = jnp.where(dx == 1, itself, 1.0)
    slab_pairs(x, itself, a_own, q_own, (x + dx - 1) * 4, b_mat, ft, near8)


def edge_pairs(x, a_edge, q_edge, b_mat, ft, near8):
    for side, y in enumerate((0, 3)):
        set_weights(b_mat, 4 + side, ft, x * 4 + y)
        rows = pl.ds(pl.multiple_of((side * 6 + x) * 64, 64), 192)
        add_pairs(
            a_edge[rows, :], lambda at: q_edge[rows, at : at + 256], b_mat, 4 + side, near8, x * 4 + y
        )


def gather_near(near8, near):
    for g in range(16):
        for zp in range(6):
            lanes = slice(zp * 128, zp * 128 + 128)
            both = near8[g, 0, :, lanes] + pltpu.roll(near8[g, 1, :, lanes], 64, 1)
            near[g : g + 1, lanes] = jnp.sum(both, axis=0, keepdims=True)


def far_kernel(
    gx, gy, gz,
    ml, ma, mb, t2, near, pos, cnt, top,
    pot_out, loc_out,
    lw, la, lb, lr, pa, ln, to_lanes,
):
    def shifted(v):
        return [v, pltpu.roll(v, 7, 0), pltpu.roll(v, 6, 0)]

    for xs in range(8):
        over_x = -1 if xs < 2 else (1 if xs >= 6 else 0)
        turned = []
        for yp in range(4):
            over_y = -1 if yp < 1 else (1 if yp >= 3 else 0)
            keep = jnp.where(inside(gx, over_x) & inside(gy, over_y), 1.0, 0.0).astype(F32)
            tile = ml[xs, yp].astype(F32) * keep
            turned.append((shifted(tile[0:8]), shifted(tile[8:16])))
        for w in range(6):
            for j in range(3):
                lw[xs, w, :, j * 128 : j * 128 + 128] = jnp.concatenate(
                    [turned[w // 2][w % 2][j], turned[w // 2 + 1][w % 2][j]], axis=0
                ).astype(BF16)
    zero8 = jnp.zeros((8, 128), F32)
    a_tiles = {}
    for xs in range(6):
        over_x = -1 if xs < 2 else (1 if xs >= 4 else 0)
        for yp in range(3):
            over_y = yp - 1
            keep = jnp.where(inside(gx, over_x) & inside(gy, over_y), 1.0, 0.0).astype(F32)
            tile = ma[xs, yp].astype(F32) * keep
            a_tiles[xs, yp] = (shifted(tile[0:8]), shifted(tile[8:16]))
    for dx in range(7):
        for w in range(6):
            for j in range(3):
                first = a_tiles[dx - 1, w // 2][w % 2][j] if dx >= 1 else zero8
                second = a_tiles[dx, w // 2][w % 2][j] if dx <= 5 else zero8
                la[dx, w, :, j * 128 : j * 128 + 128] = jnp.concatenate(
                    [first, second], axis=0
                ).astype(BF16)
    row16 = iota((16, 128), 0)
    odd_x, odd_y = lax.rem(gx, 2), lax.rem(gy, 2)
    for dx in range(7):
        ok_x = inside(gx, dx - 3)
        if dx == 0:
            ok_x = ok_x & (odd_x == 1)
        if dx == 6:
            ok_x = ok_x & (odd_x == 0)
        for w in range(6):
            dy = w + 1 - odd_y
            keep = jnp.where(ok_x & inside(gy, dy - 3), 1.0, 0.0).astype(F32)
            tile = mb[dx, dy].astype(F32) * keep
            for j in range(3):
                lb[dx, w, :, j * 128 : j * 128 + 128] = jnp.where(
                    (row16 >> 2) == j, tile, 0.0
                ).astype(BF16)

    total = [jnp.zeros((16, 256), F32) for _ in range(6)]
    for dx in range(7):
        xs_of = [x for x in range(4) if not (dx == 0 and x % 2 == 0) and not (dx == 6 and x % 2 == 1)]
        for w in range(6):
            g = dx * 7 + w + 1
            weights = jnp.concatenate(
                [t2[g * 384 : (g + 1) * 384, :], t2[(g - 1) * 384 : g * 384, :]], axis=1
            )
            left = [lw[x + dx - 1, w] for x in xs_of] + [la[dx, w], lb[dx, w]]
            made = jnp.dot(
                jnp.concatenate(left, axis=0), weights, preferred_element_type=F32
            )
            for i, slot in enumerate(xs_of + [4, 5]):
                total[slot] = total[slot] + made[i * 16 : i * 16 + 16]

    row, col = iota((64, 64), 0), iota((64, 64), 1)
    order = jnp.where(((row & 1) << 5) + (row >> 1) == col, 1.0, 0.0).astype(BF16)

    def ordered(v):
        return jnp.dot(v.astype(BF16), order, preferred_element_type=F32).astype(BF16)

    v_of = []
    for px in range(2):
        r = 49 * 384 + px * 128
        v_of.append(jnp.concatenate([t2[r : r + 64, :], t2[r + 64 : r + 128, :]], axis=1))
    sb = total[5]
    sb = sb[0:4] + sb[4:8] + sb[8:12]
    sb = jnp.where(odd_y == 1, sb[:, 128:256], sb[:, 0:128])
    parity = lax.rem(iota((4, 64), 0) + gz, 2)
    sb = jnp.where(parity == 1, sb[:, 64:128], sb[:, 0:64])
    topv = top[0]
    top4 = jnp.concatenate(
        [topv[:, 0:64], topv[:, 64:128], topv[:, 128:192], jnp.zeros((1, 64), F32)], axis=0
    )
    local_b = ordered(jnp.concatenate([top4 + 0.25 * sb, jnp.zeros((12, 64), F32)], axis=0))
    for xa in range(2):
        down = jnp.dot(local_b, v_of[xa], preferred_element_type=F32)[0:4]
        local_a = 0.5 * total[4][xa * 8 : xa * 8 + 4] + down
        for ya in range(2):
            for p in range(2):
                b = ya * 128 + p * 64
                pa[pl.ds(xa * 16 + ya * 8 + p, 4, stride=2), 0:64] = local_a[:, b : b + 64]
    for xa in range(2):
        parent = ordered(pa[xa * 16 : xa * 16 + 16, 0:64])
        for px in range(2):
            x = 2 * xa + px
            leaf = total[x] + jnp.dot(parent, v_of[px], preferred_element_type=F32)
            lr[x * 32 : x * 32 + 16, :] = leaf[:, 0:128]
            lr[x * 32 + 16 : x * 32 + 32, :] = leaf[:, 128:256]
    for x in range(4):
        for y in range(4):
            for zp in range(6):
                r = x * 32 + (y % 2) * 16 + (y // 2) * 8 + zp
                ln[x * 4 + y : x * 4 + y + 1, zp * 128 : zp * 128 + 128] = lr[r : r + 1, :]

    coef = jnp.concatenate([ln[:, zp * 128 : zp * 128 + 128] for zp in range(6)], axis=0)
    high, low = pieces(coef, 2)
    coef = jnp.concatenate([high.astype(BF16), low.astype(BF16)], axis=1)
    cheb = []
    for d in range(3):
        u = 2.0 * jnp.concatenate(
            [pos[d, x, :, zp * 128 : zp * 128 + 128] for zp in range(6) for x in range(4)], axis=0
        ) - 1.0
        second = 2.0 * u * u - 1.0
        cheb.append([None, u, second, 2.0 * u * second - u])
    out = None
    for a in range(4):
        spread = jnp.dot(
            coef, to_lanes[:, a * 2048 : a * 2048 + 2048], preferred_element_type=F32
        )
        sum_b = None
        for b in range(4):
            sum_c = None
            for c in range(4):
                term = spread[:, (4 * b + c) * 128 : (4 * b + c) * 128 + 128]
                if c:
                    term = term * cheb[2][c]
                sum_c = term if sum_c is None else sum_c + term
            if b:
                sum_c = sum_c * cheb[1][b]
            sum_b = sum_c if sum_b is None else sum_b + sum_c
        if a:
            sum_b = sum_b * cheb[0][a]
        out = sum_b if out is None else out + sum_b
    for zp in range(6):
        lanes = slice(zp * 128, zp * 128 + 128)
        value = out[zp * 16 : zp * 16 + 16] * 0.125 + near[:, lanes]
        for x in range(4):
            limit, slot = count_lanes(cnt[x], zp)
            pot_out[x, :, lanes] = jnp.where(slot < limit, value[x * 4 : x * 4 + 4], 0.0)
            loc_out[x, :, lanes] = ln[x * 4 : x * 4 + 4, lanes]


def lane_spread(to_lanes):
    row, col = iota((128, 128), 0), iota((128, 128), 1)

    def one(c, carry):
        block = jnp.where(row == (col & 64) + c, 1.0, 0.0).astype(BF16)
        lanes = pl.ds(pl.multiple_of(c * 128, 128), 128)
        to_lanes[0:128, lanes] = block
        to_lanes[128:256, lanes] = block
        return carry

    lax.fori_loop(0, 64, one, 0)


def whole_kernel(
    pos_in, chg_in, soft_in, cnt_in, top_in, bm_in, am_in, lm_in, m2l_in, l2l_in,
    pot_out, loc_out,
    t2, near, pos, cnt, top, lw, la, lb, lr, pa, ln, to_lanes,
    pf, ml, ma, mb, zs, zr, ps, mls, mas, ms, zf, mt, s2,
    chg, soft, bm, am, lm, l2l,
    a_own, q_own, a_side, q_side, a_edge, q_edge, b_mat, ft, fs, wt, near8,
    send, recv, local,
):
    gx, gy, gz = (lax.axis_index(a) for a in AXES)

    def at(ox, oy, oz):
        return (
            lax.rem(gx + (ox + 8), 8),
            lax.rem(gy + (oy + 8), 8),
            lax.rem(gz + (oz + 8), 8),
        )

    fetched = [(lm_in, lm), (am_in, am), (bm_in, bm), (pos_in, pos), (cnt_in, cnt)]
    fetched += [(chg_in, chg), (soft_in, soft), (l2l_in, l2l), (top_in, top), (m2l_in, mt)]
    fetched = [
        pltpu.make_async_copy(src, dst, local.at[i]) for i, (src, dst) in enumerate(fetched)
    ]
    for copy in fetched:
        copy.start()
    barrier = pltpu.get_barrier_semaphore()
    around = [at(0, 0, 1), at(0, 0, -1)]
    for o in (1, -1, 2, -2, 3, -3):
        around += [at(o, 0, 0), at(0, o, 0)]
    for who in around:
        pl.semaphore_signal(barrier, inc=1, device_id=who, device_id_type=MESH)

    number = [0]

    def remote(src, dst, who):
        i = number[0]
        number[0] += 1
        copy = pltpu.make_async_remote_copy(
            src_ref=src, dst_ref=dst, send_sem=send.at[i], recv_sem=recv.at[i],
            device_id=who, device_id_type=MESH,
        )
        copy.start()
        return copy

    for copy in fetched[:3]:
        copy.wait()
    for x in range(4):
        block = lm[x].astype(F32)
        for zp in range(6):
            ms[zp * 16 + x * 4 : zp * 16 + x * 4 + 4, :] = block[:, zp * 128 : zp * 128 + 128]
    for x in range(2):
        block = am[x].astype(F32)
        for zp in range(3):
            ms[96 + zp * 4 + x * 2 : 98 + zp * 4 + x * 2, :] = block[:, zp * 128 : zp * 128 + 128]
    bcells = bm[0].astype(F32)
    ms[108:109, :] = bcells[:, 0:128]
    ms[109:110, :] = jnp.concatenate([bcells[:, 64:128], bcells[:, 128:192]], axis=1)
    ms[110:112, :] = jnp.zeros((2, 128), F32)
    row, col = iota((128, 128), 0), iota((128, 128), 1)
    moved = (row & 64) + ((row & 1) << 5) + ((row & 63) >> 1)
    order = jnp.where(moved == col, 1.0, 0.0).astype(BF16)
    ms[...] = jnp.dot(ms[...].astype(BF16), order, preferred_element_type=F32)

    for copy in fetched[3:7]:
        copy.wait()
    own = []
    for x in range(4):
        own.append([pos[0, x] - 0.5, pos[1, x] - 0.5, pos[2, x] - 0.5, chg[x], soft[x]])

    def own_piece(x, f, zp):
        piece = own[x][f][:, zp * 128 : zp * 128 + 128]
        if f == 3:
            limit, slot = count_lanes(cnt[x], zp)
            piece = jnp.where(slot < limit, piece, 0.0)
        return piece

    zf[...] = jnp.zeros_like(zf)
    for side, (lp, ap) in enumerate(((0, 0), (5, 2))):
        base = side * 112
        for x in range(4):
            for f in range(5):
                zf[base + f * 16 + x * 4 : base + f * 16 + x * 4 + 4, :] = own_piece(x, f, lp)
        zf[base + 80 : base + 96, :] = ms[lp * 16 : lp * 16 + 16, :]
        zf[base + 96 : base + 100, :] = ms[96 + ap * 4 : 100 + ap * 4, :]
        zf[base + 100 : base + 102, :] = ms[108:110, :]
        zs[side] = zf[base : base + 112, :].astype(BF16)
    pl.semaphore_wait(barrier, 14)

    z_copies = [
        remote(zs.at[0], zr.at[1], at(0, 0, -1)),
        remote(zs.at[1], zr.at[0], at(0, 0, 1)),
    ]
    ps[...] = jnp.zeros_like(ps)
    mas[...] = jnp.zeros_like(mas)
    for x in range(4):
        for zp in range(6):
            for f in range(5):
                ps[pl.ds(x * 224 + f * 8 + 1 + zp, 4, stride=56), :] = own_piece(x, f, zp)
    for zp in range(6):
        for x in range(4):
            mls[pl.ds(x * 32 + zp + 1, 4, stride=8), :] = ms[
                zp * 16 + x * 4 : zp * 16 + x * 4 + 4, :
            ]
    for zp in range(3):
        for x in range(2):
            mas[pl.ds(x * 16 + zp + 1, 2, stride=8), :] = ms[
                96 + zp * 4 + x * 2 : 98 + zp * 4 + x * 2, :
            ]

    near8[...] = jnp.zeros_like(near8)
    b_mat[...] = jnp.zeros_like(b_mat)
    wt[...] = jnp.zeros_like(wt)
    target_features(pos, soft, fs, ft)
    lane_spread(to_lanes)

    for copy in fetched[7:]:
        copy.wait()

    def unpack(i, carry):
        block = mt[pl.ds(pl.multiple_of(i * 16, 16), 16), :].astype(F32)
        unpack_rows(block, i * 16, s2, 16)
        return carry

    lax.fori_loop(0, 21, unpack, 0)
    unpack_rows(mt[336:343, :].astype(F32), 336, s2, 7)
    unpack_rows(l2l[...].astype(F32), 343, s2, 8)

    for copy in z_copies:
        copy.wait()
    keep_low = jnp.where(gz > 0, 1.0, 0.0).astype(F32)
    keep_high = jnp.where(gz < 7, 1.0, 0.0).astype(F32)
    b_rows = []
    for side, (keep, zp_l, zp_a) in enumerate(((keep_low, 0, 0), (keep_high, 7, 4))):
        got = zr[side].astype(F32) * keep
        for x in range(4):
            for f in range(5):
                ps[pl.ds(x * 224 + f * 8 + zp_l, 4, stride=56), :] = got[
                    f * 16 + x * 4 : f * 16 + x * 4 + 4, :
                ]
            mls[pl.ds(x * 32 + zp_l, 4, stride=8), :] = got[80 + x * 4 : 84 + x * 4, :]
        for x in range(2):
            mas[pl.ds(x * 16 + zp_a, 2, stride=8), :] = got[96 + x * 2 : 98 + x * 2, :]
        b_rows.append((got[100:101, :], got[101:102, :]))
    (left_a, left_b), (ra, rb) = b_rows
    oa, ob = ms[108:109, :], ms[109:110, :]
    low1 = iota((1, 128), 1) < 64
    middle = jnp.where(low1, pltpu.roll(left_b, 64, 1), pltpu.roll(oa, 64, 1))
    middle_r = jnp.where(low1, pltpu.roll(ob, 64, 1), pltpu.roll(ra, 64, 1))
    pairs = [left_a, left_b, middle, oa, ob, middle_r, ra, rb]
    even_z = lax.rem(gz, 2) == 0
    zf[0:16, :] = jnp.zeros((16, 128), F32)
    for l in range(3):
        at_even = l + 1 - l % 2
        at_odd = l + 1 - (l + 1) % 2
        for j in range(3):
            zf[4 * j + l : 4 * j + l + 1, :] = jnp.where(
                even_z, pairs[at_even + 2 * j], pairs[at_odd + 2 * j]
            )
    mb[3, 3] = zf[0:16, :].astype(BF16)
    x_b = []
    for o in (1, -1, 2, -2, 3, -3):
        x_b.append(remote(mb.at[3, 3], mb.at[3 - o, 3], at(o, 0, 0)))
    for x in range(4):
        for y in range(4):
            for t in range(3):
                r = (x * 4 + y) * 56 + t * 16
                pf[1 + x, 1 + y, t] = ps[r : r + 16, :].astype(BF16)
        for yp in range(2):
            r = x * 32 + yp * 16
            ml[2 + x, 1 + yp] = mls[r : r + 16, :].astype(BF16)
    for x in range(2):
        ma[2 + x, 1] = mas[x * 16 : x * 16 + 16, :].astype(BF16)

    own_x, own_xl, own_xa = pl.ds(1, 4), pl.ds(2, 4), pl.ds(2, 2)
    up, down = at(0, 1, 0), at(0, -1, 0)
    y_copies = [
        remote(pf.at[own_x, pl.ds(4, 1)], pf.at[own_x, pl.ds(0, 1)], up),
        remote(pf.at[own_x, pl.ds(1, 1)], pf.at[own_x, pl.ds(5, 1)], down),
        remote(ml.at[own_xl, pl.ds(2, 1)], ml.at[own_xl, pl.ds(0, 1)], up),
        remote(ml.at[own_xl, pl.ds(1, 1)], ml.at[own_xl, pl.ds(3, 1)], down),
        remote(ma.at[own_xa, pl.ds(1, 1)], ma.at[own_xa, pl.ds(0, 1)], up),
        remote(ma.at[own_xa, pl.ds(1, 1)], ma.at[own_xa, pl.ds(2, 1)], down),
    ]

    low_lanes = iota((32, 128), 1) < 64

    def pair_up(g, carry):
        near = (jnp.abs(g // 7 - 3) <= 1) & (jnp.abs(lax.rem(g, 7) - 3) <= 1)
        kept = jnp.where(near, 0.0, 1.0).astype(F32)
        tables = []
        for i in range(7):
            one = s2[pl.ds(pl.multiple_of((g * 7 + i) * 40, 8), 32), :]
            if 2 <= i <= 4:
                one = one * kept
            tables.append((one, pltpu.roll(one, 64, 1)))
        for w in range(6):
            (first, turned_first), (second, turned_second) = tables[w + 1], tables[w]
            to = g * 384 + w * 64
            t2[pl.ds(pl.multiple_of(to, 32), 32), :] = jnp.where(
                low_lanes, first, turned_second
            ).astype(BF16)
            t2[pl.ds(pl.multiple_of(to + 32, 32), 32), :] = jnp.where(
                low_lanes, turned_first, second
            ).astype(BF16)
        return carry

    def own_columns(i, carry):
        where = [(i, cy, a_own, q_own, (i - 1) * 4 + cy - 1) for cy in range(1, 5)]
        source_columns(where, gx, gy, pf, wt)
        return carry

    def pair_some(i):
        for u in range(6):
            pair_up(jnp.minimum(i * 6 + u, 48), 0)

    def own_pairs(t, carry):
        own_slab(t, a_own, q_own, b_mat, ft, near8)
        pair_some(t - 1)
        return carry

    lax.fori_loop(1, 5, own_columns, 0)
    lax.fori_loop(1, 5, own_pairs, 0)
    for copy in x_b:
        copy.wait()
    y_b = []
    for o in (1, -1, 2, -2, 3, -3):
        y_b.append(remote(mb.at[:, pl.ds(3, 1)], mb.at[:, pl.ds(3 - o, 1)], at(0, o, 0)))
    for copy in y_copies:
        copy.wait()

    up, down = at(1, 0, 0), at(-1, 0, 0)
    x_copies = [
        remote(pf.at[pl.ds(4, 1)], pf.at[pl.ds(0, 1)], up),
        remote(pf.at[pl.ds(1, 1)], pf.at[pl.ds(5, 1)], down),
        remote(ml.at[pl.ds(4, 2)], ml.at[pl.ds(0, 2)], up),
        remote(ml.at[pl.ds(2, 2)], ml.at[pl.ds(6, 2)], down),
        remote(ma.at[pl.ds(2, 2)], ma.at[pl.ds(0, 2)], up),
        remote(ma.at[pl.ds(2, 2)], ma.at[pl.ds(4, 2)], down),
    ]
    def own_pairs_y(t, carry):
        cx = t - 4
        where = [(cx, 0, a_edge, q_edge, cx), (cx, 5, a_edge, q_edge, cx + 6)]
        source_columns(where, gx, gy, pf, wt)
        own_slab(t, a_own, q_own, b_mat, ft, near8)
        pair_some(t - 1)
        return carry

    lax.fori_loop(5, 9, own_pairs_y, 0)
    pair_up(48, 0)
    for child in range(4):
        r = (343 + 2 * child) * 40
        even, odd = pair_rows(s2[r : r + 32, :], s2[r + 40 : r + 40 + 32, :], low_lanes)
        to = 49 * 384 + child * 64
        t2[to : to + 32, :] = even
        t2[to + 32 : to + 64, :] = odd
    for copy in x_copies + y_b:
        copy.wait()

    def own_pairs_x(i, carry):
        cx = i * 5
        where = [(cx, 0, a_edge, q_edge, cx), (cx, 5, a_edge, q_edge, cx + 6)]
        where += [(cx, cy, a_side, q_side, i * 4 + cy - 1) for cy in range(1, 5)]
        source_columns(where, gx, gy, pf, wt)
        own_slab(i + 9, a_own, q_own, b_mat, ft, near8)
        edge_pairs(i + 1, a_edge, q_edge, b_mat, ft, near8)
        return carry

    def last_pairs(i, carry):
        slab_pairs(i * 3, None, a_side, q_side, i * 4, b_mat, ft, near8)
        edge_pairs(i * 3, a_edge, q_edge, b_mat, ft, near8)
        return carry

    lax.fori_loop(0, 2, own_pairs_x, 0)
    lax.fori_loop(0, 2, last_pairs, 0)
    gather_near(near8, near)
    far_kernel(
        gx, gy, gz, ml, ma, mb, t2, near, pos, cnt, top, pot_out, loc_out,
        lw, la, lb, lr, pa, ln, to_lanes,
    )


NEAR_SCRATCH = [
    ((1024, 256), BF16),
    ((1024, 1664), BF16),
    ((512, 256), BF16),
    ((512, 1664), BF16),
    ((768, 256), BF16),
    ((768, 1664), BF16),
    ((6, 9, 256, 256), BF16),
    ((16, 3, 2, 16, 768), BF16),
    ((6, 96, 128), F32),
    ((6, 208, 128), F32),
    ((16, 2, 8, 768), F32),
]


FAR_SCRATCH = [
    ((8, 6, 16, 384), BF16),
    ((7, 6, 16, 384), BF16),
    ((7, 6, 16, 384), BF16),
    ((128, 128), F32),
    ((32, 128), F32),
    ((16, 768), F32),
    ((256, 8192), BF16),
]


def run(*args):
    halos = [(6, 6, 3, 16, 128), (8, 4, 16, 128), (6, 3, 16, 128), (7, 7, 16, 128)]
    scratch = [((T2_ROWS, 128), BF16), ((16, 768), F32), ((3, 4, 4, 768), F32)]
    scratch += [((4, 4, 12), jnp.int32), ((1, 1, 192), F32)] + FAR_SCRATCH
    scratch += [(s, BF16) for s in halos]
    scratch += [((2, 112, 128), BF16), ((2, 112, 128), BF16), ((896, 128), F32), ((128, 128), F32)]
    scratch += [((32, 128), F32), ((112, 128), F32), ((224, 128), F32), ((343, 4096), BF16)]
    scratch += [((352 * 40, 128), F32), ((4, 4, 768), F32), ((4, 4, 768), F32)]
    scratch += [((1, 1, 192), BF16), ((2, 2, 384), BF16), ((4, 4, 768), BF16), ((8, 4096), BF16)]
    return pl.pallas_call(
        whole_kernel,
        name="downward",
        out_shape=[jax.ShapeDtypeStruct((4, 4, 768), F32)] * 2,
        in_specs=[pl.BlockSpec(memory_space=pltpu.HBM)] * 10,
        out_specs=[pl.BlockSpec(memory_space=pltpu.VMEM)] * 2,
        scratch_shapes=[pltpu.VMEM(s, t) for s, t in scratch + NEAR_SCRATCH]
        + [
            pltpu.SemaphoreType.DMA((26,)),
            pltpu.SemaphoreType.DMA((26,)),
            pltpu.SemaphoreType.DMA((10,)),
        ],
        compiler_params=pltpu.CompilerParams(
            collective_id=0, has_side_effects=True, vmem_limit_bytes=VMEM_BYTES
        ),
        cost_estimate=pl.CostEstimate(
            flops=10**10, bytes_accessed=10**7, transcendentals=2 * 10**7
        ),
    )(*args)


def hand_over_kernel(pot_in, loc_in, pot_out, loc_out, held, sems):
    arrays = ((pot_in, pot_out), (loc_in, loc_out))
    blocks = [(n, x) for n in range(2) for x in range(4)]
    came, left = [], []
    for n, x in blocks:
        i = n * 4 + x
        came.append(pltpu.make_async_copy(arrays[n][0].at[x], held.at[n, x], sems.at[0, i]))
        left.append(pltpu.make_async_copy(held.at[n, x], arrays[n][1].at[x], sems.at[1, i]))
    for copy in came:
        copy.start()
    for first, second in zip(came, left):
        first.wait()
        second.start()
    for copy in left:
        copy.wait()


def hand_over(*results):
    hbm = pl.BlockSpec(memory_space=pltpu.HBM)
    return pl.pallas_call(
        hand_over_kernel,
        name="hand_over",
        out_shape=[jax.ShapeDtypeStruct((4, 4, 768), F32)] * 2,
        in_specs=[hbm] * 2,
        out_specs=[hbm] * 2,
        scratch_shapes=[pltpu.VMEM((2, 4, 4, 768), F32), pltpu.SemaphoreType.DMA((2, 8))],
        compiler_params=pltpu.CompilerParams(vmem_limit_bytes=VMEM_BYTES),
    )(*results)


def per_device(pos, chg, soft, cnt, top, bm, am, lm, m2l, l2l):
    return tuple(hand_over(*run(pos, chg, soft, cnt, top, bm, am, lm, m2l, l2l)))


def solution(mesh):
    split = P("gx", "gy", "gz")
    in_specs = (P(None, "gx", "gy", "gz"),) + (split,) * 7 + (P(), P())
    return jax.shard_map(
        per_device, mesh=mesh, in_specs=in_specs, out_specs=(split, split), check_vma=False
    )
```

```python
import functools
import jax
import jax.numpy as jnp
from jax import lax
from jax.experimental import pallas as pl
from jax.experimental.pallas import tpu as pltpu
from jax.sharding import PartitionSpec as P

F32 = jnp.float32
BF16 = jnp.bfloat16
MESH = pl.DeviceIdType.MESH
AXES = ("gx", "gy", "gz")
T2_ROWS = 49 * 384 + 256
VMEM_BYTES = 63 * 2**20


def iota(shape, dim):
    return lax.broadcasted_iota(jnp.int32, shape, dim)


def count_lanes(counts, pair):
    rows = counts.shape[0]
    lane = iota((rows, 128), 1)
    low = counts[:, 2 * pair : 2 * pair + 1]
    high = counts[:, 2 * pair + 1 : 2 * pair + 2]
    return jnp.where(lane < 64, low, high), lane & 63


def unpack_rows(block, base, s2, rows):
    for c in range(32):
        s2[pl.ds(base * 40 + c, rows, stride=40), :] = block[:, c * 128 : (c + 1) * 128]


def pair_rows(first, second, low_lanes):
    turned_first = pltpu.roll(first, 64, 1)
    turned_second = pltpu.roll(second, 64, 1)
    even = jnp.where(low_lanes, first, turned_second)
    odd = jnp.where(low_lanes, turned_first, second)
    return even.astype(BF16), odd.astype(BF16)


def pieces(value, count):
    out = []
    for _ in range(count - 1):
        head = value.astype(BF16).astype(F32)
        out.append(head)
        value = value - head
    return out + [value]


def inside(coord, offset):
    return (coord + offset >= 0) & (coord + offset <= 7)


def source_columns(where, gx, gy, pf, wt, base=0):
    ones = jnp.ones((8, 128), F32)
    same = jnp.where(iota((128, 128), 0) == iota((128, 128), 1), 1.0, 0.0).astype(BF16)
    er, ec = iota((16, 1024), 0), iota((16, 1024), 1)
    spread = jnp.where(((er & 7) * 2 + (er >> 3)) == (ec >> 6), 1.0, 0.0).astype(BF16)
    charges = []
    for slot, (cx, cy, _, _, _) in enumerate(where):
        slot = slot + base
        xy = pf[cx, cy, 0].astype(F32)
        zq = pf[cx, cy, 1].astype(F32)
        s = pf[cx, cy, 2].astype(F32)[0:8]
        x, y, z, q = xy[0:8], xy[8:16], zq[0:8], zq[8:16]
        over_x = jnp.where(cx == 0, -1, jnp.where(cx == 5, 1, 0))
        over_y = jnp.where(cy == 0, -1, jnp.where(cy == 5, 1, 0))
        q = q * jnp.where(inside(gx, over_x) & inside(gy, over_y), 1.0, 0.0).astype(F32)
        ix = ones * (jnp.asarray(cx, F32) - 2.5)
        iy = ones * (jnp.asarray(cy, F32) - 2.5)
        n = (x + ix) * (x + ix) + (y + iy) * (y + iy) + z * z + 0.5 * (s * s)
        feats = [x, x, ix, ix, y, y, iy, iy, z, z, ones, ones, ones] + pieces(n, 3)
        for f in range(16):
            wt[slot, pl.ds(f, 8, stride=24), :] = feats[f]
        wt[slot, 192:200, :] = q
    for slot, (_, _, a_mat, q_mat, at) in enumerate(where):
        tile = [wt[slot + base, zp * 24 : zp * 24 + 16, :] for zp in range(8)]
        tile = jnp.concatenate(tile + [wt[slot + base, 192:208, :]], axis=0)
        turned = lax.dot_general(
            same, tile.astype(BF16), (((1,), (1,)), ((), ())), preferred_element_type=F32
        )
        rows = pl.ds(pl.multiple_of(at * 64, 64), 64)
        a_mat[rows, 0:128] = turned[0:64, 0:128].astype(BF16)
        a_mat[rows, 128:256] = turned[64:128, 0:128].astype(BF16)
        charges.append(
            jnp.concatenate([turned[0:64, 128:136], turned[64:128, 128:136]], axis=1)
        )
    wide = jnp.dot(
        jnp.concatenate(charges, axis=0).astype(BF16), spread, preferred_element_type=F32
    )
    low = iota((64, 128), 1) < 64
    for slot, (_, _, a_mat, q_mat, at) in enumerate(where):
        rows = pl.ds(pl.multiple_of(at * 64, 64), 64)
        v = [wide[slot * 64 : slot * 64 + 64, m * 128 : m * 128 + 128] for m in range(8)]
        for m in range(6):
            q_mat[rows, m * 128 : m * 128 + 128] = v[m + 1].astype(BF16)
        for m in range(7):
            q_mat[rows, 768 + m * 128 : 896 + m * 128] = jnp.where(low, v[m + 1], v[m]).astype(BF16)


def target_features(pos, soft, fs, ft):
    lane = iota((64, 128), 1)

    def put(f, v):
        for zp in range(6):
            fs[zp, pl.ds(f, 4, stride=24), :] = v[:, zp * 128 : zp * 128 + 128]

    for x in range(4):
        px, py, pz = (pos[d, x] - 0.5 for d in range(3))
        s = soft[x]
        fx = px + (x - 1.5)
        fy = py + (iota((4, 768), 0).astype(F32) - 1.5)
        ax, bx = pieces(fx, 2)
        ay, by = pieces(fy, 2)
        bx, by = bx.astype(BF16).astype(F32), by.astype(BF16).astype(F32)
        xx, yy = ax + bx, ay + by
        base = xx * xx + yy * yy + 0.5 * (s * s)
        for f, v in ((0, ax), (1, bx), (2, ax), (3, bx), (4, ay), (5, by), (6, ay), (7, by)):
            put(f, -2.0 * v)
        for f in (13, 14, 15):
            put(f, jnp.ones((4, 768), F32))
        for d in range(3):
            az, bz = pieces(pz - (d - 1.0), 2)
            bz = bz.astype(BF16).astype(F32)
            zz = az + bz
            n = base + zz * zz
            for f, v in zip((8, 9, 10, 11, 12), [-2.0 * az, -2.0 * bz] + pieces(n, 3)):
                put(f, v)
            for zp in range(6):
                made = jnp.concatenate(
                    [fs[zp, y * 24 : y * 24 + 16, :] for y in range(4)], axis=0
                )
                if d != 1:
                    made = pltpu.roll(made, 64, 1)
                for e in range(2):
                    mine = lane < 64 if (e == 0) == (d == 1) else lane >= 64
                    half = jnp.where(mine, made, 0.0).astype(BF16)
                    for y in range(4):
                        ft[x * 4 + y, d, e, :, zp * 128 : zp * 128 + 128] = half[
                            y * 16 : y * 16 + 16
                        ]


Q_AT = (768, 0, 896)


def set_weights(b_mat, slot, ft, g):
    for k in range(3):
        for d in range(3):
            for h in range(2):
                for e in range(2):
                    cell = 4 * k + 2 + 2 * h + e + d - 1
                    r = (cell % 2) * 128 + (cell // 2) * 16
                    b_mat[slot, k * 3 + d, r : r + 16, h * 128 : h * 128 + 128] = ft[
                        g, d, e, :, (2 * k + h) * 128 : (2 * k + h) * 128 + 128
                    ]


def add_pairs(left, q_of, b_mat, slot, near8, g, own=None):
    rows = left.shape[0]
    for k in range(3):
        lanes = slice(256 * k, 256 * k + 256)
        for d in range(3):
            r2 = jnp.dot(left, b_mat[slot, k * 3 + d], preferred_element_type=F32)
            q = q_of(Q_AT[d] + 256 * k).astype(F32)
            if d == 1 and own is not None:
                q = q * own
            part = jnp.sum((lax.rsqrt(r2) * q).reshape(rows // 8, 8, 256), axis=0)
            if d == 0:
                swapped = part
            elif d == 1:
                plain = part
            else:
                swapped = swapped + part
        near8[g, 0, :, lanes] += plain
        near8[g, 1, :, lanes] += swapped


def slab_pairs(x, itself, a_mat, q_mat, at, b_mat, ft, near8):
    one = jnp.ones((64, 256), F32)
    for y in range(4):
        low, high = max(0, y - 1), min(3, y + 1)
        set_weights(b_mat, y, ft, x * 4 + y)
        rows = pl.ds(pl.multiple_of((at + low) * 64, 64), (high - low + 1) * 64)
        own = None
        if itself is not None:
            own = jnp.concatenate(
                [itself if cy == y else one for cy in range(low, high + 1)], axis=0
            )
        add_pairs(
            a_mat[rows, :], lambda at: q_mat[rows, at : at + 256], b_mat, y, near8, x * 4 + y, own
        )


def own_slab(t, a_own, q_own, b_mat, ft, near8):
    x, dx = t // 3, lax.rem(t, 3)
    itself = jnp.where(iota((64, 256), 0) == (iota((64, 256), 1) & 63), 0.0, 1.0).astype(F32)
    itself = jnp.where(dx == 1, itself, 1.0)
    slab_pairs(x, itself, a_own, q_own, (x + dx - 1) * 4, b_mat, ft, near8)


def edge_pairs(x, a_edge, q_edge, b_mat, ft, near8):
    for side, y in enumerate((0, 3)):
        set_weights(b_mat, 4 + side, ft, x * 4 + y)
        rows = pl.ds(pl.multiple_of((side * 6 + x) * 64, 64), 192)
        add_pairs(
            a_edge[rows, :], lambda at: q_edge[rows, at : at + 256], b_mat, 4 + side, near8, x * 4 + y
        )


def gather_near(near8, near):
    for g in range(16):
        for zp in range(6):
            lanes = slice(zp * 128, zp * 128 + 128)
            both = near8[g, 0, :, lanes] + pltpu.roll(near8[g, 1, :, lanes], 64, 1)
            near[g : g + 1, lanes] = jnp.sum(both, axis=0, keepdims=True)


def far_kernel(
    gx, gy, gz,
    ml, ma, mb, t2, near, pos, cnt, top,
    pot_out, loc_out,
    lw, la, lb, lr, pa, ln, to_lanes,
):
    def shifted(v):
        return [v, pltpu.roll(v, 7, 0), pltpu.roll(v, 6, 0)]

    for xs in range(8):
        over_x = -1 if xs < 2 else (1 if xs >= 6 else 0)
        turned = []
        for yp in range(4):
            over_y = -1 if yp < 1 else (1 if yp >= 3 else 0)
            keep = jnp.where(inside(gx, over_x) & inside(gy, over_y), 1.0, 0.0).astype(F32)
            tile = ml[xs, yp].astype(F32) * keep
            turned.append((shifted(tile[0:8]), shifted(tile[8:16])))
        for w in range(6):
            for j in range(3):
                lw[xs, w, :, j * 128 : j * 128 + 128] = jnp.concatenate(
                    [turned[w // 2][w % 2][j], turned[w // 2 + 1][w % 2][j]], axis=0
                ).astype(BF16)
    zero8 = jnp.zeros((8, 128), F32)
    a_tiles = {}
    for xs in range(6):
        over_x = -1 if xs < 2 else (1 if xs >= 4 else 0)
        for yp in range(3):
            over_y = yp - 1
            keep = jnp.where(inside(gx, over_x) & inside(gy, over_y), 1.0, 0.0).astype(F32)
            tile = ma[xs, yp].astype(F32) * keep
            a_tiles[xs, yp] = (shifted(tile[0:8]), shifted(tile[8:16]))
    for dx in range(7):
        for w in range(6):
            for j in range(3):
                first = a_tiles[dx - 1, w // 2][w % 2][j] if dx >= 1 else zero8
                second = a_tiles[dx, w // 2][w % 2][j] if dx <= 5 else zero8
                la[dx, w, :, j * 128 : j * 128 + 128] = jnp.concatenate(
                    [first, second], axis=0
                ).astype(BF16)
    row16 = iota((16, 128), 0)
    odd_x, odd_y = lax.rem(gx, 2), lax.rem(gy, 2)
    for dx in range(7):
        ok_x = inside(gx, dx - 3)
        if dx == 0:
            ok_x = ok_x & (odd_x == 1)
        if dx == 6:
            ok_x = ok_x & (odd_x == 0)
        for w in range(6):
            dy = w + 1 - odd_y
            keep = jnp.where(ok_x & inside(gy, dy - 3), 1.0, 0.0).astype(F32)
            tile = mb[dx, dy].astype(F32) * keep
            for j in range(3):
                lb[dx, w, :, j * 128 : j * 128 + 128] = jnp.where(
                    (row16 >> 2) == j, tile, 0.0
                ).astype(BF16)

    total = [jnp.zeros((16, 256), F32) for _ in range(6)]
    for dx in range(7):
        xs_of = [x for x in range(4) if not (dx == 0 and x % 2 == 0) and not (dx == 6 and x % 2 == 1)]
        for w in range(6):
            g = dx * 7 + w + 1
            weights = jnp.concatenate(
                [t2[g * 384 : (g + 1) * 384, :], t2[(g - 1) * 384 : g * 384, :]], axis=1
            )
            left = [lw[x + dx - 1, w] for x in xs_of] + [la[dx, w], lb[dx, w]]
            made = jnp.dot(
                jnp.concatenate(left, axis=0), weights, preferred_element_type=F32
            )
            for i, slot in enumerate(xs_of + [4, 5]):
                total[slot] = total[slot] + made[i * 16 : i * 16 + 16]

    row, col = iota((64, 64), 0), iota((64, 64), 1)
    order = jnp.where(((row & 1) << 5) + (row >> 1) == col, 1.0, 0.0).astype(BF16)

    def ordered(v):
        return jnp.dot(v.astype(BF16), order, preferred_element_type=F32).astype(BF16)

    v_of = []
    for px in range(2):
        r = 49 * 384 + px * 128
        v_of.append(jnp.concatenate([t2[r : r + 64, :], t2[r + 64 : r + 128, :]], axis=1))
    sb = total[5]
    sb = sb[0:4] + sb[4:8] + sb[8:12]
    sb = jnp.where(odd_y == 1, sb[:, 128:256], sb[:, 0:128])
    parity = lax.rem(iota((4, 64), 0) + gz, 2)
    sb = jnp.where(parity == 1, sb[:, 64:128], sb[:, 0:64])
    topv = top[0]
    top4 = jnp.concatenate(
        [topv[:, 0:64], topv[:, 64:128], topv[:, 128:192], jnp.zeros((1, 64), F32)], axis=0
    )
    local_b = ordered(jnp.concatenate([top4 + 0.25 * sb, jnp.zeros((12, 64), F32)], axis=0))
    for xa in range(2):
        down = jnp.dot(local_b, v_of[xa], preferred_element_type=F32)[0:4]
        local_a = 0.5 * total[4][xa * 8 : xa * 8 + 4] + down
        for ya in range(2):
            for p in range(2):
                b = ya * 128 + p * 64
                pa[pl.ds(xa * 16 + ya * 8 + p, 4, stride=2), 0:64] = local_a[:, b : b + 64]
    for xa in range(2):
        parent = ordered(pa[xa * 16 : xa * 16 + 16, 0:64])
        for px in range(2):
            x = 2 * xa + px
            leaf = total[x] + jnp.dot(parent, v_of[px], preferred_element_type=F32)
            lr[x * 32 : x * 32 + 16, :] = leaf[:, 0:128]
            lr[x * 32 + 16 : x * 32 + 32, :] = leaf[:, 128:256]
    for x in range(4):
        for y in range(4):
            for zp in range(6):
                r = x * 32 + (y % 2) * 16 + (y // 2) * 8 + zp
                ln[x * 4 + y : x * 4 + y + 1, zp * 128 : zp * 128 + 128] = lr[r : r + 1, :]

    coef = jnp.concatenate([ln[:, zp * 128 : zp * 128 + 128] for zp in range(6)], axis=0)
    high, low = pieces(coef, 2)
    coef = jnp.concatenate([high.astype(BF16), low.astype(BF16)], axis=1)
    cheb = []
    for d in range(3):
        u = 2.0 * jnp.concatenate(
            [pos[d, x, :, zp * 128 : zp * 128 + 128] for zp in range(6) for x in range(4)], axis=0
        ) - 1.0
        second = 2.0 * u * u - 1.0
        cheb.append([None, u, second, 2.0 * u * second - u])
    out = None
    for a in range(4):
        spread = jnp.dot(
            coef, to_lanes[:, a * 2048 : a * 2048 + 2048], preferred_element_type=F32
        )
        sum_b = None
        for b in range(4):
            sum_c = None
            for c in range(4):
                term = spread[:, (4 * b + c) * 128 : (4 * b + c) * 128 + 128]
                if c:
                    term = term * cheb[2][c]
                sum_c = term if sum_c is None else sum_c + term
            if b:
                sum_c = sum_c * cheb[1][b]
            sum_b = sum_c if sum_b is None else sum_b + sum_c
        if a:
            sum_b = sum_b * cheb[0][a]
        out = sum_b if out is None else out + sum_b
    for zp in range(6):
        lanes = slice(zp * 128, zp * 128 + 128)
        value = out[zp * 16 : zp * 16 + 16] * 0.125 + near[:, lanes]
        for x in range(4):
            limit, slot = count_lanes(cnt[x], zp)
            pot_out[x, :, lanes] = jnp.where(slot < limit, value[x * 4 : x * 4 + 4], 0.0)
            loc_out[x, :, lanes] = ln[x * 4 : x * 4 + 4, lanes]


def lane_spread(to_lanes):
    row, col = iota((128, 128), 0), iota((128, 128), 1)

    def one(c, carry):
        block = jnp.where(row == (col & 64) + c, 1.0, 0.0).astype(BF16)
        lanes = pl.ds(pl.multiple_of(c * 128, 128), 128)
        to_lanes[0:128, lanes] = block
        to_lanes[128:256, lanes] = block
        return carry

    lax.fori_loop(0, 64, one, 0, unroll=4)


def whole_kernel(
    pos_in, chg_in, soft_in, cnt_in, top_in, bm_in, am_in, lm_in, m2l_in, l2l_in,
    pot_out, loc_out,
    t2, near, pos, cnt, top, lw, la, lb, lr, pa, ln, to_lanes,
    pf, ml, ma, mb, zs, zr, ps, mls, mas, ms, zf, mt, s2,
    chg, soft, bm, am, lm, l2l,
    a_own, q_own, a_side, q_side, a_edge, q_edge, b_mat, ft, fs, wt, near8,
    send, recv, local,
):
    gx, gy, gz = (lax.axis_index(a) for a in AXES)

    def at(ox, oy, oz):
        return (
            lax.rem(gx + (ox + 8), 8),
            lax.rem(gy + (oy + 8), 8),
            lax.rem(gz + (oz + 8), 8),
        )

    fetched = [(lm_in, lm), (am_in, am), (bm_in, bm), (pos_in, pos), (cnt_in, cnt)]
    fetched += [(chg_in, chg), (soft_in, soft), (l2l_in, l2l), (top_in, top), (m2l_in, mt)]
    fetched = [
        pltpu.make_async_copy(src, dst, local.at[i]) for i, (src, dst) in enumerate(fetched)
    ]
    for copy in fetched:
        copy.start()
    barrier = pltpu.get_barrier_semaphore()
    around = [at(0, 0, 1), at(0, 0, -1)]
    for o in (1, -1, 2, -2, 3, -3):
        around += [at(o, 0, 0), at(0, o, 0)]
    for who in around:
        pl.semaphore_signal(barrier, inc=1, device_id=who, device_id_type=MESH)

    number = [0]

    def remote(src, dst, who):
        i = number[0]
        number[0] += 1
        copy = pltpu.make_async_remote_copy(
            src_ref=src, dst_ref=dst, send_sem=send.at[i], recv_sem=recv.at[i],
            device_id=who, device_id_type=MESH,
        )
        copy.start()
        return copy

    for copy in fetched[:3]:
        copy.wait()
    for x in range(4):
        block = lm[x].astype(F32)
        for zp in range(6):
            ms[zp * 16 + x * 4 : zp * 16 + x * 4 + 4, :] = block[:, zp * 128 : zp * 128 + 128]
    for x in range(2):
        block = am[x].astype(F32)
        for zp in range(3):
            ms[96 + zp * 4 + x * 2 : 98 + zp * 4 + x * 2, :] = block[:, zp * 128 : zp * 128 + 128]
    bcells = bm[0].astype(F32)
    ms[108:109, :] = bcells[:, 0:128]
    ms[109:110, :] = jnp.concatenate([bcells[:, 64:128], bcells[:, 128:192]], axis=1)
    ms[110:112, :] = jnp.zeros((2, 128), F32)
    row, col = iota((128, 128), 0), iota((128, 128), 1)
    moved = (row & 64) + ((row & 1) << 5) + ((row & 63) >> 1)
    order = jnp.where(moved == col, 1.0, 0.0).astype(BF16)
    ms[...] = jnp.dot(ms[...].astype(BF16), order, preferred_element_type=F32)

    for copy in fetched[3:7]:
        copy.wait()
    own = []
    for x in range(4):
        own.append([pos[0, x] - 0.5, pos[1, x] - 0.5, pos[2, x] - 0.5, chg[x], soft[x]])

    def own_piece(x, f, zp):
        piece = own[x][f][:, zp * 128 : zp * 128 + 128]
        if f == 3:
            limit, slot = count_lanes(cnt[x], zp)
            piece = jnp.where(slot < limit, piece, 0.0)
        return piece

    zf[...] = jnp.zeros_like(zf)
    for side, (lp, ap) in enumerate(((0, 0), (5, 2))):
        base = side * 112
        for x in range(4):
            for f in range(5):
                zf[base + f * 16 + x * 4 : base + f * 16 + x * 4 + 4, :] = own_piece(x, f, lp)
        zf[base + 80 : base + 96, :] = ms[lp * 16 : lp * 16 + 16, :]
        zf[base + 96 : base + 100, :] = ms[96 + ap * 4 : 100 + ap * 4, :]
        zf[base + 100 : base + 102, :] = ms[108:110, :]
        zs[side] = zf[base : base + 112, :].astype(BF16)
    pl.semaphore_wait(barrier, 14)

    z_copies = [
        remote(zs.at[0], zr.at[1], at(0, 0, -1)),
        remote(zs.at[1], zr.at[0], at(0, 0, 1)),
    ]
    ps[...] = jnp.zeros_like(ps)
    mas[...] = jnp.zeros_like(mas)
    for x in range(4):
        for zp in range(6):
            for f in range(5):
                ps[pl.ds(x * 224 + f * 8 + 1 + zp, 4, stride=56), :] = own_piece(x, f, zp)
    for zp in range(6):
        for x in range(4):
            mls[pl.ds(x * 32 + zp + 1, 4, stride=8), :] = ms[
                zp * 16 + x * 4 : zp * 16 + x * 4 + 4, :
            ]
    for zp in range(3):
        for x in range(2):
            mas[pl.ds(x * 16 + zp + 1, 2, stride=8), :] = ms[
                96 + zp * 4 + x * 2 : 98 + zp * 4 + x * 2, :
            ]

    near8[...] = jnp.zeros_like(near8)
    b_mat[...] = jnp.zeros_like(b_mat)
    wt[...] = jnp.zeros_like(wt)
    target_features(pos, soft, fs, ft)
    lane_spread(to_lanes)

    for copy in fetched[7:]:
        copy.wait()

    def unpack(i, carry):
        block = mt[pl.ds(pl.multiple_of(i * 16, 16), 16), :].astype(F32)
        unpack_rows(block, i * 16, s2, 16)
        return carry

    lax.fori_loop(0, 21, unpack, 0, unroll=3)
    unpack_rows(mt[336:343, :].astype(F32), 336, s2, 7)
    unpack_rows(l2l[...].astype(F32), 343, s2, 8)

    for copy in z_copies:
        copy.wait()
    keep_low = jnp.where(gz > 0, 1.0, 0.0).astype(F32)
    keep_high = jnp.where(gz < 7, 1.0, 0.0).astype(F32)
    b_rows = []
    for side, (keep, zp_l, zp_a) in enumerate(((keep_low, 0, 0), (keep_high, 7, 4))):
        got = zr[side].astype(F32) * keep
        for x in range(4):
            for f in range(5):
                ps[pl.ds(x * 224 + f * 8 + zp_l, 4, stride=56), :] = got[
                    f * 16 + x * 4 : f * 16 + x * 4 + 4, :
                ]
            mls[pl.ds(x * 32 + zp_l, 4, stride=8), :] = got[80 + x * 4 : 84 + x * 4, :]
        for x in range(2):
            mas[pl.ds(x * 16 + zp_a, 2, stride=8), :] = got[96 + x * 2 : 98 + x * 2, :]
        b_rows.append((got[100:101, :], got[101:102, :]))
    (left_a, left_b), (ra, rb) = b_rows
    oa, ob = ms[108:109, :], ms[109:110, :]
    low1 = iota((1, 128), 1) < 64
    middle = jnp.where(low1, pltpu.roll(left_b, 64, 1), pltpu.roll(oa, 64, 1))
    middle_r = jnp.where(low1, pltpu.roll(ob, 64, 1), pltpu.roll(ra, 64, 1))
    pairs = [left_a, left_b, middle, oa, ob, middle_r, ra, rb]
    even_z = lax.rem(gz, 2) == 0
    zf[0:16, :] = jnp.zeros((16, 128), F32)
    for l in range(3):
        at_even = l + 1 - l % 2
        at_odd = l + 1 - (l + 1) % 2
        for j in range(3):
            zf[4 * j + l : 4 * j + l + 1, :] = jnp.where(
                even_z, pairs[at_even + 2 * j], pairs[at_odd + 2 * j]
            )
    mb[3, 3] = zf[0:16, :].astype(BF16)
    x_b = []
    for o in (1, -1, 2, -2, 3, -3):
        x_b.append(remote(mb.at[3, 3], mb.at[3 - o, 3], at(o, 0, 0)))
    for x in range(4):
        for y in range(4):
            for t in range(3):
                r = (x * 4 + y) * 56 + t * 16
                pf[1 + x, 1 + y, t] = ps[r : r + 16, :].astype(BF16)
        for yp in range(2):
            r = x * 32 + yp * 16
            ml[2 + x, 1 + yp] = mls[r : r + 16, :].astype(BF16)
    for x in range(2):
        ma[2 + x, 1] = mas[x * 16 : x * 16 + 16, :].astype(BF16)

    own_x, own_xl, own_xa = pl.ds(1, 4), pl.ds(2, 4), pl.ds(2, 2)
    up, down = at(0, 1, 0), at(0, -1, 0)
    y_copies = [
        remote(pf.at[own_x, pl.ds(4, 1)], pf.at[own_x, pl.ds(0, 1)], up),
        remote(pf.at[own_x, pl.ds(1, 1)], pf.at[own_x, pl.ds(5, 1)], down),
        remote(ml.at[own_xl, pl.ds(2, 1)], ml.at[own_xl, pl.ds(0, 1)], up),
        remote(ml.at[own_xl, pl.ds(1, 1)], ml.at[own_xl, pl.ds(3, 1)], down),
        remote(ma.at[own_xa, pl.ds(1, 1)], ma.at[own_xa, pl.ds(0, 1)], up),
        remote(ma.at[own_xa, pl.ds(1, 1)], ma.at[own_xa, pl.ds(2, 1)], down),
    ]

    low_lanes = iota((32, 128), 1) < 64

    def pair_up(g, carry):
        near = (jnp.abs(g // 7 - 3) <= 1) & (jnp.abs(lax.rem(g, 7) - 3) <= 1)
        kept = jnp.where(near, 0.0, 1.0).astype(F32)
        tables = []
        for i in range(7):
            one = s2[pl.ds(pl.multiple_of((g * 7 + i) * 40, 8), 32), :]
            if 2 <= i <= 4:
                one = one * kept
            tables.append((one, pltpu.roll(one, 64, 1)))
        for w in range(6):
            (first, turned_first), (second, turned_second) = tables[w + 1], tables[w]
            to = g * 384 + w * 64
            t2[pl.ds(pl.multiple_of(to, 32), 32), :] = jnp.where(
                low_lanes, first, turned_second
            ).astype(BF16)
            t2[pl.ds(pl.multiple_of(to + 32, 32), 32), :] = jnp.where(
                low_lanes, turned_first, second
            ).astype(BF16)
        return carry

    def own_columns(i, carry):
        where = [(i, cy, a_own, q_own, (i - 1) * 4 + cy - 1) for cy in range(1, 5)]
        source_columns(where, gx, gy, pf, wt)
        return carry

    def pair_some(i):
        for u in range(6):
            pair_up(jnp.minimum(i * 6 + u, 48), 0)

    def own_pairs(t, carry):
        own_slab(t, a_own, q_own, b_mat, ft, near8)
        pair_some(t - 1)
        return carry

    lax.fori_loop(1, 5, own_columns, 0, unroll=2)
    lax.fori_loop(1, 5, own_pairs, 0)
    for copy in x_b:
        copy.wait()
    y_b = []
    for o in (1, -1, 2, -2, 3, -3):
        y_b.append(remote(mb.at[:, pl.ds(3, 1)], mb.at[:, pl.ds(3 - o, 1)], at(0, o, 0)))
    for copy in y_copies:
        copy.wait()

    up, down = at(1, 0, 0), at(-1, 0, 0)
    x_copies = [
        remote(pf.at[pl.ds(4, 1)], pf.at[pl.ds(0, 1)], up),
        remote(pf.at[pl.ds(1, 1)], pf.at[pl.ds(5, 1)], down),
        remote(ml.at[pl.ds(4, 2)], ml.at[pl.ds(0, 2)], up),
        remote(ml.at[pl.ds(2, 2)], ml.at[pl.ds(6, 2)], down),
        remote(ma.at[pl.ds(2, 2)], ma.at[pl.ds(0, 2)], up),
        remote(ma.at[pl.ds(2, 2)], ma.at[pl.ds(4, 2)], down),
    ]
    def own_pairs_y(t, carry):
        cx = t - 4
        where = [(cx, 0, a_edge, q_edge, cx), (cx, 5, a_edge, q_edge, cx + 6)]
        source_columns(where, gx, gy, pf, wt)
        own_slab(t, a_own, q_own, b_mat, ft, near8)
        pair_some(t - 1)
        return carry

    lax.fori_loop(5, 9, own_pairs_y, 0)
    pair_up(48, 0)
    for child in range(4):
        r = (343 + 2 * child) * 40
        even, odd = pair_rows(s2[r : r + 32, :], s2[r + 40 : r + 40 + 32, :], low_lanes)
        to = 49 * 384 + child * 64
        t2[to : to + 32, :] = even
        t2[to + 32 : to + 64, :] = odd
    for copy in x_copies + y_b:
        copy.wait()

    def own_pairs_x(i, carry):
        cx = i * 5
        where = [(cx, 0, a_edge, q_edge, cx), (cx, 5, a_edge, q_edge, cx + 6)]
        where += [(cx, cy, a_side, q_side, i * 4 + cy - 1) for cy in range(1, 5)]
        source_columns(where, gx, gy, pf, wt)
        own_slab(i + 9, a_own, q_own, b_mat, ft, near8)
        edge_pairs(i + 1, a_edge, q_edge, b_mat, ft, near8)
        return carry

    def last_pairs(i, carry):
        slab_pairs(i * 3, None, a_side, q_side, i * 4, b_mat, ft, near8)
        edge_pairs(i * 3, a_edge, q_edge, b_mat, ft, near8)
        return carry

    lax.fori_loop(0, 2, own_pairs_x, 0)
    lax.fori_loop(0, 2, last_pairs, 0, unroll=True)
    gather_near(near8, near)
    far_kernel(
        gx, gy, gz, ml, ma, mb, t2, near, pos, cnt, top, pot_out, loc_out,
        lw, la, lb, lr, pa, ln, to_lanes,
    )


NEAR_SCRATCH = [
    ((1024, 256), BF16),
    ((1024, 1664), BF16),
    ((512, 256), BF16),
    ((512, 1664), BF16),
    ((768, 256), BF16),
    ((768, 1664), BF16),
    ((6, 9, 256, 256), BF16),
    ((16, 3, 2, 16, 768), BF16),
    ((6, 96, 128), F32),
    ((6, 208, 128), F32),
    ((16, 2, 8, 768), F32),
]


FAR_SCRATCH = [
    ((8, 6, 16, 384), BF16),
    ((7, 6, 16, 384), BF16),
    ((7, 6, 16, 384), BF16),
    ((128, 128), F32),
    ((32, 128), F32),
    ((16, 768), F32),
    ((256, 8192), BF16),
]


def run(*args):
    halos = [(6, 6, 3, 16, 128), (8, 4, 16, 128), (6, 3, 16, 128), (7, 7, 16, 128)]
    scratch = [((T2_ROWS, 128), BF16), ((16, 768), F32), ((3, 4, 4, 768), F32)]
    scratch += [((4, 4, 12), jnp.int32), ((1, 1, 192), F32)] + FAR_SCRATCH
    scratch += [(s, BF16) for s in halos]
    scratch += [((2, 112, 128), BF16), ((2, 112, 128), BF16), ((896, 128), F32), ((128, 128), F32)]
    scratch += [((32, 128), F32), ((112, 128), F32), ((224, 128), F32), ((343, 4096), BF16)]
    scratch += [((352 * 40, 128), F32), ((4, 4, 768), F32), ((4, 4, 768), F32)]
    scratch += [((1, 1, 192), BF16), ((2, 2, 384), BF16), ((4, 4, 768), BF16), ((8, 4096), BF16)]
    return pl.pallas_call(
        whole_kernel,
        name="downward",
        out_shape=[jax.ShapeDtypeStruct((4, 4, 768), F32)] * 2,
        in_specs=[pl.BlockSpec(memory_space=pltpu.HBM)] * 10,
        out_specs=[pl.BlockSpec(memory_space=pltpu.VMEM)] * 2,
        scratch_shapes=[pltpu.VMEM(s, t) for s, t in scratch + NEAR_SCRATCH]
        + [
            pltpu.SemaphoreType.DMA((26,)),
            pltpu.SemaphoreType.DMA((26,)),
            pltpu.SemaphoreType.DMA((10,)),
        ],
        compiler_params=pltpu.CompilerParams(
            collective_id=0, has_side_effects=True, vmem_limit_bytes=VMEM_BYTES
        ),
        cost_estimate=pl.CostEstimate(
            flops=10**10, bytes_accessed=10**7, transcendentals=2 * 10**7
        ),
    )(*args)


def hand_over_kernel(pot_in, loc_in, pot_out, loc_out, held, sems):
    arrays = ((pot_in, pot_out), (loc_in, loc_out))
    blocks = [(n, x) for n in range(2) for x in range(4)]
    came, left = [], []
    for n, x in blocks:
        i = n * 4 + x
        came.append(pltpu.make_async_copy(arrays[n][0].at[x], held.at[n, x], sems.at[0, i]))
        left.append(pltpu.make_async_copy(held.at[n, x], arrays[n][1].at[x], sems.at[1, i]))
    for copy in came:
        copy.start()
    for first, second in zip(came, left):
        first.wait()
        second.start()
    for copy in left:
        copy.wait()


def hand_over(*results):
    hbm = pl.BlockSpec(memory_space=pltpu.HBM)
    return pl.pallas_call(
        hand_over_kernel,
        name="hand_over",
        out_shape=[jax.ShapeDtypeStruct((4, 4, 768), F32)] * 2,
        in_specs=[hbm] * 2,
        out_specs=[hbm] * 2,
        scratch_shapes=[pltpu.VMEM((2, 4, 4, 768), F32), pltpu.SemaphoreType.DMA((2, 8))],
        compiler_params=pltpu.CompilerParams(vmem_limit_bytes=VMEM_BYTES),
    )(*results)


def per_device(pos, chg, soft, cnt, top, bm, am, lm, m2l, l2l):
    return tuple(hand_over(*run(pos, chg, soft, cnt, top, bm, am, lm, m2l, l2l)))


def solution(mesh):
    split = P("gx", "gy", "gz")
    in_specs = (P(None, "gx", "gy", "gz"),) + (split,) * 7 + (P(), P())
    return jax.shard_map(
        per_device, mesh=mesh, in_specs=in_specs, out_specs=(split, split), check_vma=False
    )
```
